256 devices in a mesh: dp: 4 (over y_hi, core), tm: 64 (over y_lo, x, z).
Axes of the slice: x: 4, y: 4 (y_hi: 2, y_lo: 2; y = y_hi * 2 + y_lo), z: 8, core: 2. Of those that a mesh axis runs over, the one named last changes fastest.
Arguments:
- frames: bfloat16 [4, 16384, 256], P('dp', 'tm'), may hold values from -6 to 6
- frames_grad: bfloat16 [4, 16384, 256], P('dp', 'tm'), may hold values from -6 to 6
- w_query: bfloat16 [2, 256, 256], replicated, may hold values from -32 to 32, as said below
- w_key: bfloat16 [2, 256, 256], replicated, may hold values from -0.375 to 0.375
- w_value: bfloat16 [2, 256, 256], replicated, may hold values from -0.375 to 0.375
- w_out: bfloat16 [2, 256, 256], replicated, may hold values from -0.375 to 0.375
- norm_gains: float32 [2, 256], replicated, may hold values from 0.1 to 1.9
Outputs:
- grad_frames: bfloat16 [4, 16384, 256], P('dp', 'tm')
- grad_query: float32 [2, 256, 256], replicated
- grad_key: float32 [2, 256, 256], replicated
- grad_value: float32 [2, 256, 256], replicated
- grad_out: float32 [2, 256, 256], replicated
- grad_gains: float32 [2, 256], replicated
The draws below stay inside these ranges and needn't reach their ends.
Inputs may be any that keep to these rules, and one draw needn't show every extreme that they name: `w_query`: query projections of the two layers, full rank.
All inputs are finite; a program needn't handle non-finite values.
Results may differ from the reference program's by a relative error of at most 0.03.
The reference program's roundings to bfloat16 on the way count: a program that leaves them out, or rounds other values in their place, can miss the bound.
Values may be sent and summed in bfloat16 or wider, within the bound.
No kernel may reach another device: no remote copies, remote signals or barrier semaphores. Data moves between devices by JAX's collectives and lax.ppermute only.
A program may use at most 64 MiB of HBM per device.

```python
import math
import jax
import jax.numpy as jnp
from jax import lax

D = 256
HEADS = 8
K = 256
HOP = 128
MIXTURES = 4
GROUPS = 128
FRAMES = 16384


def draw_w_query(key, part):
    key = jax.random.fold_in(key, 11)
    first_key = jax.random.fold_in(key, 0)
    base = jax.random.truncated_normal(first_key, -6.0, 6.0, (2, D, D), jnp.float32) / math.sqrt(D)
    return base.astype(jnp.bfloat16)


def block_scale(rng, extent, pieces, low, largest):
    loudness = 1.0
    for dim, shards_of in pieces:
        steps = jax.random.uniform(jax.random.fold_in(jax.random.fold_in(rng, 6), dim), (shards_of,), jnp.float32, low / len(pieces), largest / len(pieces))
        loudness = loudness * jnp.repeat(jnp.exp(steps), extent[dim] // shards_of).reshape((-1,) + (1,) * (len(extent) - 1 - dim))
    return loudness


def noise(stream_key, extent, scale, most, cuts=(), held_as=jnp.bfloat16):
    level = block_scale(stream_key, extent, cuts, -0.22, 0.18) if cuts else 1.0
    result = jax.random.normal(stream_key, extent, jnp.float32) * scale * level
    return jnp.minimum(jnp.maximum(result, -most), most).astype(held_as)


def setup_inputs(seed: int = 0) -> dict:
    streams_of = jax.random.split(jax.random.key(seed), 8)
    frames = noise(streams_of[0], (MIXTURES, FRAMES, D), 1.0, 6.0, ((0, 4), (1, 64)))
    frames_grad = noise(streams_of[1], (MIXTURES, FRAMES, D), 1.0, 6.0, ((0, 4), (1, 64)))
    w_query = draw_w_query(jax.random.fold_in(streams_of[7], 71), 0)
    w_key = noise(streams_of[3], (2, D, D), D ** -0.5, 0.375)
    w_value = noise(streams_of[4], (2, D, D), D ** -0.5, 0.375)
    w_out = noise(streams_of[5], (2, D, D), D ** -0.5, 0.375)
    norm_gains = jnp.clip(1.0 + 0.18 * jax.random.normal(streams_of[6], (2, D), jnp.float32), 0.1, 1.9)
    return {"frames": frames, "frames_grad": frames_grad, "w_query": w_query, "w_key": w_key, "w_value": w_value, "w_out": w_out, "norm_gains": norm_gains}


EPSILON = 1e-05

def rounded(value):
    return lax.optimization_barrier(value.astype(jnp.bfloat16))

def normalize(activations, gain):
    average = lax.optimization_barrier(jnp.mean(activations, axis=-1, keepdims=True))
    centered = activations - average
    variance = lax.optimization_barrier(jnp.mean(centered * centered, axis=-1, keepdims=True))
    return centered * lax.rsqrt(variance + EPSILON) * gain

def project(left, weight):
    return jnp.dot(left, weight, preferred_element_type=jnp.float32)

def back_project(grad_rows, weight):
    return lax.dot_general(grad_rows, weight, (((grad_rows.ndim - 1,), (1,)), ((), ())), preferred_element_type=jnp.float32)

def contract_tokens(left, right):
    left_rows = left.reshape(-1, left.shape[-1])
    right_rows = right.reshape(-1, right.shape[-1])
    return lax.dot_general(left_rows, right_rows, (((0,), (0,)), ((), ())), preferred_element_type=jnp.float32)

def product(form, left, right):
    return jnp.einsum(form, left.astype(jnp.float32), right.astype(jnp.float32), precision=lax.Precision.HIGHEST)

def attention_probs(queries, key_rows):
    scaling = queries.shape[-1] ** (-0.5)
    scores = product('gqmd,gkmd->gmqk', queries, key_rows) * scaling
    highest = lax.optimization_barrier(jnp.max(scores, axis=-1, keepdims=True))
    exponentials = jnp.exp(scores - highest)
    return exponentials / lax.optimization_barrier(jnp.sum(exponentials, axis=-1, keepdims=True))

def head_forward(queries, key_rows, value_rows):
    weights_low = rounded(attention_probs(queries, key_rows))
    return (rounded(product('gmqk,gkmd->gqmd', weights_low, value_rows)),)

def head_backward(queries, key_rows, value_rows, grad_context):
    scaling = queries.shape[-1] ** (-0.5)
    probabilities = attention_probs(queries, key_rows)
    weights_low = rounded(probabilities)
    context = rounded(product('gmqk,gkmd->gqmd', weights_low, value_rows))
    grad_probs = product('gqmd,gkmd->gmqk', grad_context, value_rows)
    grad_values = rounded(product('gmqk,gqmd->gkmd', weights_low, grad_context))
    inner = lax.optimization_barrier(jnp.sum(grad_probs * probabilities, axis=-1, keepdims=True))
    grad_scores = rounded(probabilities * (grad_probs - inner) * scaling)
    grad_queries = rounded(product('gmqk,gkmd->gqmd', grad_scores, key_rows))
    grad_keys = rounded(product('gmqk,gqmd->gkmd', grad_scores, queries))
    return (context, grad_queries, grad_keys, grad_values)

def over_heads(function, operands):
    head_width = operands[0].shape[-1] // HEADS

    def single_head(head_index):
        offset = head_index * head_width
        return function(*[lax.dynamic_slice_in_dim(operand, offset, head_width, axis=3) for operand in operands])
    stacked = lax.map(single_head, jnp.arange(HEADS))
    return tuple((jnp.moveaxis(result_part, 0, 3).reshape(operands[0].shape) for result_part in stacked))

def layer_front(inputs, gain, weight_query, weight_key, weight_value):
    normed = rounded(normalize(inputs.astype(jnp.float32), gain))
    return (normed, rounded(project(normed, weight_query)), rounded(project(normed, weight_key)), rounded(project(normed, weight_value)))

def layer_output(inputs, context, weight_out):
    return rounded(inputs.astype(jnp.float32) + project(context, weight_out))

def layer_back(inputs, front, grad_rows, gain, weight_query, weight_key, weight_value, weight_out):
    normed, queries, key_rows, value_rows = front
    grad_context = rounded(back_project(grad_rows, weight_out))
    context, grad_queries, grad_keys, grad_values = over_heads(head_backward, (queries, key_rows, value_rows, grad_context))
    grad_normed = back_project(grad_queries, weight_query) + back_project(grad_keys, weight_key) + back_project(grad_values, weight_value)
    unused_value, pullback = jax.vjp(normalize, inputs.astype(jnp.float32), gain)
    grad_inputs, grad_gain = pullback(grad_normed)
    parts = (contract_tokens(normed, grad_queries), contract_tokens(normed, grad_keys), contract_tokens(normed, grad_values), contract_tokens(context, grad_rows), grad_gain)
    return (grad_rows.astype(jnp.float32) + grad_inputs, parts)

def segment(blocks):
    following = jnp.concatenate([blocks[1:], jnp.zeros_like(blocks[:1])], axis=0)
    return jnp.concatenate([blocks, following], axis=1)

def reference(frames, frames_grad, w_query, w_key, w_value, w_out, norm_gains):
    width = frames.shape[-1]

    def one_mixture(mixture_pair):
        mixture_frames, mixture_grad = mixture_pair
        grouped = segment(mixture_frames.reshape(GROUPS, HOP, width)).reshape(GROUPS, K, 1, width)
        front_intra = layer_front(grouped, norm_gains[0], w_query[0], w_key[0], w_value[0])
        context_intra, = over_heads(head_forward, front_intra[1:])
        middle = layer_output(grouped, context_intra, w_out[0]).reshape(1, GROUPS, K, width)
        grad_across = segment(mixture_grad.reshape(GROUPS, HOP, width)).reshape(1, GROUPS, K, width)
        front_inter = layer_front(middle, norm_gains[1], w_query[1], w_key[1], w_value[1])
        grad_middle, parts_inter = layer_back(middle, front_inter, grad_across, norm_gains[1], w_query[1], w_key[1], w_value[1], w_out[1])
        grad_middle = rounded(grad_middle).reshape(GROUPS, K, 1, width)
        grad_grouped, parts_intra = layer_back(grouped, front_intra, grad_middle, norm_gains[0], w_query[0], w_key[0], w_value[0], w_out[0])
        halves = rounded(grad_grouped).reshape(GROUPS, 2, HOP, width).astype(jnp.float32)
        earlier = jnp.concatenate([jnp.zeros_like(halves[:1, 1]), halves[:-1, 1]], axis=0)
        grad_input = rounded(halves[:, 0] + earlier).reshape(GROUPS * HOP, width)
        stacked = tuple((jnp.stack([intra_part, inter_part]) for intra_part, inter_part in zip(parts_intra, parts_inter)))
        return (grad_input, stacked)
    grad_frames, summed = lax.map(one_mixture, (frames, frames_grad))
    totals = tuple((lax.optimization_barrier(jnp.sum(per_mixture, axis=0)) for per_mixture in summed))
    return (grad_frames, totals[0], totals[1], totals[2], totals[3], totals[4])
```

```python
import math

import jax
import jax.numpy as jnp
from jax import lax
from jax.experimental import pallas as pl
from jax.experimental.pallas import tpu as pltpu
from jax.sharding import Mesh, PartitionSpec as P

HEADS = 8
HEAD = 32
D = 256
K = 256
HOP = 128
SEGMENTS = 128
EPSILON = 1e-05
SCALE = HEAD ** (-0.5)
LOG2E = math.log2(math.e)
BF = jnp.bfloat16
F32 = jnp.float32
VMEM_LIMIT = 48 * 1024 * 1024

AXES = ("yh", "core", "yl", "x", "z")
DP = ("yh", "core")
TM = ("yl", "x", "z")
PLANE = ("yh", "yl", "x")


def dot(left, right, left_dim, right_dim):
    return lax.dot_general(
        left, right, (((left_dim,), (right_dim,)), ((), ())), preferred_element_type=F32
    )


def nn(left, right):
    return dot(left, right, 1, 0)


def nt(left, right):
    return dot(left, right, 1, 1)


def tn(left, right):
    return dot(left, right, 0, 0)


def standardize(rows):
    average = jnp.mean(rows, axis=-1, keepdims=True)
    centered = rows - average
    variance = jnp.mean(centered * centered, axis=-1, keepdims=True)
    inverse = lax.rsqrt(variance + EPSILON)
    return centered * inverse, inverse


def norm_pullback(grad_normed, unit, inverse, gain):
    grad_unit = grad_normed * gain
    first = jnp.mean(grad_unit, axis=-1, keepdims=True)
    second = jnp.mean(grad_unit * unit, axis=-1, keepdims=True)
    return inverse * (grad_unit - first - unit * second)


def head_masks():
    lane = lax.broadcasted_iota(jnp.int32, (1, 128), 1)
    return [jnp.where(lane // HEAD == i, 1.0, 0.0).astype(BF) for i in range(4)]


def row_masks():
    row = lax.broadcasted_iota(jnp.int32, (128, 1), 0)
    return [jnp.where(row // HEAD == i, 1.0, 0.0).astype(BF) for i in range(4)]


def select_rows(out_rows, in_rows, source):
    out = lax.broadcasted_iota(jnp.int32, (out_rows, in_rows), 0)
    col = lax.broadcasted_iota(jnp.int32, (out_rows, in_rows), 1)
    return jnp.where(source(out) == col, 1.0, 0.0).astype(BF)


def softmax_keys(scores):
    highest = jnp.max(scores, axis=0, keepdims=True)
    powers = jnp.exp2((scores - highest) * (SCALE * LOG2E))
    return powers * (1.0 / jnp.sum(powers, axis=0, keepdims=True))


def owner_source(out):
    return ((out // 2) % 4) * 64 + (out // 8) * 2 + out % 2


def owner_target(out):
    return ((out % 64) // 2) * 8 + (out // 64) * 2 + out % 2


def segment_source(out):
    return (out % 64) * 4 + out // 64


def segment_target(out):
    return (out % 4) * 64 + out // 4


def intra_forward_kernel(f_ref, n_ref, gain_ref, wq_ref, wk_ref, wv_ref, wo_ref, mid_ref, ctx_ref):
    rows = jnp.concatenate([f_ref[...], n_ref[...]], axis=0).astype(F32)
    unit, _ = standardize(rows)
    normed = (unit * gain_ref[0:1, :]).astype(BF)
    keys = nn(normed, wk_ref[0]).astype(BF)
    queries_t = nt(wq_ref[0].T, normed).astype(BF)
    values_t = nt(wv_ref[0].T, normed).astype(BF)
    masks = head_masks()
    mids = []
    for g in range(2):
        at = g * HOP
        for h in range(HEADS):
            block = slice((h // 4) * 128, (h // 4) * 128 + 128)
            feats = slice(h * HEAD, h * HEAD + HEAD)
            scores = nn(
                keys[at : at + K, block] * masks[h % 4], queries_t[block, at : at + K]
            )
            low = softmax_keys(scores).astype(BF)
            ctx_ref[g, feats, :] = nn(values_t[feats, at : at + K], low).astype(BF)
        mids.append((rows[at : at + K] + tn(ctx_ref[g], wo_ref[0])).astype(BF))
    pick = select_rows(256, 256, owner_source)
    for t in range(2):
        part = jnp.concatenate(
            [mids[g][h * HOP + 64 * t : h * HOP + 64 * t + 64] for g in range(2) for h in range(2)],
            axis=0,
        )
        mid_ref[256 * t : 256 * t + 256, :] = nn(pick, part).astype(BF)


def intra_forward(frames, following, gains, wq, wk, wv, wo):
    return pl.pallas_call(
        intra_forward_kernel,
        out_shape=(
            jax.ShapeDtypeStruct((2 * K, D), BF),
            jax.ShapeDtypeStruct((2, D, K), BF),
        ),
        compiler_params=pltpu.CompilerParams(vmem_limit_bytes=VMEM_LIMIT),
        name="intra_forward",
    )(frames, following, gains, wq, wk, wv, wo)


def inter_kernel(
    m_ref, g_ref, gain_ref, wq_ref, wk_ref, wv_ref, wo_ref, out_ref, dw_ref,
    ctx_t, gq_t, gk_ref, gv_ref,
):
    gain = gain_ref[1:2, :]
    pick = select_rows(256, 256, segment_source)
    tiles = [nn(pick, m_ref[256 * t : 256 * t + 256, :]) for t in range(2)]
    rows = jnp.concatenate(
        [tiles[t][64 * p : 64 * p + 64] for p in range(4) for t in range(2)], axis=0
    )

    def grad_source(out):
        segment = out % 128 + out // 256
        return jnp.where(segment < SEGMENTS, segment * 2 + (out // 128) % 2, -1)

    grads = nn(select_rows(512, 256, grad_source), g_ref[...]).astype(BF)
    unit, inverse = standardize(rows)
    normed = (unit * gain).astype(BF)
    normed_t = normed.T
    wq, wk, wv, wo = wq_ref[1], wk_ref[1], wv_ref[1], wo_ref[1]
    queries = nn(normed, wq).astype(BF)
    keys = nn(normed, wk).astype(BF)
    values = nn(normed, wv).astype(BF)
    grad_context = nt(grads, wo).astype(BF)
    queries_t = queries.T
    keys_t = keys.T
    values_t = values.T
    grad_context_t = grad_context.T
    masks = head_masks()
    downs = row_masks()
    for p in range(4):
        at = slice(128 * p, 128 * p + 128)
        for b in range(2):
            block = slice(128 * b, 128 * b + 128)
            gv = jnp.zeros((128, 128), F32)
            gk = jnp.zeros((128, 128), F32)
            for pair in range(2):
                first, second = 2 * pair, 2 * pair + 1
                feats = slice(128 * b + 64 * pair, 128 * b + 64 * pair + 64)
                top = slice(128 * b + 64 * pair, 128 * b + 64 * pair + 32)
                low_half = slice(128 * b + 64 * pair + 32, 128 * b + 64 * pair + 64)
                qt, gt = queries_t[block, at], grad_context_t[block, at]
                scores = nn(
                    keys[at, block],
                    jnp.concatenate([qt * downs[first], qt * downs[second]], axis=1),
                )
                probs = softmax_keys(scores)
                low = probs.astype(BF)
                both = nn(values_t[feats, at], low).astype(BF)
                ctx_t[top, at] = both[:32, :128]
                ctx_t[low_half, at] = both[32:, 128:]
                grad_probs = nn(
                    values[at, block],
                    jnp.concatenate([gt * downs[first], gt * downs[second]], axis=1),
                )
                inner = jnp.sum(grad_probs * probs, axis=0, keepdims=True)
                grad_scores = (probs * (grad_probs - inner) * SCALE).astype(BF)
                gc = grad_context[at, block]
                gv += nn(low, jnp.concatenate([gc * masks[first], gc * masks[second]], axis=0))
                qs = queries[at, block]
                gk += nn(
                    grad_scores, jnp.concatenate([qs * masks[first], qs * masks[second]], axis=0)
                )
                both = nn(keys_t[feats, at], grad_scores).astype(BF)
                gq_t[top, at] = both[:32, :128]
                gq_t[low_half, at] = both[32:, 128:]
            gk_ref[at, block] = gk.astype(BF)
            gv_ref[at, block] = gv.astype(BF)
    gqt, gk, gv = gq_t[...], gk_ref[...], gv_ref[...]
    dw_ref[0] = nt(normed_t, gqt)
    dw_ref[1] = nn(normed_t, gk)
    dw_ref[2] = nn(normed_t, gv)
    dw_ref[3] = nn(ctx_t[...], grads)
    grad_normed = nt(gqt.T, wq) + nt(gk, wk) + nt(gv, wv)
    result = (grads.astype(F32) + norm_pullback(grad_normed, unit, inverse, gain)).astype(BF)
    back = select_rows(256, 256, segment_target)
    for t in range(2):
        part = jnp.concatenate(
            [result[128 * p + 64 * t : 128 * p + 64 * t + 64] for p in range(4)], axis=0
        )
        out_ref[256 * t : 256 * t + 256, :] = nn(back, part).astype(BF)


def inter(middle, grads, gains, wq, wk, wv, wo):
    return pl.pallas_call(
        inter_kernel,
        out_shape=(
            jax.ShapeDtypeStruct((512, D), BF),
            jax.ShapeDtypeStruct((4, D, D), F32),
        ),
        scratch_shapes=[
            pltpu.VMEM((D, 512), BF),
            pltpu.VMEM((D, 512), BF),
            pltpu.VMEM((512, D), BF),
            pltpu.VMEM((512, D), BF),
        ],
        compiler_params=pltpu.CompilerParams(vmem_limit_bytes=VMEM_LIMIT),
        name="inter",
    )(middle, grads, gains, wq, wk, wv, wo)


def intra_backward_kernel(
    core_ref, m_ref, ctx_ref, dw1_ref, f_ref, n_ref, gain_ref, wq_ref, wk_ref, wv_ref, wo_ref,
    first_ref, second_ref, carry_ref, keep_ref, send_ref,
    gq_t, gk_ref, gv_ref,
):
    gain = gain_ref[0:1, :]
    rows = jnp.concatenate([f_ref[...], n_ref[...]], axis=0).astype(F32)
    unit, inverse = standardize(rows)
    normed = (unit * gain).astype(BF)
    normed_t = normed.T
    wq, wk, wv, wo = wq_ref[0], wk_ref[0], wv_ref[0], wo_ref[0]
    queries = nn(normed, wq).astype(BF)
    keys = nn(normed, wk).astype(BF)
    values = nn(normed, wv).astype(BF)
    queries_t = queries.T
    keys_t = keys.T
    masks = head_masks()
    pick = select_rows(256, 256, owner_target)
    tiles = [nn(pick, m_ref[256 * t : 256 * t + 256, :]).astype(BF) for t in range(2)]
    totals = [jnp.zeros((D, D), F32) for _ in range(4)]
    halves = []
    for g in range(2):
        at = slice(g * HOP, g * HOP + K)
        grads = jnp.concatenate(
            [tiles[t][128 * g + 64 * h : 128 * g + 64 * h + 64] for h in range(2) for t in range(2)],
            axis=0,
        )
        grad_context = nt(grads, wo).astype(BF)
        grad_context_t = grad_context.T
        for b in range(2):
            block = slice(128 * b, 128 * b + 128)
            gv = jnp.zeros((K, 128), F32)
            gk = jnp.zeros((K, 128), F32)
            for i in range(4):
                feats = slice(128 * b + HEAD * i, 128 * b + HEAD * i + HEAD)
                scores = nn(keys[at, block] * masks[i], queries_t[block, at])
                probs = softmax_keys(scores)
                low = probs.astype(BF)
                grad_probs = nn(values[at, block] * masks[i], grad_context_t[block, :])
                inner = jnp.sum(grad_probs * probs, axis=0, keepdims=True)
                grad_scores = (probs * (grad_probs - inner) * SCALE).astype(BF)
                gv += nn(low, grad_context[:, block] * masks[i])
                gk += nn(grad_scores, queries[at, block] * masks[i])
                gq_t[feats, :] = nn(keys_t[feats, at], grad_scores).astype(BF)
            gk_ref[:, block] = gk.astype(BF)
            gv_ref[:, block] = gv.astype(BF)
        gqt, gk, gv = gq_t[...], gk_ref[...], gv_ref[...]
        totals[0] += nt(normed_t[:, at], gqt)
        totals[1] += nn(normed_t[:, at], gk)
        totals[2] += nn(normed_t[:, at], gv)
        totals[3] += nn(ctx_ref[g], grads)
        grad_normed = nt(gqt.T, wq) + nt(gk, wk) + nt(gv, wv)
        result = grads.astype(F32) + norm_pullback(grad_normed, unit[at], inverse[at], gain)
        result = result.astype(BF)
        halves.append((result[:HOP], result[HOP:]))
    first_ref[...] = halves[0][0]
    second_ref[...] = (halves[1][0].astype(F32) + halves[0][1].astype(F32)).astype(BF)
    carry_ref[...] = halves[1][1]
    low_core = core_ref[0] == 0
    for i in range(2):
        for layer, pair in ((0, (totals[i], totals[2 + i])), (1, (dw1_ref[i], dw1_ref[2 + i]))):
            keep_ref[i, layer] = jnp.where(low_core, pair[0], pair[1])
            send_ref[i, layer] = jnp.where(low_core, pair[1], pair[0]).astype(BF)


def intra_backward(core, grads, ctx, dw1, frames, following, gains, wq, wk, wv, wo):
    vmem = pl.BlockSpec(memory_space=pltpu.VMEM)
    return pl.pallas_call(
        intra_backward_kernel,
        in_specs=[pl.BlockSpec(memory_space=pltpu.SMEM)] + [vmem] * 10,
        out_shape=(
            jax.ShapeDtypeStruct((HOP, D), BF),
            jax.ShapeDtypeStruct((HOP, D), BF),
            jax.ShapeDtypeStruct((HOP, D), BF),
            jax.ShapeDtypeStruct((2, 2, D, D), F32),
            jax.ShapeDtypeStruct((2, 2, D, D), BF),
        ),
        scratch_shapes=[
            pltpu.VMEM((D, K), BF),
            pltpu.VMEM((K, D), BF),
            pltpu.VMEM((K, D), BF),
        ],
        compiler_params=pltpu.CompilerParams(vmem_limit_bytes=VMEM_LIMIT),
        name="intra_backward",
    )(core, grads, ctx, dw1, frames, following, gains, wq, wk, wv, wo)


def finish_kernel(
    core_ref, mine_ref, other_ref, gain_ref, wq_ref, wk_ref, wv_ref,
    dq_ref, dk_ref, dv_ref, do_ref, dg_ref,
):
    low_core = core_ref[0] == 0
    for layer in range(2):
        lead = [mine_ref[i, layer].astype(F32) for i in range(2)]
        rest = [other_ref[i, layer].astype(F32) for i in range(2)]
        dq = jnp.where(low_core, lead[0], rest[0])
        dk = jnp.where(low_core, lead[1], rest[1])
        dv = jnp.where(low_core, rest[0], lead[0])
        dq_ref[layer] = dq
        dk_ref[layer] = dk
        dv_ref[layer] = dv
        do_ref[layer] = jnp.where(low_core, rest[1], lead[1])
        through = (
            dq * wq_ref[layer].astype(F32)
            + dk * wk_ref[layer].astype(F32)
            + dv * wv_ref[layer].astype(F32)
        )
        column = jnp.sum(through.T, axis=0, keepdims=True)
        dg_ref[layer : layer + 1, :] = column / gain_ref[layer : layer + 1, :]


def finish(core, mine, other, gains, wq, wk, wv):
    vmem = pl.BlockSpec(memory_space=pltpu.VMEM)
    full = jax.ShapeDtypeStruct((2, D, D), F32)
    return pl.pallas_call(
        finish_kernel,
        in_specs=[pl.BlockSpec(memory_space=pltpu.SMEM)] + [vmem] * 6,
        out_shape=(full, full, full, full, jax.ShapeDtypeStruct((2, D), F32)),
        compiler_params=pltpu.CompilerParams(vmem_limit_bytes=VMEM_LIMIT),
        name="finish",
    )(core, mine, other, gains, wq, wk, wv)


def shifted(shard, by):
    length = lax.axis_size(TM)
    pairs = [(i, i + by) for i in range(length) if 0 <= i + by < length]
    return lax.ppermute(shard, TM, pairs)


def exchanged(shard, axes):
    return lax.all_to_all(shard, axes, split_axis=0, concat_axis=0, tiled=True)


def swapped(shard):
    return lax.ppermute(shard, "core", [(0, 1), (1, 0)])


def shards(frames, frames_grad, wq, wk, wv, wo, gains):
    frames = frames[0]
    core = lax.axis_index("core").astype(jnp.int32).reshape(1)
    following = shifted(frames[:HOP], -1)
    by_owner = frames_grad.reshape(2, 64, 2, D).transpose(1, 0, 2, 3).reshape(64, 4, D)
    grads = exchanged(by_owner, TM).reshape(256, D)
    middle, ctx = intra_forward(frames, following, gains, wq, wk, wv, wo)
    across = exchanged(middle.reshape(64, 8, D), TM).reshape(512, D)
    grad_middle, dw1 = inter(across, grads, gains, wq, wk, wv, wo)
    grad_local = exchanged(grad_middle.reshape(64, 8, D), TM).reshape(512, D)
    first, second, carry, keep, send = intra_backward(
        core, grad_local, ctx, dw1, frames, following, gains, wq, wk, wv, wo
    )
    carried = shifted(carry, 1)
    arrived = swapped(send)
    half = (keep + arrived.astype(F32)).astype(BF).reshape(16, 64, D)
    pieces = exchanged(half, PLANE)
    piece = jnp.sum(pieces.astype(F32), axis=0).astype(BF)
    pieces = exchanged(jnp.broadcast_to(piece[None], (8, 64, D)), "z")
    piece = jnp.sum(pieces.astype(F32), axis=0).astype(BF)
    whole = exchanged(jnp.broadcast_to(piece[None], (16, 64, D)), PLANE).reshape(2, 2, D, D)
    other = swapped(whole)
    dq, dk, dv, do, dg = finish(core, whole, other, gains, wq, wk, wv)
    head = (first.astype(F32) + carried.astype(F32)).astype(BF)
    grad_frames = jnp.concatenate([head, second], axis=0)[None]
    return grad_frames, dq, dk, dv, do, dg


def solution(mesh):
    split = Mesh(mesh.devices.reshape(2, 2, 2, 4, 8), AXES)
    placed = (P(DP, TM, None), P(DP, TM, None), P(), P(), P(), P(), P())
    return jax.shard_map(
        shards,
        mesh=split,
        in_specs=placed,
        out_specs=(P(DP, TM, None), P(), P(), P(), P(), P()),
        check_vma=False,
    )
```

```python
import math

import jax
import jax.numpy as jnp
from jax import lax
from jax.experimental import pallas as pl
from jax.experimental.pallas import tpu as pltpu
from jax.sharding import Mesh, PartitionSpec as P

HEADS = 8
HEAD = 32
D = 256
K = 256
HOP = 128
SEGMENTS = 128
EPSILON = 1e-05
SCALE = HEAD ** (-0.5)
LOG2E = math.log2(math.e)
BF = jnp.bfloat16
F32 = jnp.float32
VMEM_LIMIT = 24 * 1024 * 1024

AXES = ("yh", "core", "yl", "x", "z")
DP = ("yh", "core")
TM = ("yl", "x", "z")
PLANE = ("yh", "yl", "x")


def dot(left, right, left_dim, right_dim):
    return lax.dot_general(
        left, right, (((left_dim,), (right_dim,)), ((), ())), preferred_element_type=F32
    )


def nn(left, right):
    return dot(left, right, 1, 0)


def nt(left, right):
    return dot(left, right, 1, 1)


def tn(left, right):
    return dot(left, right, 0, 0)


def standardize(rows):
    average = jnp.mean(rows, axis=-1, keepdims=True)
    centered = rows - average
    variance = jnp.mean(centered * centered, axis=-1, keepdims=True)
    inverse = lax.rsqrt(variance + EPSILON)
    return centered * inverse, inverse


def norm_pullback(grad_normed, unit, inverse, gain):
    grad_unit = grad_normed * gain
    first = jnp.mean(grad_unit, axis=-1, keepdims=True)
    second = jnp.mean(grad_unit * unit, axis=-1, keepdims=True)
    return inverse * (grad_unit - first - unit * second)


def head_masks():
    lane = lax.broadcasted_iota(jnp.int32, (1, 128), 1)
    return [jnp.where(lane // HEAD == i, 1.0, 0.0).astype(BF) for i in range(4)]


def row_masks():
    row = lax.broadcasted_iota(jnp.int32, (128, 1), 0)
    return [jnp.where(row // HEAD == i, 1.0, 0.0).astype(BF) for i in range(4)]


def select_rows(out_rows, in_rows, source):
    out = lax.broadcasted_iota(jnp.int32, (out_rows, in_rows), 0)
    col = lax.broadcasted_iota(jnp.int32, (out_rows, in_rows), 1)
    return jnp.where(source(out) == col, 1.0, 0.0).astype(BF)


def softmax_keys(scores):
    highest = jnp.max(scores, axis=0, keepdims=True)
    powers = jnp.exp2((scores - highest) * (SCALE * LOG2E))
    return powers * (1.0 / jnp.sum(powers, axis=0, keepdims=True))


def owner_target(out):
    return ((out % 64) // 2) * 8 + (out // 64) * 2 + out % 2


def segment_target(out):
    return (out % 4) * 64 + out // 4


def packed_source(out):
    device, row = out // 24, out % 24
    part = row % 8
    middle = (row // 8) * 128 + (part // 2) * 32 + device * 2 + part % 2
    rest = row - 16
    grads = 256 + (rest // 4) * 64 + ((rest % 4) // 2) * 32 + device * 2 + rest % 2
    return jnp.where(row < 16, middle, grads)


def unpacked_source(out):
    column, place = out // 128, out % 128
    segment = place % 32
    middle = (segment // 2) * 24 + column * 8 + (segment % 2) * 4 + place // 32
    rest = out - 256
    column, place = rest // 64, rest % 64
    segment = place % 32
    grads = (segment // 2) * 24 + 16 + column * 4 + (segment % 2) * 2 + place // 32
    return jnp.where(out < 256, middle, grads)


def staged(count, *stages):
    held = [{} for _ in stages]
    for t in range(count + len(stages) - 1):
        for i, stage in enumerate(stages):
            step = t - i
            if 0 <= step < count:
                held[i][step] = stage(step, *([held[i - 1].pop(step)] if i else []))


def attend(keys, queries_t, values_t, ctx_ref):
    masks = head_masks()

    def scores_of(h):
        block = slice((h // 4) * 128, (h // 4) * 128 + 128)
        return nn(keys[:, block] * masks[h % 4], queries_t[block, :])

    def weigh(h, scores):
        return softmax_keys(scores).astype(BF)

    def collect(h, low):
        feats = slice(h * HEAD, h * HEAD + HEAD)
        ctx_ref[feats, :] = nn(values_t[feats, :], low).astype(BF)

    staged(HEADS, scores_of, weigh, collect)


def intra_first_kernel(
    f_ref, gain_ref, wq_ref, wk_ref, wv_ref, wo_ref, mid_ref, ctx_ref, keys_ref, queries_ref, values_ref
):
    rows = f_ref[...].astype(F32)
    unit, _ = standardize(rows)
    normed = (unit * gain_ref[0:1, :]).astype(BF)
    keys = nn(normed, wk_ref[0]).astype(BF)
    queries_t = nt(wq_ref[0].T, normed).astype(BF)
    values_t = nt(wv_ref[0].T, normed).astype(BF)
    attend(keys, queries_t, values_t, ctx_ref)
    mid_ref[...] = (rows + tn(ctx_ref[...], wo_ref[0])).astype(BF)
    keys_ref[...] = keys[HOP:]
    queries_ref[...] = queries_t[:, HOP:]
    values_ref[...] = values_t[:, HOP:]


def intra_second_kernel(
    f_ref, n_ref, grad_ref, mid_in_ref, keys_ref, queries_ref, values_ref,
    gain_ref, wq_ref, wk_ref, wv_ref, wo_ref, packed_ref, ctx_ref,
):
    rows = n_ref[...].astype(F32)
    unit, _ = standardize(rows)
    normed = (unit * gain_ref[0:1, :]).astype(BF)
    keys = jnp.concatenate([keys_ref[...], nn(normed, wk_ref[0]).astype(BF)], axis=0)
    queries_t = jnp.concatenate(
        [queries_ref[...], nt(wq_ref[0].T, normed).astype(BF)], axis=1
    )
    values_t = jnp.concatenate([values_ref[...], nt(wv_ref[0].T, normed).astype(BF)], axis=1)
    attend(keys, queries_t, values_t, ctx_ref)
    rows = jnp.concatenate([f_ref[HOP:, :].astype(F32), rows], axis=0)
    mids = (mid_in_ref[...], (rows + tn(ctx_ref[...], wo_ref[0])).astype(BF))
    grads = grad_ref[...]
    pick = select_rows(384, 384, packed_source)
    for t in range(4):
        middle = jnp.concatenate(
            [mids[g][h * HOP + 32 * t : h * HOP + 32 * t + 32] for g in range(2) for h in range(2)],
            axis=0,
        )
        cotangent = jnp.concatenate(
            [grads[h * HOP + 32 * t : h * HOP + 32 * t + 32] for h in range(2)], axis=0
        )
        part = jnp.concatenate(
            [middle[:, :128], middle[:, 128:], cotangent[:, :128], cotangent[:, 128:]], axis=0
        )
        packed_ref[384 * t : 384 * t + 384, :] = nn(pick, part).astype(BF)


def params():
    return pltpu.CompilerParams(vmem_limit_bytes=VMEM_LIMIT)


def cost(micros):
    return pl.CostEstimate(flops=int(micros * 400e6), bytes_accessed=1 << 20, transcendentals=0)


def bf16(*shape):
    return jax.ShapeDtypeStruct(shape, BF)


def f32(*shape):
    return jax.ShapeDtypeStruct(shape, F32)


def intra_first(frames, gains, wq, wk, wv, wo):
    return pl.pallas_call(
        intra_first_kernel,
        out_shape=(bf16(K, D), bf16(D, K), bf16(HOP, D), bf16(D, HOP), bf16(D, HOP)),
        compiler_params=params(),
        cost_estimate=cost(4),
        name="intra_first",
    )(frames, gains, wq, wk, wv, wo)


def intra_second(frames, following, grads, mid, keys, queries, values, gains, wq, wk, wv, wo):
    return pl.pallas_call(
        intra_second_kernel,
        out_shape=(bf16(64 * 24, 128), bf16(D, K)),
        compiler_params=params(),
        cost_estimate=cost(4),
        name="intra_second",
    )(frames, following, grads, mid, keys, queries, values, gains, wq, wk, wv, wo)


def inter_kernel(
    packed_ref, gain_ref, wq_ref, wk_ref, wv_ref, wo_ref,
    out_ref, normed_t_ref, grads_ref, ctx_t, gq_t, gk_ref, gv_ref,
):
    gain = gain_ref[1:2, :]
    pick = select_rows(384, 384, unpacked_source)
    tiles = [nn(pick, packed_ref[384 * t : 384 * t + 384, :]) for t in range(4)]
    rows = jnp.concatenate(
        [
            jnp.concatenate(
                [tiles[t][c * 128 + 32 * p : c * 128 + 32 * p + 32] for c in range(2)], axis=1
            )
            for p in range(4)
            for t in range(4)
        ],
        axis=0,
    )
    hops = [
        jnp.concatenate(
            [
                jnp.concatenate(
                    [tiles[t][256 + c * 64 + 32 * r : 256 + c * 64 + 32 * r + 32] for c in range(2)],
                    axis=1,
                )
                for t in range(4)
            ],
            axis=0,
        )
        for r in range(2)
    ]
    last = jnp.zeros((1, D), F32)
    late = [jnp.concatenate([hop[1:], last], axis=0) for hop in hops]
    grads = jnp.concatenate(hops + late, axis=0).astype(BF)
    grads_ref[...] = grads
    unit, inverse = standardize(rows)
    normed = (unit * gain).astype(BF)
    normed_t_ref[...] = normed.T
    wq, wk, wv, wo = wq_ref[1], wk_ref[1], wv_ref[1], wo_ref[1]
    queries = nn(normed, wq).astype(BF)
    keys = nn(normed, wk).astype(BF)
    values = nn(normed, wv).astype(BF)
    grad_context = nt(grads, wo).astype(BF)
    queries_t = queries.T
    keys_t = keys.T
    values_t = values.T
    grad_context_t = grad_context.T
    masks = head_masks()
    downs = row_masks()

    def place(step):
        p, b = step // 2, step % 2
        return slice(128 * p, 128 * p + 128), slice(128 * b, 128 * b + 128)

    def columns(rows_t):
        return jnp.concatenate([rows_t * down for down in downs], axis=1)

    def stacked(rows):
        return jnp.concatenate([rows * mask for mask in masks], axis=0)

    def products(step):
        at, block = place(step)
        scores = nn(keys[at, block], columns(queries_t[block, at]))
        grad_probs = nn(values[at, block], columns(grad_context_t[block, at]))
        return scores, grad_probs

    def weigh(step, held):
        scores, grad_probs = held
        probs = softmax_keys(scores)
        inner = jnp.sum(grad_probs * probs, axis=0, keepdims=True)
        return probs.astype(BF), (probs * (grad_probs - inner) * SCALE).astype(BF)

    def collect(step, held):
        low, grad_scores = held
        at, block = place(step)
        gv_ref[at, block] = nn(low, stacked(grad_context[at, block])).astype(BF)
        gk_ref[at, block] = nn(grad_scores, stacked(queries[at, block])).astype(BF)
        for i in range(4):
            feats = slice(block.start + HEAD * i, block.start + HEAD * i + HEAD)
            cols = slice(128 * i, 128 * i + 128)
            ctx_t[feats, at] = nn(values_t[feats, at], low[:, cols]).astype(BF)
            gq_t[feats, at] = nn(keys_t[feats, at], grad_scores[:, cols]).astype(BF)

    staged(8, products, weigh, collect)
    gqt, gk, gv = gq_t[...], gk_ref[...], gv_ref[...]
    grad_normed = nt(gqt.T, wq) + nt(gk, wk) + nt(gv, wv)
    result = (grads.astype(F32) + norm_pullback(grad_normed, unit, inverse, gain)).astype(BF)
    back = select_rows(256, 256, segment_target)
    for t in range(2):
        part = jnp.concatenate(
            [result[128 * p + 64 * t : 128 * p + 64 * t + 64] for p in range(4)], axis=0
        )
        out_ref[256 * t : 256 * t + 256, :] = nn(back, part).astype(BF)


def inter(packed, gains, wq, wk, wv, wo):
    return pl.pallas_call(
        inter_kernel,
        out_shape=(
            bf16(512, D), bf16(D, 512), bf16(512, D), bf16(D, 512), bf16(D, 512), bf16(512, D),
            bf16(512, D),
        ),
        compiler_params=params(),
        cost_estimate=cost(9),
        name="inter",
    )(packed, gains, wq, wk, wv, wo)


def split_by_core(core_ref, weights, keep_ref, send_ref):
    low_core = core_ref[0] == 0
    for i in range(2):
        keep_ref[i] = jnp.where(low_core, weights[i], weights[2 + i])
        send_ref[i] = jnp.where(low_core, weights[2 + i], weights[i]).astype(BF)


def inter_weights_kernel(
    core_ref, normed_t_ref, grads_ref, ctx_t_ref, gq_t_ref, gk_ref, gv_ref, keep_ref, send_ref
):
    normed_t = normed_t_ref[...]
    weights = (
        nt(normed_t, gq_t_ref[...]),
        nn(normed_t, gk_ref[...]),
        nn(normed_t, gv_ref[...]),
        nn(ctx_t_ref[...], grads_ref[...]),
    )
    split_by_core(core_ref, weights, keep_ref, send_ref)


def specs(count):
    vmem = pl.BlockSpec(memory_space=pltpu.VMEM)
    return [pl.BlockSpec(memory_space=pltpu.SMEM)] + [vmem] * count


def inter_weights(core, *operands):
    return pl.pallas_call(
        inter_weights_kernel,
        in_specs=specs(6),
        out_shape=(f32(2, D, D), bf16(2, D, D)),
        compiler_params=params(),
        cost_estimate=cost(1),
        name="inter_weights",
    )(core, *operands)


def intra_prepare_kernel(
    f_ref, n_ref, gain_ref, wq_ref, wk_ref, wv_ref,
    normed_t_ref, queries_ref, keys_t_ref, values_ref, probs_ref,
):
    rows = jnp.concatenate([f_ref[...], n_ref[...]], axis=0).astype(F32)
    unit, _ = standardize(rows)
    normed = (unit * gain_ref[0:1, :]).astype(BF)
    normed_t_ref[...] = normed.T
    queries = nn(normed, wq_ref[0]).astype(BF)
    keys = nn(normed, wk_ref[0]).astype(BF)
    queries_ref[...] = queries
    values_ref[...] = nn(normed, wv_ref[0]).astype(BF)
    queries_t = queries.T
    keys_t_ref[...] = keys.T
    masks = head_masks()

    def scores_of(step):
        g, h = step // HEADS, step % HEADS
        at = slice(g * HOP, g * HOP + K)
        block = slice((h // 4) * 128, (h // 4) * 128 + 128)
        return nn(keys[at, block] * masks[h % 4], queries_t[block, at])

    def weigh(step, scores):
        probs_ref[step] = softmax_keys(scores)

    staged(2 * HEADS, scores_of, weigh)


def intra_prepare(frames, following, gains, wq, wk, wv):
    return pl.pallas_call(
        intra_prepare_kernel,
        out_shape=(
            bf16(D, 3 * HOP), bf16(3 * HOP, D), bf16(D, 3 * HOP), bf16(3 * HOP, D),
            f32(2 * HEADS, K, K),
        ),
        compiler_params=params(),
        cost_estimate=cost(4),
        name="intra_prepare",
    )(frames, following, gains, wq, wk, wv)


def intra_backward_kernel(
    core_ref, m_ref, ctx_a_ref, ctx_b_ref, normed_t_ref, queries_ref, keys_t_ref, values_ref,
    probs_ref, wo_ref,
    keep_ref, send_ref, grads_ref, gq_t, gk_ref, gv_ref,
):
    pick = select_rows(256, 256, owner_target)
    tiles = [nn(pick, m_ref[256 * t : 256 * t + 256, :]).astype(BF) for t in range(2)]
    masks = head_masks()
    context, context_t = [], []
    for g in range(2):
        grads_ref[g] = jnp.concatenate(
            [tiles[t][128 * g + 64 * h : 128 * g + 64 * h + 64] for h in range(2) for t in range(2)],
            axis=0,
        )
        context.append(nt(grads_ref[g], wo_ref[0]).astype(BF))
        context_t.append(context[g].T)

    def place(step):
        g, h = step // HEADS, step % HEADS
        return g, slice(g * HOP, g * HOP + K), h // 4, h % 4

    def products(step):
        g, at, b, i = place(step)
        block = slice(128 * b, 128 * b + 128)
        return nn(values_ref[at, block] * masks[i], context_t[g][block, :])

    def weigh(step, grad_probs):
        probs = probs_ref[step]
        inner = jnp.sum(grad_probs * probs, axis=0, keepdims=True)
        return probs.astype(BF), (probs * (grad_probs - inner) * SCALE).astype(BF)

    sums = {}

    def collect(step, held):
        low, grad_scores = held
        g, at, b, i = place(step)
        block = slice(128 * b, 128 * b + 128)
        feats = slice(128 * b + HEAD * i, 128 * b + HEAD * i + HEAD)
        gv = nn(low, context[g][:, block] * masks[i])
        gk = nn(grad_scores, queries_ref[at, block] * masks[i])
        gq_t[g, feats, :] = nn(keys_t_ref[feats, at], grad_scores).astype(BF)
        sums["v"] = gv if i == 0 else sums["v"] + gv
        sums["k"] = gk if i == 0 else sums["k"] + gk
        if i == 3:
            gv_ref[g, :, block] = sums["v"].astype(BF)
            gk_ref[g, :, block] = sums["k"].astype(BF)

    staged(2 * HEADS, products, weigh, collect)
    contexts = (ctx_a_ref, ctx_b_ref)
    parts = [
        (
            nt(normed_t_ref[:, g * HOP : g * HOP + K], gq_t[g]),
            nn(normed_t_ref[:, g * HOP : g * HOP + K], gk_ref[g]),
            nn(normed_t_ref[:, g * HOP : g * HOP + K], gv_ref[g]),
            nn(contexts[g][...], grads_ref[g]),
        )
        for g in range(2)
    ]
    totals = [first + second for first, second in zip(*parts)]
    split_by_core(core_ref, totals, keep_ref, send_ref)


def intra_backward(core, grads, ctx_a, ctx_b, *rest):
    return pl.pallas_call(
        intra_backward_kernel,
        in_specs=specs(9),
        out_shape=(
            f32(2, D, D), bf16(2, D, D), bf16(2, K, D), bf16(2, D, K), bf16(2, K, D), bf16(2, K, D),
        ),
        compiler_params=params(),
        cost_estimate=cost(6),
        name="intra_backward",
    )(core, grads, ctx_a, ctx_b, *rest)


def intra_tail_kernel(
    grads_ref, gq_t_ref, gk_ref, gv_ref, f_ref, n_ref, gain_ref, wq_ref, wk_ref, wv_ref,
    first_ref, second_ref, carry_ref,
):
    rows = jnp.concatenate([f_ref[...], n_ref[...]], axis=0).astype(F32)
    unit, inverse = standardize(rows)
    halves = []
    for g in range(2):
        at = slice(g * HOP, g * HOP + K)
        grad_normed = (
            nt(gq_t_ref[g].T, wq_ref[0]) + nt(gk_ref[g], wk_ref[0]) + nt(gv_ref[g], wv_ref[0])
        )
        pulled = norm_pullback(grad_normed, unit[at], inverse[at], gain_ref[0:1, :])
        result = (grads_ref[g].astype(F32) + pulled).astype(BF)
        halves.append((result[:HOP], result[HOP:]))
    first_ref[...] = halves[0][0]
    second_ref[...] = (halves[1][0].astype(F32) + halves[0][1].astype(F32)).astype(BF)
    carry_ref[...] = halves[1][1]


def intra_tail(*operands):
    return pl.pallas_call(
        intra_tail_kernel,
        out_shape=(bf16(HOP, D), bf16(HOP, D), bf16(HOP, D)),
        compiler_params=params(),
        cost_estimate=cost(2),
        name="intra_tail",
    )(*operands)


def finish_kernel(
    core_ref, mine_ref, other_ref, first_ref, second_ref, carried_ref, gain_ref, wq_ref, wk_ref, wv_ref,
    frames_ref, dq_ref, dk_ref, dv_ref, do_ref, dg_ref,
):
    frames_ref[:HOP] = (first_ref[...].astype(F32) + carried_ref[...].astype(F32)).astype(BF)
    frames_ref[HOP:] = second_ref[...]
    low_core = core_ref[0] == 0
    for layer in range(2):
        mine = mine_ref[:, layer].reshape(2, D, D).astype(F32)
        other = other_ref[:, layer].reshape(2, D, D).astype(F32)
        dq = jnp.where(low_core, mine[0], other[0])
        dk = jnp.where(low_core, mine[1], other[1])
        dv = jnp.where(low_core, other[0], mine[0])
        dq_ref[layer] = dq
        dk_ref[layer] = dk
        dv_ref[layer] = dv
        do_ref[layer] = jnp.where(low_core, other[1], mine[1])
        through = (
            dq * wq_ref[layer].astype(F32)
            + dk * wk_ref[layer].astype(F32)
            + dv * wv_ref[layer].astype(F32)
        )
        column = jnp.sum(through.T, axis=0, keepdims=True)
        dg_ref[layer : layer + 1, :] = column / gain_ref[layer : layer + 1, :]


def finish(core, mine, other, first, second, carried, gains, wq, wk, wv):
    full = f32(2, D, D)
    return pl.pallas_call(
        finish_kernel,
        in_specs=specs(9),
        out_shape=(bf16(K, D), full, full, full, full, f32(2, D)),
        compiler_params=params(),
        cost_estimate=cost(2),
        name="finish",
    )(core, mine, other, first, second, carried, gains, wq, wk, wv)


def shifted(shard, by):
    length = lax.axis_size(TM)
    pairs = [(i, i + by) for i in range(length) if 0 <= i + by < length]
    return lax.ppermute(shard, TM, pairs)


def exchanged(shard, axes):
    return lax.all_to_all(shard, axes, split_axis=0, concat_axis=0, tiled=True)


def swapped(shard):
    return lax.ppermute(shard, "core", [(0, 1), (1, 0)])


def copies(piece, count):
    return jnp.broadcast_to(piece[None], (count,) + piece.shape)


def summed(pieces):
    return jnp.sum(pieces.astype(F32), axis=0).astype(BF)


def core_sum(keep, send):
    return (keep + swapped(send).astype(F32)).astype(BF).reshape(16, 32, D)


def shards(frames, frames_grad, wq, wk, wv, wo, gains):
    frames = frames[0]
    core = lax.axis_index("core").astype(jnp.int32).reshape(1)
    following = shifted(frames[:HOP], -1)
    mid, ctx_a, *front = intra_first(frames, gains, wq, wk, wv, wo)
    packed, ctx_b = intra_second(
        frames, following, frames_grad[0], mid, *front, gains, wq, wk, wv, wo
    )
    across = exchanged(packed.reshape(64, 24, 128), TM).reshape(64 * 24, 128)
    grad_middle, *operands = inter(across, gains, wq, wk, wv, wo)
    grad_local = exchanged(grad_middle.reshape(64, 8, D), TM).reshape(512, D)
    inter_half = core_sum(*inter_weights(core, *operands))
    prepared = intra_prepare(frames, following, gains, wq, wk, wv)
    keep, send, *rest = intra_backward(core, grad_local, ctx_a, ctx_b, *prepared, wo)
    half = jnp.concatenate([core_sum(keep, send), inter_half], axis=1)
    first, second, carry = intra_tail(*rest, frames, following, gains, wq, wk, wv)
    carried = shifted(carry, 1)
    pieces = exchanged(half, PLANE)
    piece = summed(pieces)
    pieces = exchanged(copies(piece, 8), "z")
    pieces, carried = lax.optimization_barrier((pieces, carried))
    piece = summed(pieces)
    whole = exchanged(copies(piece, 16), PLANE).reshape(16, 2, 32, D)
    other = swapped(whole)
    grad_frames, *weights = finish(
        core, whole, other, first, second, carried, gains, wq, wk, wv
    )
    return (grad_frames[None], *weights)


def solution(mesh):
    split = Mesh(mesh.devices.reshape(2, 2, 2, 4, 8), AXES)
    placed = (P(DP, TM, None), P(DP, TM, None), P(), P(), P(), P(), P())
    return jax.shard_map(
        shards,
        mesh=split,
        in_specs=placed,
        out_specs=(P(DP, TM, None), P(), P(), P(), P(), P()),
        check_vma=False,
    )
```

```python
import math

import jax
import jax.numpy as jnp
from jax import lax
from jax.experimental import pallas as pl
from jax.experimental.pallas import tpu as pltpu
from jax.sharding import Mesh, PartitionSpec as P

HEADS = 8
HEAD = 32
D = 256
K = 256
HOP = 128
SEGMENTS = 128
EPSILON = 1e-05
SCALE = HEAD ** (-0.5)
LOG2E = math.log2(math.e)
BF = jnp.bfloat16
F32 = jnp.float32
VMEM_LIMIT = 16 * 1024 * 1024
WHOLE_LIMIT = 62 * 1024 * 1024
PREPARE_LIMIT = 56 * 1024 * 1024
BACKWARD_LIMIT = 16 * 1024 * 1024

AXES = ("yh", "core", "yl", "x", "z")
DP = ("yh", "core")
TM = ("yl", "x", "z")
PLANE = ("yh", "yl", "x")


def dot(left, right, left_dim, right_dim):
    return lax.dot_general(
        left, right, (((left_dim,), (right_dim,)), ((), ())), preferred_element_type=F32
    )


def nn(left, right):
    return dot(left, right, 1, 0)


def nt(left, right):
    return dot(left, right, 1, 1)


def tn(left, right):
    return dot(left, right, 0, 0)


def standardize(rows):
    average = jnp.mean(rows, axis=-1, keepdims=True)
    centered = rows - average
    variance = jnp.mean(centered * centered, axis=-1, keepdims=True)
    inverse = lax.rsqrt(variance + EPSILON)
    return centered * inverse, inverse


def norm_pullback(grad_normed, unit, inverse, gain):
    grad_unit = grad_normed * gain
    first = jnp.mean(grad_unit, axis=-1, keepdims=True)
    second = jnp.mean(grad_unit * unit, axis=-1, keepdims=True)
    return inverse * (grad_unit - first - unit * second)


def head_masks():
    lane = lax.broadcasted_iota(jnp.int32, (1, 128), 1)
    return [jnp.where(lane // HEAD == i, 1.0, 0.0).astype(BF) for i in range(4)]


def row_masks():
    row = lax.broadcasted_iota(jnp.int32, (128, 1), 0)
    return [jnp.where(row // HEAD == i, 1.0, 0.0).astype(BF) for i in range(4)]


def select_rows(out_rows, in_rows, source):
    out = lax.broadcasted_iota(jnp.int32, (out_rows, in_rows), 0)
    col = lax.broadcasted_iota(jnp.int32, (out_rows, in_rows), 1)
    return jnp.where(source(out) == col, 1.0, 0.0).astype(BF)


def softmax_keys(scores):
    highest = jnp.max(scores, axis=0, keepdims=True)
    powers = jnp.exp2((scores - highest) * (SCALE * LOG2E))
    return powers * (1.0 / jnp.sum(powers, axis=0, keepdims=True))


def owner_target(out):
    return ((out % 64) // 2) * 8 + (out // 64) * 2 + out % 2


def segment_target(out):
    return (out % 4) * 64 + out // 4


def packed_source(out):
    device, row = out // 24, out % 24
    part = row % 8
    middle = (row // 8) * 128 + (part // 2) * 32 + device * 2 + part % 2
    rest = row - 16
    grads = 256 + (rest // 4) * 64 + ((rest % 4) // 2) * 32 + device * 2 + rest % 2
    return jnp.where(row < 16, middle, grads)


def unpacked_source(out):
    column, place = out // 128, out % 128
    segment = place % 32
    middle = (segment // 2) * 24 + column * 8 + (segment % 2) * 4 + place // 32
    rest = out - 256
    column, place = rest // 64, rest % 64
    segment = place % 32
    grads = (segment // 2) * 24 + 16 + column * 4 + (segment % 2) * 2 + place // 32
    return jnp.where(out < 256, middle, grads)


def staged(count, *stages):
    held = [{} for _ in stages]
    for t in range(count + len(stages) - 1):
        for i, stage in enumerate(stages):
            step = t - i
            if 0 <= step < count:
                held[i][step] = stage(step, *([held[i - 1].pop(step)] if i else []))


def attend(keys, queries_t, values_t, ctx_ref):
    masks = head_masks()

    def scores_of(h):
        block = slice((h // 4) * 128, (h // 4) * 128 + 128)
        return nn(keys[:, block] * masks[h % 4], queries_t[block, :])

    def weigh(h, scores):
        return softmax_keys(scores).astype(BF)

    def collect(h, low):
        feats = slice(h * HEAD, h * HEAD + HEAD)
        ctx_ref[feats, :] = nn(values_t[feats, :], low).astype(BF)

    staged(HEADS, scores_of, weigh, collect)


VMEM = pl.BlockSpec(memory_space=pltpu.VMEM)
SMEM = pl.BlockSpec(memory_space=pltpu.SMEM)
HBM = pl.BlockSpec(memory_space=pltpu.HBM)


def begin(sems, *pairs):
    copies = [pltpu.make_async_copy(src, dst, sems.at[i]) for i, (src, dst) in enumerate(pairs)]
    for copy in copies:
        copy.start()
    return copies


def settle(copies):
    for copy in copies:
        copy.wait()


def bf16(*shape):
    return jax.ShapeDtypeStruct(shape, BF)


def f32(*shape):
    return jax.ShapeDtypeStruct(shape, F32)


def kernel_call(kernel, name, micros, in_specs, out_specs, out_shape, scratch, limit=VMEM_LIMIT):
    return pl.pallas_call(
        kernel,
        in_specs=in_specs,
        out_specs=out_specs,
        out_shape=out_shape,
        scratch_shapes=scratch,
        compiler_params=pltpu.CompilerParams(vmem_limit_bytes=limit),
        cost_estimate=pl.CostEstimate(
            flops=int(micros * 400e6), bytes_accessed=1 << 20, transcendentals=0
        ),
        name=name,
    )


def dma(count):
    return pltpu.SemaphoreType.DMA((count,))


def vbf(*shape):
    return pltpu.VMEM(shape, BF)


def intra_first_kernel(
    f_any, gain_any, wq_any, wk_any, wv_any, wo_any,
    mid_ref, keys_ref, queries_ref, values_ref,
    w_ref, gain_ref, f_ref, ctx_ref, sems,
):
    copies = begin(
        sems,
        (f_any, f_ref),
        (gain_any, gain_ref),
        (wk_any.at[0], w_ref.at[1]),
        (wq_any.at[0], w_ref.at[0]),
        (wv_any.at[0], w_ref.at[2]),
        (wo_any.at[0], w_ref.at[3]),
    )
    copies[0].wait()
    rows = f_ref[...].astype(F32)
    unit, _ = standardize(rows)
    copies[1].wait()
    normed = (unit * gain_ref[0:1, :]).astype(BF)
    settle(copies[2:5])
    keys = nn(normed, w_ref[1]).astype(BF)
    queries_t = nt(w_ref[0].T, normed).astype(BF)
    values_t = nt(w_ref[2].T, normed).astype(BF)
    attend(keys, queries_t, values_t, ctx_ref)
    copies[5].wait()
    mid_ref[...] = (rows + tn(ctx_ref[...], w_ref[3])).astype(BF)
    keys_ref[...] = keys[HOP:]
    queries_ref[...] = queries_t[:, HOP:]
    values_ref[...] = values_t[:, HOP:]


def intra_second_kernel(
    n_any, f_any, grad_any, mid_any, keys_any, queries_any, values_any,
    gain_any, wq_any, wk_any, wv_any, wo_any, packed_ref,
    n_ref, f_ref, grad_ref, mid_in_ref, keys_ref, queries_ref, values_ref, gain_ref, w_ref, ctx_ref, sems,
):
    copies = begin(
        sems,
        (n_any.at[pl.ds(0, HOP)], n_ref),
        (gain_any, gain_ref),
        (wk_any.at[0], w_ref.at[1]),
        (wq_any.at[0], w_ref.at[0]),
        (wv_any.at[0], w_ref.at[2]),
        (keys_any, keys_ref),
        (queries_any, queries_ref),
        (values_any, values_ref),
        (wo_any.at[0], w_ref.at[3]),
        (mid_any, mid_in_ref),
        (f_any.at[pl.ds(HOP, HOP)], f_ref),
        (grad_any, grad_ref),
    )
    copies[0].wait()
    rows = n_ref[...].astype(F32)
    unit, _ = standardize(rows)
    settle(copies[1:8])
    normed = (unit * gain_ref[0:1, :]).astype(BF)
    keys = jnp.concatenate([keys_ref[...], nn(normed, w_ref[1]).astype(BF)], axis=0)
    queries_t = jnp.concatenate(
        [queries_ref[...], nt(w_ref[0].T, normed).astype(BF)], axis=1
    )
    values_t = jnp.concatenate([values_ref[...], nt(w_ref[2].T, normed).astype(BF)], axis=1)
    attend(keys, queries_t, values_t, ctx_ref)
    settle(copies[8:])
    rows = jnp.concatenate([f_ref[...].astype(F32), rows], axis=0)
    mids = (mid_in_ref[...], (rows + tn(ctx_ref[...], w_ref[3])).astype(BF))
    grads = grad_ref[...]
    pick = select_rows(384, 384, packed_source)
    for t in range(4):
        middle = jnp.concatenate(
            [mids[g][h * HOP + 32 * t : h * HOP + 32 * t + 32] for g in range(2) for h in range(2)],
            axis=0,
        )
        cotangent = jnp.concatenate(
            [grads[h * HOP + 32 * t : h * HOP + 32 * t + 32] for h in range(2)], axis=0
        )
        part = jnp.concatenate(
            [middle[:, :128], middle[:, 128:], cotangent[:, :128], cotangent[:, 128:]], axis=0
        )
        packed_ref[384 * t : 384 * t + 384, :] = nn(pick, part).astype(BF)


def intra_first(frames, gains, wq, wk, wv, wo):
    return kernel_call(
        intra_first_kernel, "intra_first", 3, [HBM] * 6, [VMEM] * 4,
        (bf16(K, D), bf16(HOP, D), bf16(D, HOP), bf16(D, HOP)),
        [vbf(4, D, D), pltpu.VMEM((2, D), F32), vbf(K, D), vbf(D, K), dma(6)],
        WHOLE_LIMIT,
    )(frames, gains, wq, wk, wv, wo)


def intra_second(following, frames, grads, *rest):
    return kernel_call(
        intra_second_kernel, "intra_second", 3, [HBM] * 12, VMEM, bf16(64 * 24, 128),
        [
            vbf(HOP, D), vbf(HOP, D), vbf(K, D), vbf(K, D), vbf(HOP, D), vbf(D, HOP), vbf(D, HOP),
            pltpu.VMEM((2, D), F32), vbf(4, D, D), vbf(D, K), dma(12),
        ],
        WHOLE_LIMIT,
    )(following, frames, grads, *rest)


def inter_kernel(
    packed_ref, gain_ref, wq_ref, wk_ref, wv_ref, wo_ref,
    out_ref, normed_t_ref, grads_ref, ctx_t, gq_t, gk_ref, gv_ref,
):
    gain = gain_ref[1:2, :]
    pick = select_rows(384, 384, unpacked_source)
    tiles = [nn(pick, packed_ref[384 * t : 384 * t + 384, :]) for t in range(4)]
    rows = jnp.concatenate(
        [
            jnp.concatenate(
                [tiles[t][c * 128 + 32 * p : c * 128 + 32 * p + 32] for c in range(2)], axis=1
            )
            for p in range(4)
            for t in range(4)
        ],
        axis=0,
    )
    hops = [
        jnp.concatenate(
            [
                jnp.concatenate(
                    [tiles[t][256 + c * 64 + 32 * r : 256 + c * 64 + 32 * r + 32] for c in range(2)],
                    axis=1,
                )
                for t in range(4)
            ],
            axis=0,
        )
        for r in range(2)
    ]
    last = jnp.zeros((1, D), F32)
    late = [jnp.concatenate([hop[1:], last], axis=0) for hop in hops]
    grads = jnp.concatenate(hops + late, axis=0).astype(BF)
    grads_ref[...] = grads
    unit, inverse = standardize(rows)
    normed = (unit * gain).astype(BF)
    normed_t_ref[...] = normed.T
    wq, wk, wv, wo = wq_ref[1], wk_ref[1], wv_ref[1], wo_ref[1]
    queries = nn(normed, wq).astype(BF)
    keys = nn(normed, wk).astype(BF)
    values = nn(normed, wv).astype(BF)
    grad_context = nt(grads, wo).astype(BF)
    queries_t = queries.T
    keys_t = keys.T
    values_t = values.T
    grad_context_t = grad_context.T
    masks = head_masks()
    downs = row_masks()

    def place(step):
        p, b = step // 2, step % 2
        return slice(128 * p, 128 * p + 128), slice(128 * b, 128 * b + 128)

    def columns(rows_t):
        return jnp.concatenate([rows_t * down for down in downs], axis=1)

    def stacked(rows):
        return jnp.concatenate([rows * mask for mask in masks], axis=0)

    def products(step):
        at, block = place(step)
        scores = nn(keys[at, block], columns(queries_t[block, at]))
        grad_probs = nn(values[at, block], columns(grad_context_t[block, at]))
        return scores, grad_probs

    def weigh(step, held):
        scores, grad_probs = held
        probs = softmax_keys(scores)
        inner = jnp.sum(grad_probs * probs, axis=0, keepdims=True)
        return probs.astype(BF), (probs * (grad_probs - inner) * SCALE).astype(BF)

    def collect(step, held):
        low, grad_scores = held
        at, block = place(step)
        gv_ref[at, block] = nn(low, stacked(grad_context[at, block])).astype(BF)
        gk_ref[at, block] = nn(grad_scores, stacked(queries[at, block])).astype(BF)
        for i in range(4):
            feats = slice(block.start + HEAD * i, block.start + HEAD * i + HEAD)
            cols = slice(128 * i, 128 * i + 128)
            ctx_t[feats, at] = nn(values_t[feats, at], low[:, cols]).astype(BF)
            gq_t[feats, at] = nn(keys_t[feats, at], grad_scores[:, cols]).astype(BF)

    staged(8, products, weigh, collect)
    gqt, gk, gv = gq_t[...], gk_ref[...], gv_ref[...]
    grad_normed = nt(gqt.T, wq) + nt(gk, wk) + nt(gv, wv)
    result = (grads.astype(F32) + norm_pullback(grad_normed, unit, inverse, gain)).astype(BF)
    back = select_rows(256, 256, segment_target)
    for t in range(2):
        part = jnp.concatenate(
            [result[128 * p + 64 * t : 128 * p + 64 * t + 64] for p in range(4)], axis=0
        )
        out_ref[256 * t : 256 * t + 256, :] = nn(back, part).astype(BF)


def inter(packed, gains, wq, wk, wv, wo):
    return kernel_call(
        inter_kernel, "inter", 5, [VMEM] * 6, [VMEM] * 7,
        (
            bf16(512, D), bf16(D, 512), bf16(512, D), bf16(D, 512), bf16(D, 512), bf16(512, D),
            bf16(512, D),
        ),
        [],
    )(packed, gains, wq, wk, wv, wo)


def split_by_core(core_ref, weights, keep_ref, send_ref):
    low_core = core_ref[0] == 0
    for i in range(2):
        keep_ref[i] = jnp.where(low_core, weights[i], weights[2 + i])
        send_ref[i] = jnp.where(low_core, weights[2 + i], weights[i]).astype(BF)


def inter_weights_kernel(
    core_ref, normed_t_ref, grads_ref, ctx_t_ref, gq_t_ref, gk_ref, gv_ref, keep_ref, send_ref
):
    normed_t = normed_t_ref[...]
    weights = (
        nt(normed_t, gq_t_ref[...]),
        nn(normed_t, gk_ref[...]),
        nn(normed_t, gv_ref[...]),
        nn(ctx_t_ref[...], grads_ref[...]),
    )
    split_by_core(core_ref, weights, keep_ref, send_ref)


def inter_weights(core, *operands):
    return kernel_call(
        inter_weights_kernel, "inter_weights", 1, [SMEM] + [VMEM] * 6, [VMEM] * 2,
        (f32(2, D, D), bf16(2, D, D)), [],
    )(core, *operands)


NORMED_T, QUERIES, QUERIES_T, KEYS, KEYS_T, VALUES, CONTEXT = (768 * i for i in range(7))
HANDED_ROWS = 768 * 6 + 1024


def put_blocks(handed_ref, start, array):
    for i in range(array.shape[1] // 128):
        at = start + i * array.shape[0]
        handed_ref[at : at + array.shape[0], :] = array[:, 128 * i : 128 * i + 128]


def features_of(handed_ref, start, rows, at):
    return jnp.concatenate(
        [
            handed_ref[start + 256 * i + rows.start : start + 256 * i + rows.stop, :]
            for i in range(at.start // 128, at.stop // 128)
        ],
        axis=1,
    )


def tokens_of(handed_ref, start, at, b):
    return handed_ref[start + 384 * b + at.start : start + 384 * b + at.stop, :]


def begin_layer(sems, f_any, n_any, gain_any, wq_any, wk_any, wv_any, rows_ref, gain_ref, w_ref):
    return begin(
        sems,
        (f_any, rows_ref.at[pl.ds(0, K)]),
        (n_any.at[pl.ds(0, HOP)], rows_ref.at[pl.ds(K, HOP)]),
        (gain_any, gain_ref),
        (wq_any.at[0], w_ref.at[0]),
        (wk_any.at[0], w_ref.at[1]),
        (wv_any.at[0], w_ref.at[2]),
    )


def layer_scratch():
    return [vbf(3 * HOP, D), pltpu.VMEM((2, D), F32), vbf(3, D, D)]


def intra_prepare_kernel(
    f_any, n_any, gain_any, wq_any, wk_any, wv_any, handed_ref, stats_ref,
    ctx_ref, rows_ref, gain_ref, w_ref, sems,
):
    settle(begin_layer(sems, f_any, n_any, gain_any, wq_any, wk_any, wv_any, rows_ref, gain_ref, w_ref))
    unit, _ = standardize(rows_ref[...].astype(F32))
    normed = (unit * gain_ref[0:1, :]).astype(BF)
    queries = nn(normed, w_ref[0]).astype(BF)
    keys = nn(normed, w_ref[1]).astype(BF)
    values = nn(normed, w_ref[2]).astype(BF)
    queries_t = queries.T
    values_t = values.T
    put_blocks(handed_ref, NORMED_T, normed.T)
    put_blocks(handed_ref, QUERIES, queries)
    put_blocks(handed_ref, QUERIES_T, queries_t)
    put_blocks(handed_ref, KEYS, keys)
    put_blocks(handed_ref, KEYS_T, keys.T)
    put_blocks(handed_ref, VALUES, values)
    masks = head_masks()

    def scores_of(step):
        g, h = step // HEADS, step % HEADS
        at = slice(g * HOP, g * HOP + K)
        block = slice((h // 4) * 128, (h // 4) * 128 + 128)
        return nn(keys[at, block] * masks[h % 4], queries_t[block, at])

    def weigh(step, scores):
        highest = jnp.max(scores, axis=0, keepdims=True)
        powers = jnp.exp2((scores - highest) * (SCALE * LOG2E))
        inverse = 1.0 / jnp.sum(powers, axis=0, keepdims=True)
        stats_ref[2 * step : 2 * step + 1, :] = highest
        stats_ref[2 * step + 1 : 2 * step + 2, :] = inverse
        return (powers * inverse).astype(BF)

    def collect(step, low):
        g, h = step // HEADS, step % HEADS
        feats = slice(h * HEAD, h * HEAD + HEAD)
        ctx_ref[g, feats, :] = nn(values_t[feats, g * HOP : g * HOP + K], low).astype(BF)

    staged(2 * HEADS, scores_of, weigh, collect)
    for g in range(2):
        put_blocks(handed_ref, CONTEXT + 512 * g, ctx_ref[g])


def intra_prepare(frames, following, gains, wq, wk, wv):
    return kernel_call(
        intra_prepare_kernel, "intra_prepare", 3, [HBM] * 6, [VMEM] * 2,
        (bf16(HANDED_ROWS, 128), f32(4 * HEADS, K)),
        [vbf(2, D, K)] + layer_scratch() + [dma(6)],
        PREPARE_LIMIT,
    )(frames, following, gains, wq, wk, wv)


def intra_backward_kernel(
    core_ref, m_ref, handed_any, stats_any, wo_any,
    keep_ref, send_ref, grads_ref, gq_t, gk_ref, gv_ref,
    handed_ref, stats_ref, wo_ref, sems,
):
    copies = begin(
        sems, (wo_any.at[0], wo_ref), (stats_any, stats_ref), (handed_any, handed_ref)
    )
    pick = select_rows(256, 256, owner_target)
    tiles = [nn(pick, m_ref[256 * t : 256 * t + 256, :]).astype(BF) for t in range(2)]
    masks = head_masks()
    context, context_t = [], []
    for g in range(2):
        grads_ref[g] = jnp.concatenate(
            [tiles[t][128 * g + 64 * h : 128 * g + 64 * h + 64] for h in range(2) for t in range(2)],
            axis=0,
        )
        if g == 0:
            copies[0].wait()
        context.append(nt(grads_ref[g], wo_ref[...]).astype(BF))
        context_t.append(context[g].T)

    settle(copies[1:])

    def place(step):
        g, h = step // HEADS, step % HEADS
        return g, slice(g * HOP, g * HOP + K), h // 4, h % 4

    def products(step):
        g, at, b, i = place(step)
        block = slice(128 * b, 128 * b + 128)
        keys = tokens_of(handed_ref, KEYS, at, b) * masks[i]
        scores = nn(keys, features_of(handed_ref, QUERIES_T, block, at))
        values = tokens_of(handed_ref, VALUES, at, b) * masks[i]
        return scores, nn(values, context_t[g][block, :])

    def weigh(step, held):
        scores, grad_probs = held
        powers = jnp.exp2((scores - stats_ref[2 * step : 2 * step + 1, :]) * (SCALE * LOG2E))
        probs = powers * stats_ref[2 * step + 1 : 2 * step + 2, :]
        inner = jnp.sum(grad_probs * probs, axis=0, keepdims=True)
        return probs.astype(BF), (probs * (grad_probs - inner) * SCALE).astype(BF)

    sums = {}

    def collect(step, held):
        low, grad_scores = held
        g, at, b, i = place(step)
        block = slice(128 * b, 128 * b + 128)
        feats = slice(128 * b + HEAD * i, 128 * b + HEAD * i + HEAD)
        gv = nn(low, context[g][:, block] * masks[i])
        gk = nn(grad_scores, tokens_of(handed_ref, QUERIES, at, b) * masks[i])
        keys_t = features_of(handed_ref, KEYS_T, feats, at)
        gq_t[g, feats, :] = nn(keys_t, grad_scores).astype(BF)
        sums["v"] = gv if i == 0 else sums["v"] + gv
        sums["k"] = gk if i == 0 else sums["k"] + gk
        if i == 3:
            gv_ref[g, :, block] = sums["v"].astype(BF)
            gk_ref[g, :, block] = sums["k"].astype(BF)

    staged(2 * HEADS, products, weigh, collect)
    parts = []
    for g in range(2):
        normed_t = features_of(
            handed_ref, NORMED_T, slice(0, D), slice(g * HOP, g * HOP + K)
        )
        context_0 = jnp.concatenate(
            [handed_ref[pl.ds(CONTEXT + 512 * g + 256 * i, 256), :] for i in range(2)], axis=1
        )
        parts.append(
            (
                nt(normed_t, gq_t[g]),
                nn(normed_t, gk_ref[g]),
                nn(normed_t, gv_ref[g]),
                nn(context_0, grads_ref[g]),
            )
        )
    totals = [first + second for first, second in zip(*parts)]
    split_by_core(core_ref, totals, keep_ref, send_ref)


def intra_backward(core, grads, *rest):
    return kernel_call(
        intra_backward_kernel, "intra_backward", 4, [SMEM, VMEM] + [HBM] * 3, [VMEM] * 6,
        (
            f32(2, D, D), bf16(2, D, D), bf16(2, K, D), bf16(2, D, K), bf16(2, K, D), bf16(2, K, D),
        ),
        [vbf(HANDED_ROWS, 128), pltpu.VMEM((4 * HEADS, K), F32), vbf(D, D), dma(3)],
        BACKWARD_LIMIT,
    )(core, grads, *rest)


def intra_tail_kernel(
    grads_any, gq_t_any, gk_any, gv_any, f_any, n_any, gain_any, wq_any, wk_any, wv_any,
    first_ref, second_ref, carry_ref,
    grads_ref, gq_t_ref, gk_ref, gv_ref, rows_ref, gain_ref, w_ref, sems, own_sems,
):
    copies = begin_layer(sems, f_any, n_any, gain_any, wq_any, wk_any, wv_any, rows_ref, gain_ref, w_ref)
    copies += begin(
        own_sems,
        (grads_any, grads_ref), (gq_t_any, gq_t_ref), (gk_any, gk_ref), (gv_any, gv_ref),
    )
    settle(copies)
    unit, inverse = standardize(rows_ref[...].astype(F32))
    halves = []
    for g in range(2):
        at = slice(g * HOP, g * HOP + K)
        grad_normed = (
            nt(gq_t_ref[g].T, w_ref[0]) + nt(gk_ref[g], w_ref[1]) + nt(gv_ref[g], w_ref[2])
        )
        pulled = norm_pullback(grad_normed, unit[at], inverse[at], gain_ref[0:1, :])
        result = (grads_ref[g].astype(F32) + pulled).astype(BF)
        halves.append((result[:HOP], result[HOP:]))
    first_ref[...] = halves[0][0]
    second_ref[...] = (halves[1][0].astype(F32) + halves[0][1].astype(F32)).astype(BF)
    carry_ref[...] = halves[1][1]


def intra_tail(*operands):
    return kernel_call(
        intra_tail_kernel, "intra_tail", 2, [HBM] * 10, [VMEM] * 3,
        (bf16(HOP, D), bf16(HOP, D), bf16(HOP, D)),
        [vbf(2, K, D), vbf(2, D, K), vbf(2, K, D), vbf(2, K, D)]
        + layer_scratch()
        + [dma(6), dma(4)],
    )(*operands)


def finish_kernel(
    core_ref, mine_ref, other_ref, first_ref, second_ref, carried_ref, gain_ref, wq_ref, wk_ref, wv_ref,
    frames_ref, dq_ref, dk_ref, dv_ref, do_ref, dg_ref,
):
    frames_ref[:HOP] = (first_ref[...].astype(F32) + carried_ref[...].astype(F32)).astype(BF)
    frames_ref[HOP:] = second_ref[...]
    low_core = core_ref[0] == 0
    for layer in range(2):
        mine = mine_ref[:, layer].reshape(2, D, D).astype(F32)
        other = other_ref[:, layer].reshape(2, D, D).astype(F32)
        dq = jnp.where(low_core, mine[0], other[0])
        dk = jnp.where(low_core, mine[1], other[1])
        dv = jnp.where(low_core, other[0], mine[0])
        dq_ref[layer] = dq
        dk_ref[layer] = dk
        dv_ref[layer] = dv
        do_ref[layer] = jnp.where(low_core, other[1], mine[1])
        through = (
            dq * wq_ref[layer].astype(F32)
            + dk * wk_ref[layer].astype(F32)
            + dv * wv_ref[layer].astype(F32)
        )
        column = jnp.sum(through.T, axis=0, keepdims=True)
        dg_ref[layer : layer + 1, :] = column / gain_ref[layer : layer + 1, :]


def finish(core, *operands):
    full = f32(2, D, D)
    return kernel_call(
        finish_kernel, "finish", 2, [SMEM] + [VMEM] * 9, [VMEM] * 6,
        (bf16(K, D), full, full, full, full, f32(2, D)), [],
    )(core, *operands)


def shifted(shard, by):
    length = lax.axis_size(TM)
    pairs = [(i, i + by) for i in range(length) if 0 <= i + by < length]
    return lax.ppermute(shard, TM, pairs)


def exchanged(shard, axes):
    return lax.all_to_all(shard, axes, split_axis=0, concat_axis=0, tiled=True)


def swapped(shard):
    return lax.ppermute(shard, "core", [(0, 1), (1, 0)])


def copies(piece, count):
    return jnp.broadcast_to(piece[None], (count,) + piece.shape)


def summed(pieces):
    return jnp.sum(pieces.astype(F32), axis=0).astype(BF)


def core_sum(keep, send):
    return (keep + swapped(send).astype(F32)).astype(BF).reshape(16, 32, D)


def shards(frames, frames_grad, wq, wk, wv, wo, gains):
    frames = frames[0]
    core = lax.axis_index("core").astype(jnp.int32).reshape(1)
    following = shifted(frames, -1)
    front = intra_first(frames, gains, wq, wk, wv, wo)
    packed = intra_second(following, frames, frames_grad[0], *front, gains, wq, wk, wv, wo)
    across = exchanged(packed.reshape(64, 24, 128), TM).reshape(64 * 24, 128)
    grad_middle, *operands = inter(across, gains, wq, wk, wv, wo)
    grad_local = exchanged(grad_middle.reshape(64, 8, D), TM).reshape(512, D)
    inter_half = core_sum(*inter_weights(core, *operands))
    grad_local, inter_half = lax.optimization_barrier((grad_local, inter_half))
    prepared = intra_prepare(frames, following, gains, wq, wk, wv)
    keep, send, *rest = intra_backward(core, grad_local, *prepared, wo)
    half = jnp.concatenate([core_sum(keep, send), inter_half], axis=1)
    first, second, carry = intra_tail(*rest, frames, following, gains, wq, wk, wv)
    pieces = exchanged(half, PLANE)
    pieces, first, second, carry = lax.optimization_barrier((pieces, first, second, carry))
    carried = shifted(carry, 1)
    piece = summed(pieces)
    pieces = exchanged(copies(piece, 8), "z")
    pieces, carried = lax.optimization_barrier((pieces, carried))
    piece = summed(pieces)
    whole = exchanged(copies(piece, 16), PLANE).reshape(16, 2, 32, D)
    other = swapped(whole)
    grad_frames, *weights = finish(
        core, whole, other, first, second, carried, gains, wq, wk, wv
    )
    return (grad_frames[None], *weights)


def solution(mesh):
    split = Mesh(mesh.devices.reshape(2, 2, 2, 4, 8), AXES)
    placed = (P(DP, TM, None), P(DP, TM, None), P(), P(), P(), P(), P())
    return jax.shard_map(
        shards,
        mesh=split,
        in_specs=placed,
        out_specs=(P(DP, TM, None), P(), P(), P(), P(), P()),
        check_vma=False,
    )
```

```python
import math

import jax
import jax.numpy as jnp
from jax import lax
from jax.experimental import pallas as pl
from jax.experimental.pallas import tpu as pltpu
from jax.sharding import Mesh, PartitionSpec as P

HEADS = 8
HEAD = 32
D = 256
K = 256
HOP = 128
SEGMENTS = 128
EPSILON = 1e-05
SCALE = HEAD ** (-0.5)
LOG2E = math.log2(math.e)
BF = jnp.bfloat16
F32 = jnp.float32
VMEM_LIMIT = 16 * 1024 * 1024
FIRST_LIMIT = 54800 * 1024
SECOND_LIMIT = 54300 * 1024
PREPARE_LIMIT = 56 * 1024 * 1024
BACKWARD_LIMIT = 52850 * 1024

AXES = ("yh", "core", "yl", "x", "z")
DP = ("yh", "core")
TM = ("yl", "x", "z")
PLANE = ("yh", "yl", "x")


def dot(left, right, left_dim, right_dim):
    return lax.dot_general(
        left, right, (((left_dim,), (right_dim,)), ((), ())), preferred_element_type=F32
    )


def nn(left, right):
    return dot(left, right, 1, 0)


def nt(left, right):
    return dot(left, right, 1, 1)


def tn(left, right):
    return dot(left, right, 0, 0)


def standardize(rows):
    average = jnp.mean(rows, axis=-1, keepdims=True)
    centered = rows - average
    variance = jnp.mean(centered * centered, axis=-1, keepdims=True)
    inverse = lax.rsqrt(variance + EPSILON)
    return centered * inverse, inverse


def norm_pullback(grad_normed, unit, inverse, gain):
    grad_unit = grad_normed * gain
    first = jnp.mean(grad_unit, axis=-1, keepdims=True)
    second = jnp.mean(grad_unit * unit, axis=-1, keepdims=True)
    return inverse * (grad_unit - first - unit * second)


def head_masks():
    lane = lax.broadcasted_iota(jnp.int32, (1, 128), 1)
    return [jnp.where(lane // HEAD == i, 1.0, 0.0).astype(BF) for i in range(4)]


def row_masks():
    row = lax.broadcasted_iota(jnp.int32, (128, 1), 0)
    return [jnp.where(row // HEAD == i, 1.0, 0.0).astype(BF) for i in range(4)]


def select_rows(out_rows, in_rows, source):
    out = lax.broadcasted_iota(jnp.int32, (out_rows, in_rows), 0)
    col = lax.broadcasted_iota(jnp.int32, (out_rows, in_rows), 1)
    return jnp.where(source(out) == col, 1.0, 0.0).astype(BF)


def softmax_keys(scores):
    highest = jnp.max(scores, axis=0, keepdims=True)
    powers = jnp.exp2((scores - highest) * (SCALE * LOG2E))
    return powers * (1.0 / jnp.sum(powers, axis=0, keepdims=True))


def owner_target(out):
    return ((out % 64) // 2) * 8 + (out // 64) * 2 + out % 2


def segment_target(out):
    return (out % 4) * 64 + out // 4


def packed_source(out):
    device, row = out // 24, out % 24
    part = row % 8
    middle = (row // 8) * 128 + (part // 2) * 32 + device * 2 + part % 2
    rest = row - 16
    grads = 256 + (rest // 4) * 64 + ((rest % 4) // 2) * 32 + device * 2 + rest % 2
    return jnp.where(row < 16, middle, grads)


def unpacked_source(out):
    column, place = out // 128, out % 128
    segment = place % 32
    middle = (segment // 2) * 24 + column * 8 + (segment % 2) * 4 + place // 32
    rest = out - 256
    column, place = rest // 64, rest % 64
    segment = place % 32
    grads = (segment // 2) * 24 + 16 + column * 4 + (segment % 2) * 2 + place // 32
    return jnp.where(out < 256, middle, grads)


def staged(count, *stages):
    held = [{} for _ in stages]
    for t in range(count + len(stages) - 1):
        for i, stage in enumerate(stages):
            step = t - i
            if 0 <= step < count:
                held[i][step] = stage(step, *([held[i - 1].pop(step)] if i else []))


def attend(keys, queries_t, values_t, ctx_ref):
    masks = head_masks()

    def scores_of(h):
        block = slice((h // 4) * 128, (h // 4) * 128 + 128)
        return nn(keys[:, block] * masks[h % 4], queries_t[block, :])

    def weigh(h, scores):
        return softmax_keys(scores).astype(BF)

    def collect(h, low):
        feats = slice(h * HEAD, h * HEAD + HEAD)
        ctx_ref[feats, :] = nn(values_t[feats, :], low).astype(BF)

    staged(HEADS, scores_of, weigh, collect)


VMEM = pl.BlockSpec(memory_space=pltpu.VMEM)
SMEM = pl.BlockSpec(memory_space=pltpu.SMEM)
HBM = pl.BlockSpec(memory_space=pltpu.HBM)


def begin(sems, *pairs):
    copies = [pltpu.make_async_copy(src, dst, sems.at[i]) for i, (src, dst) in enumerate(pairs)]
    for copy in copies:
        copy.start()
    return copies


def settle(copies):
    for copy in copies:
        copy.wait()


def bf16(*shape):
    return jax.ShapeDtypeStruct(shape, BF)


def f32(*shape):
    return jax.ShapeDtypeStruct(shape, F32)


def kernel_call(kernel, name, micros, in_specs, out_specs, out_shape, scratch, limit=VMEM_LIMIT):
    return pl.pallas_call(
        kernel,
        in_specs=in_specs,
        out_specs=out_specs,
        out_shape=out_shape,
        scratch_shapes=scratch,
        compiler_params=pltpu.CompilerParams(vmem_limit_bytes=limit),
        cost_estimate=pl.CostEstimate(
            flops=int(micros * 400e6), bytes_accessed=1 << 20, transcendentals=0
        ),
        name=name,
    )


def dma(count):
    return pltpu.SemaphoreType.DMA((count,))


def vbf(*shape):
    return pltpu.VMEM(shape, BF)


def intra_first_kernel(
    f_any, gain_any, wq_any, wk_any, wv_any, wo_any,
    mid_ref, keys_ref, queries_ref, values_ref,
    w_ref, gain_ref, f_ref, ctx_ref, sems,
):
    copies = begin(
        sems,
        (f_any, f_ref),
        (gain_any, gain_ref),
        (wk_any.at[0], w_ref.at[1]),
        (wq_any.at[0], w_ref.at[0]),
        (wv_any.at[0], w_ref.at[2]),
        (wo_any.at[0], w_ref.at[3]),
    )
    copies[0].wait()
    rows = f_ref[...].astype(F32)
    unit, _ = standardize(rows)
    copies[1].wait()
    normed = (unit * gain_ref[0:1, :]).astype(BF)
    settle(copies[2:5])
    keys = nn(normed, w_ref[1]).astype(BF)
    queries_t = nt(w_ref[0].T, normed).astype(BF)
    values_t = nt(w_ref[2].T, normed).astype(BF)
    attend(keys, queries_t, values_t, ctx_ref)
    copies[5].wait()
    mid_ref[...] = (rows + tn(ctx_ref[...], w_ref[3])).astype(BF)
    keys_ref[...] = keys[HOP:]
    queries_ref[...] = queries_t[:, HOP:]
    values_ref[...] = values_t[:, HOP:]


def intra_second_kernel(
    n_ref, mid_in_ref, keys_ref, queries_ref, values_ref,
    f_any, grad_any, gain_any, wq_any, wk_any, wv_any, wo_any, packed_ref,
    f_ref, grad_ref, gain_ref, w_ref, ctx_ref, sems,
):
    copies = begin(
        sems,
        (gain_any, gain_ref),
        (wk_any.at[0], w_ref.at[1]),
        (wq_any.at[0], w_ref.at[0]),
        (wv_any.at[0], w_ref.at[2]),
        (wo_any.at[0], w_ref.at[3]),
        (f_any.at[pl.ds(HOP, HOP)], f_ref),
        (grad_any, grad_ref),
    )
    rows = n_ref[:HOP].astype(F32)
    unit, _ = standardize(rows)
    settle(copies[:4])
    normed = (unit * gain_ref[0:1, :]).astype(BF)
    keys = jnp.concatenate([keys_ref[...], nn(normed, w_ref[1]).astype(BF)], axis=0)
    queries_t = jnp.concatenate(
        [queries_ref[...], nt(w_ref[0].T, normed).astype(BF)], axis=1
    )
    values_t = jnp.concatenate([values_ref[...], nt(w_ref[2].T, normed).astype(BF)], axis=1)
    attend(keys, queries_t, values_t, ctx_ref)
    settle(copies[4:])
    rows = jnp.concatenate([f_ref[...].astype(F32), rows], axis=0)
    mids = (mid_in_ref[...], (rows + tn(ctx_ref[...], w_ref[3])).astype(BF))
    grads = grad_ref[...]
    pick = select_rows(384, 384, packed_source)
    for t in range(4):
        middle = jnp.concatenate(
            [mids[g][h * HOP + 32 * t : h * HOP + 32 * t + 32] for g in range(2) for h in range(2)],
            axis=0,
        )
        cotangent = jnp.concatenate(
            [grads[h * HOP + 32 * t : h * HOP + 32 * t + 32] for h in range(2)], axis=0
        )
        part = jnp.concatenate(
            [middle[:, :128], middle[:, 128:], cotangent[:, :128], cotangent[:, 128:]], axis=0
        )
        packed_ref[384 * t : 384 * t + 384, :] = nn(pick, part).astype(BF)


def intra_first(frames, gains, wq, wk, wv, wo):
    return kernel_call(
        intra_first_kernel, "intra_first", 3, [HBM] * 6, [VMEM] * 4,
        (bf16(K, D), bf16(HOP, D), bf16(D, HOP), bf16(D, HOP)),
        [vbf(4, D, D), pltpu.VMEM((2, D), F32), vbf(K, D), vbf(D, K), dma(6)],
        FIRST_LIMIT,
    )(frames, gains, wq, wk, wv, wo)


def intra_second(following, *rest):
    return kernel_call(
        intra_second_kernel, "intra_second", 3, [VMEM] * 5 + [HBM] * 7, VMEM,
        bf16(64 * 24, 128),
        [
            vbf(HOP, D), vbf(K, D), pltpu.VMEM((2, D), F32), vbf(4, D, D), vbf(D, K), dma(7),
        ],
        SECOND_LIMIT,
    )(following, *rest)


def inter_kernel(
    packed_ref, gain_ref, wq_ref, wk_ref, wv_ref, wo_ref,
    out_ref, normed_t_ref, grads_ref, ctx_t, gq_t, gk_ref, gv_ref,
):
    gain = gain_ref[1:2, :]
    pick = select_rows(384, 384, unpacked_source)
    tiles = [nn(pick, packed_ref[384 * t : 384 * t + 384, :]) for t in range(4)]
    rows = jnp.concatenate(
        [
            jnp.concatenate(
                [tiles[t][c * 128 + 32 * p : c * 128 + 32 * p + 32] for c in range(2)], axis=1
            )
            for p in range(4)
            for t in range(4)
        ],
        axis=0,
    )
    hops = [
        jnp.concatenate(
            [
                jnp.concatenate(
                    [tiles[t][256 + c * 64 + 32 * r : 256 + c * 64 + 32 * r + 32] for c in range(2)],
                    axis=1,
                )
                for t in range(4)
            ],
            axis=0,
        )
        for r in range(2)
    ]
    last = jnp.zeros((1, D), F32)
    late = [jnp.concatenate([hop[1:], last], axis=0) for hop in hops]
    grads = jnp.concatenate(hops + late, axis=0).astype(BF)
    grads_ref[...] = grads
    unit, inverse = standardize(rows)
    normed = (unit * gain).astype(BF)
    normed_t_ref[...] = normed.T
    wq, wk, wv, wo = wq_ref[1], wk_ref[1], wv_ref[1], wo_ref[1]
    queries = nn(normed, wq).astype(BF)
    keys = nn(normed, wk).astype(BF)
    values = nn(normed, wv).astype(BF)
    grad_context = nt(grads, wo).astype(BF)
    queries_t = queries.T
    keys_t = keys.T
    values_t = values.T
    grad_context_t = grad_context.T
    masks = head_masks()
    downs = row_masks()

    def place(step):
        p, b = step // 2, step % 2
        return slice(128 * p, 128 * p + 128), slice(128 * b, 128 * b + 128)

    def columns(rows_t):
        return jnp.concatenate([rows_t * down for down in downs], axis=1)

    def stacked(rows):
        return jnp.concatenate([rows * mask for mask in masks], axis=0)

    def products(step):
        at, block = place(step)
        scores = nn(keys[at, block], columns(queries_t[block, at]))
        grad_probs = nn(values[at, block], columns(grad_context_t[block, at]))
        return scores, grad_probs

    def weigh(step, held):
        scores, grad_probs = held
        probs = softmax_keys(scores)
        inner = jnp.sum(grad_probs * probs, axis=0, keepdims=True)
        return probs.astype(BF), (probs * (grad_probs - inner) * SCALE).astype(BF)

    def collect(step, held):
        low, grad_scores = held
        at, block = place(step)
        gv_ref[at, block] = nn(low, stacked(grad_context[at, block])).astype(BF)
        gk_ref[at, block] = nn(grad_scores, stacked(queries[at, block])).astype(BF)
        for i in range(4):
            feats = slice(block.start + HEAD * i, block.start + HEAD * i + HEAD)
            cols = slice(128 * i, 128 * i + 128)
            ctx_t[feats, at] = nn(values_t[feats, at], low[:, cols]).astype(BF)
            gq_t[feats, at] = nn(keys_t[feats, at], grad_scores[:, cols]).astype(BF)

    staged(8, products, weigh, collect)
    gqt, gk, gv = gq_t[...], gk_ref[...], gv_ref[...]
    grad_normed = nt(gqt.T, wq) + nt(gk, wk) + nt(gv, wv)
    result = (grads.astype(F32) + norm_pullback(grad_normed, unit, inverse, gain)).astype(BF)
    back = select_rows(256, 256, segment_target)
    for t in range(2):
        part = jnp.concatenate(
            [result[128 * p + 64 * t : 128 * p + 64 * t + 64] for p in range(4)], axis=0
        )
        out_ref[256 * t : 256 * t + 256, :] = nn(back, part).astype(BF)


def inter(packed, gains, wq, wk, wv, wo):
    return kernel_call(
        inter_kernel, "inter", 5, [VMEM] * 6, [VMEM] * 7,
        (
            bf16(512, D), bf16(D, 512), bf16(512, D), bf16(D, 512), bf16(D, 512), bf16(512, D),
            bf16(512, D),
        ),
        [],
    )(packed, gains, wq, wk, wv, wo)


def split_by_core(core_ref, weights, keep_ref, send_ref):
    low_core = core_ref[0] == 0
    for i in range(2):
        keep_ref[i] = jnp.where(low_core, weights[i], weights[2 + i])
        send_ref[i] = jnp.where(low_core, weights[2 + i], weights[i]).astype(BF)


def inter_weights_kernel(
    core_ref, normed_t_ref, grads_ref, ctx_t_ref, gq_t_ref, gk_ref, gv_ref, keep_ref, send_ref
):
    normed_t = normed_t_ref[...]
    weights = (
        nt(normed_t, gq_t_ref[...]),
        nn(normed_t, gk_ref[...]),
        nn(normed_t, gv_ref[...]),
        nn(ctx_t_ref[...], grads_ref[...]),
    )
    split_by_core(core_ref, weights, keep_ref, send_ref)


def inter_weights(core, *operands):
    return kernel_call(
        inter_weights_kernel, "inter_weights", 1, [SMEM] + [VMEM] * 6, [VMEM] * 2,
        (f32(2, D, D), bf16(2, D, D)), [],
    )(core, *operands)


KEYS, QUERIES_T, VALUES, STATS = 0, 768, 1536, 2304
QUERIES, KEYS_T, NORMED_T, CONTEXT = 2496, 3264, 4032, 4800
HANDED_ROWS = 5824


def put_stats(handed_ref, stats):
    for i in range(3):
        part = stats.astype(BF)
        stats = stats - part.astype(F32)
        put_blocks(handed_ref, STATS + 64 * i, part)


def stats_of(handed_ref):
    parts = [
        jnp.concatenate(
            [
                handed_ref[STATS + 64 * i + 32 * j : STATS + 64 * i + 32 * j + 32, :].astype(F32)
                for j in range(2)
            ],
            axis=1,
        )
        for i in range(3)
    ]
    return parts[0] + parts[1] + parts[2]


def put_blocks(handed_ref, start, array):
    for i in range(array.shape[1] // 128):
        at = start + i * array.shape[0]
        handed_ref[at : at + array.shape[0], :] = array[:, 128 * i : 128 * i + 128]


def features_of(handed_ref, start, rows, at):
    return jnp.concatenate(
        [
            handed_ref[start + 256 * i + rows.start : start + 256 * i + rows.stop, :]
            for i in range(at.start // 128, at.stop // 128)
        ],
        axis=1,
    )


def tokens_of(handed_ref, start, at, b):
    return handed_ref[start + 384 * b + at.start : start + 384 * b + at.stop, :]


def begin_layer(sems, f_any, n_any, gain_any, wq_any, wk_any, wv_any, rows_ref, gain_ref, w_ref):
    return begin(
        sems,
        (f_any, rows_ref.at[pl.ds(0, K)]),
        (n_any.at[pl.ds(0, HOP)], rows_ref.at[pl.ds(K, HOP)]),
        (gain_any, gain_ref),
        (wq_any.at[0], w_ref.at[0]),
        (wk_any.at[0], w_ref.at[1]),
        (wv_any.at[0], w_ref.at[2]),
    )


def layer_scratch():
    return [vbf(3 * HOP, D), pltpu.VMEM((2, D), F32), vbf(3, D, D)]


def intra_prepare_kernel(
    f_any, n_any, gain_any, wq_any, wk_any, wv_any, handed_ref,
    stats_ref, ctx_ref, rows_ref, gain_ref, w_ref, sems,
):
    settle(begin_layer(sems, f_any, n_any, gain_any, wq_any, wk_any, wv_any, rows_ref, gain_ref, w_ref))
    unit, _ = standardize(rows_ref[...].astype(F32))
    normed = (unit * gain_ref[0:1, :]).astype(BF)
    queries = nn(normed, w_ref[0]).astype(BF)
    keys = nn(normed, w_ref[1]).astype(BF)
    values = nn(normed, w_ref[2]).astype(BF)
    queries_t = queries.T
    values_t = values.T
    put_blocks(handed_ref, NORMED_T, normed.T)
    put_blocks(handed_ref, QUERIES, queries)
    put_blocks(handed_ref, QUERIES_T, queries_t)
    put_blocks(handed_ref, KEYS, keys)
    put_blocks(handed_ref, KEYS_T, keys.T)
    put_blocks(handed_ref, VALUES, values)
    masks = head_masks()

    def scores_of(step):
        g, h = step // HEADS, step % HEADS
        at = slice(g * HOP, g * HOP + K)
        block = slice((h // 4) * 128, (h // 4) * 128 + 128)
        return nn(keys[at, block] * masks[h % 4], queries_t[block, at])

    def weigh(step, scores):
        highest = jnp.max(scores, axis=0, keepdims=True)
        powers = jnp.exp2((scores - highest) * (SCALE * LOG2E))
        inverse = 1.0 / jnp.sum(powers, axis=0, keepdims=True)
        stats_ref[2 * step : 2 * step + 1, :] = highest
        stats_ref[2 * step + 1 : 2 * step + 2, :] = inverse
        return (powers * inverse).astype(BF)

    def collect(step, low):
        g, h = step // HEADS, step % HEADS
        feats = slice(h * HEAD, h * HEAD + HEAD)
        ctx_ref[g, feats, :] = nn(values_t[feats, g * HOP : g * HOP + K], low).astype(BF)

    staged(2 * HEADS, scores_of, weigh, collect)
    for g in range(2):
        put_blocks(handed_ref, CONTEXT + 512 * g, ctx_ref[g])
    put_stats(handed_ref, stats_ref[...])


def intra_prepare(frames, following, gains, wq, wk, wv):
    return kernel_call(
        intra_prepare_kernel, "intra_prepare", 3, [HBM] * 6, VMEM, bf16(HANDED_ROWS, 128),
        [pltpu.VMEM((4 * HEADS, K), F32), vbf(2, D, K)] + layer_scratch() + [dma(6)],
        PREPARE_LIMIT,
    )(frames, following, gains, wq, wk, wv)


def intra_backward_kernel(
    core_ref, m_ref, handed_any, wo_any,
    keep_ref, send_ref, grads_ref, gq_t, gk_ref, gv_ref,
    handed_ref, stats_ref, wo_ref, sems,
):
    cuts = (KEYS, QUERIES, NORMED_T, HANDED_ROWS)
    spans = [pl.ds(start, end - start) for start, end in zip(cuts, cuts[1:])]
    copies = begin(
        sems,
        (wo_any.at[0], wo_ref),
        *[(handed_any.at[span], handed_ref.at[span]) for span in spans],
    )
    pick = select_rows(256, 256, owner_target)
    tiles = [nn(pick, m_ref[256 * t : 256 * t + 256, :]).astype(BF) for t in range(2)]
    masks = head_masks()
    context, context_t = [], []
    for g in range(2):
        grads_ref[g] = jnp.concatenate(
            [tiles[t][128 * g + 64 * h : 128 * g + 64 * h + 64] for h in range(2) for t in range(2)],
            axis=0,
        )
        if g == 0:
            copies[0].wait()
        context.append(nt(grads_ref[g], wo_ref[...]).astype(BF))
        context_t.append(context[g].T)

    copies[1].wait()
    stats_ref[...] = stats_of(handed_ref)

    def place(step):
        g, h = step // HEADS, step % HEADS
        return g, slice(g * HOP, g * HOP + K), h // 4, h % 4

    def products(step):
        g, at, b, i = place(step)
        block = slice(128 * b, 128 * b + 128)
        keys = tokens_of(handed_ref, KEYS, at, b) * masks[i]
        scores = nn(keys, features_of(handed_ref, QUERIES_T, block, at))
        values = tokens_of(handed_ref, VALUES, at, b) * masks[i]
        return scores, nn(values, context_t[g][block, :])

    def weigh(step, held):
        scores, grad_probs = held
        powers = jnp.exp2((scores - stats_ref[2 * step : 2 * step + 1, :]) * (SCALE * LOG2E))
        probs = powers * stats_ref[2 * step + 1 : 2 * step + 2, :]
        inner = jnp.sum(grad_probs * probs, axis=0, keepdims=True)
        return probs.astype(BF), (probs * (grad_probs - inner) * SCALE).astype(BF)

    sums = {}

    def collect(step, held):
        if step == 0:
            copies[2].wait()
        low, grad_scores = held
        g, at, b, i = place(step)
        block = slice(128 * b, 128 * b + 128)
        feats = slice(128 * b + HEAD * i, 128 * b + HEAD * i + HEAD)
        gv = nn(low, context[g][:, block] * masks[i])
        gk = nn(grad_scores, tokens_of(handed_ref, QUERIES, at, b) * masks[i])
        keys_t = features_of(handed_ref, KEYS_T, feats, at)
        gq_t[g, feats, :] = nn(keys_t, grad_scores).astype(BF)
        sums["v"] = gv if i == 0 else sums["v"] + gv
        sums["k"] = gk if i == 0 else sums["k"] + gk
        if i == 3:
            gv_ref[g, :, block] = sums["v"].astype(BF)
            gk_ref[g, :, block] = sums["k"].astype(BF)

    staged(2 * HEADS, products, weigh, collect)
    copies[3].wait()
    parts = []
    for g in range(2):
        normed_t = features_of(
            handed_ref, NORMED_T, slice(0, D), slice(g * HOP, g * HOP + K)
        )
        context_0 = jnp.concatenate(
            [handed_ref[pl.ds(CONTEXT + 512 * g + 256 * i, 256), :] for i in range(2)], axis=1
        )
        parts.append(
            (
                nt(normed_t, gq_t[g]),
                nn(normed_t, gk_ref[g]),
                nn(normed_t, gv_ref[g]),
                nn(context_0, grads_ref[g]),
            )
        )
    totals = [first + second for first, second in zip(*parts)]
    split_by_core(core_ref, totals, keep_ref, send_ref)


def intra_backward(core, grads, *rest):
    return kernel_call(
        intra_backward_kernel, "intra_backward", 4, [SMEM, VMEM] + [HBM] * 2, [VMEM] * 6,
        (
            f32(2, D, D), bf16(2, D, D), bf16(2, K, D), bf16(2, D, K), bf16(2, K, D), bf16(2, K, D),
        ),
        [vbf(HANDED_ROWS, 128), pltpu.VMEM((4 * HEADS, K), F32), vbf(D, D), dma(4)],
        BACKWARD_LIMIT,
    )(core, grads, *rest)


def intra_tail_kernel(
    grads_any, gq_t_any, gk_any, gv_any, f_any, n_any, gain_any, wq_any, wk_any, wv_any,
    first_ref, second_ref, carry_ref,
    grads_ref, gq_t_ref, gk_ref, gv_ref, rows_ref, gain_ref, w_ref, sems, own_sems,
):
    copies = begin_layer(sems, f_any, n_any, gain_any, wq_any, wk_any, wv_any, rows_ref, gain_ref, w_ref)
    copies += begin(
        own_sems,
        (grads_any, grads_ref), (gq_t_any, gq_t_ref), (gk_any, gk_ref), (gv_any, gv_ref),
    )
    settle(copies)
    unit, inverse = standardize(rows_ref[...].astype(F32))
    halves = []
    for g in range(2):
        at = slice(g * HOP, g * HOP + K)
        grad_normed = (
            nt(gq_t_ref[g].T, w_ref[0]) + nt(gk_ref[g], w_ref[1]) + nt(gv_ref[g], w_ref[2])
        )
        pulled = norm_pullback(grad_normed, unit[at], inverse[at], gain_ref[0:1, :])
        result = (grads_ref[g].astype(F32) + pulled).astype(BF)
        halves.append((result[:HOP], result[HOP:]))
    first_ref[...] = halves[0][0]
    second_ref[...] = (halves[1][0].astype(F32) + halves[0][1].astype(F32)).astype(BF)
    carry_ref[...] = halves[1][1]


def intra_tail(*operands):
    return kernel_call(
        intra_tail_kernel, "intra_tail", 2, [HBM] * 10, [VMEM] * 3,
        (bf16(HOP, D), bf16(HOP, D), bf16(HOP, D)),
        [vbf(2, K, D), vbf(2, D, K), vbf(2, K, D), vbf(2, K, D)]
        + layer_scratch()
        + [dma(6), dma(4)],
    )(*operands)


def finish_kernel(
    core_ref, mine_ref, other_ref, first_ref, second_ref, carried_ref, gain_ref, wq_ref, wk_ref, wv_ref,
    frames_ref, dq_ref, dk_ref, dv_ref, do_ref, dg_ref,
):
    frames_ref[:HOP] = (first_ref[...].astype(F32) + carried_ref[...].astype(F32)).astype(BF)
    frames_ref[HOP:] = second_ref[...]
    low_core = core_ref[0] == 0
    for layer in range(2):
        mine = mine_ref[:, layer].reshape(2, D, D).astype(F32)
        other = other_ref[:, layer].reshape(2, D, D).astype(F32)
        dq = jnp.where(low_core, mine[0], other[0])
        dk = jnp.where(low_core, mine[1], other[1])
        dv = jnp.where(low_core, other[0], mine[0])
        dq_ref[layer] = dq
        dk_ref[layer] = dk
        dv_ref[layer] = dv
        do_ref[layer] = jnp.where(low_core, other[1], mine[1])
        through = (
            dq * wq_ref[layer].astype(F32)
            + dk * wk_ref[layer].astype(F32)
            + dv * wv_ref[layer].astype(F32)
        )
        column = jnp.sum(through.T, axis=0, keepdims=True)
        dg_ref[layer : layer + 1, :] = column / gain_ref[layer : layer + 1, :]


def finish(core, *operands):
    full = f32(2, D, D)
    return kernel_call(
        finish_kernel, "finish", 2, [SMEM] + [VMEM] * 9, [VMEM] * 6,
        (bf16(K, D), full, full, full, full, f32(2, D)), [],
    )(core, *operands)


def shifted(shard, by):
    length = lax.axis_size(TM)
    pairs = [(i, i + by) for i in range(length) if 0 <= i + by < length]
    return lax.ppermute(shard, TM, pairs)


def exchanged(shard, axes):
    return lax.all_to_all(shard, axes, split_axis=0, concat_axis=0, tiled=True)


def swapped(shard):
    return lax.ppermute(shard, "core", [(0, 1), (1, 0)])


def copies(piece, count):
    return jnp.broadcast_to(piece[None], (count,) + piece.shape)


def summed(pieces):
    return jnp.sum(pieces.astype(F32), axis=0).astype(BF)


def core_sum(keep, send):
    return (keep + swapped(send).astype(F32)).astype(BF).reshape(16, 32, D)


def shards(frames, frames_grad, wq, wk, wv, wo, gains):
    frames = frames[0]
    core = lax.axis_index("core").astype(jnp.int32).reshape(1)
    following = shifted(frames, -1)
    front = intra_first(frames, gains, wq, wk, wv, wo)
    packed = intra_second(
        following, *front, frames, frames_grad[0], gains, wq, wk, wv, wo
    )
    across = exchanged(packed.reshape(64, 24, 128), TM).reshape(64 * 24, 128)
    grad_middle, *operands = inter(across, gains, wq, wk, wv, wo)
    grad_local = exchanged(grad_middle.reshape(64, 8, D), TM).reshape(512, D)
    inter_half = core_sum(*inter_weights(core, *operands))
    grad_local, inter_half = lax.optimization_barrier((grad_local, inter_half))
    handed = intra_prepare(frames, following, gains, wq, wk, wv)
    keep, send, *rest = intra_backward(core, grad_local, handed, wo)
    half = jnp.concatenate([core_sum(keep, send), inter_half], axis=1)
    first, second, carry = intra_tail(*rest, frames, following, gains, wq, wk, wv)
    carried = shifted(carry, 1)
    sent = copies(summed(exchanged(half, PLANE)), 8)
    sent, carried = lax.optimization_barrier((sent, carried))
    piece = summed(exchanged(sent, "z"))
    whole = exchanged(copies(piece, 16), PLANE).reshape(16, 2, 32, D)
    other = swapped(whole)
    grad_frames, *weights = finish(
        core, whole, other, first, second, carried, gains, wq, wk, wv
    )
    return (grad_frames[None], *weights)


def solution(mesh):
    split = Mesh(mesh.devices.reshape(2, 2, 2, 4, 8), AXES)
    placed = (P(DP, TM, None), P(DP, TM, None), P(), P(), P(), P(), P())
    return jax.shard_map(
        shards,
        mesh=split,
        in_specs=placed,
        out_specs=(P(DP, TM, None), P(), P(), P(), P(), P()),
        check_vma=False,
    )
```

```python
import math

import jax
import jax.numpy as jnp
from jax import lax
from jax.experimental import pallas as pl
from jax.experimental.pallas import tpu as pltpu
from jax.sharding import Mesh, PartitionSpec as P

HEADS = 8
HEAD = 32
D = 256
K = 256
HOP = 128
SEGMENTS = 128
EPSILON = 1e-05
SCALE = HEAD ** (-0.5)
LOG2E = math.log2(math.e)
BF = jnp.bfloat16
F32 = jnp.float32
VMEM_LIMIT = 16 * 1024 * 1024
FIRST_LIMIT = 54800 * 1024
SECOND_LIMIT = 54300 * 1024
PREPARE_LIMIT = 56 * 1024 * 1024
BACKWARD_LIMIT = 52850 * 1024

AXES = ("yh", "core", "yl", "x", "za", "zb")
DP = ("yh", "core")
TM = ("yl", "x", "za", "zb")
PLANE = ("yh", "yl", "x", "zb")


def dot(left, right, left_dim, right_dim):
    return lax.dot_general(
        left, right, (((left_dim,), (right_dim,)), ((), ())), preferred_element_type=F32
    )


def nn(left, right):
    return dot(left, right, 1, 0)


def nt(left, right):
    return dot(left, right, 1, 1)


def tn(left, right):
    return dot(left, right, 0, 0)


def standardize(rows):
    average = jnp.mean(rows, axis=-1, keepdims=True)
    centered = rows - average
    variance = jnp.mean(centered * centered, axis=-1, keepdims=True)
    inverse = lax.rsqrt(variance + EPSILON)
    return centered * inverse, inverse


def norm_pullback(grad_normed, unit, inverse, gain):
    grad_unit = grad_normed * gain
    first = jnp.mean(grad_unit, axis=-1, keepdims=True)
    second = jnp.mean(grad_unit * unit, axis=-1, keepdims=True)
    return inverse * (grad_unit - first - unit * second)


def head_masks():
    lane = lax.broadcasted_iota(jnp.int32, (1, 128), 1)
    return [jnp.where(lane // HEAD == i, 1.0, 0.0).astype(BF) for i in range(4)]


def row_masks():
    row = lax.broadcasted_iota(jnp.int32, (128, 1), 0)
    return [jnp.where(row // HEAD == i, 1.0, 0.0).astype(BF) for i in range(4)]


def select_rows(out_rows, in_rows, source):
    out = lax.broadcasted_iota(jnp.int32, (out_rows, in_rows), 0)
    col = lax.broadcasted_iota(jnp.int32, (out_rows, in_rows), 1)
    return jnp.where(source(out) == col, 1.0, 0.0).astype(BF)


def softmax_keys(scores):
    highest = jnp.max(scores, axis=0, keepdims=True)
    powers = jnp.exp2((scores - highest) * (SCALE * LOG2E))
    return powers * (1.0 / jnp.sum(powers, axis=0, keepdims=True))


def owner_target(out):
    return ((out % 64) // 2) * 8 + (out // 64) * 2 + out % 2


def segment_target(out):
    return (out % 4) * 64 + out // 4


def packed_source(out):
    return ((out // 2) % 4) * 64 + (out // 8) * 2 + out % 2


def middle_source(out):
    return ((out % 64) // 2) * 8 + (out % 2) * 4 + out // 64


def cotangent_source(out):
    hop = out % 64
    return (hop // 2) * 8 + (out // 128) * 4 + (hop % 2) * 2 + (out // 64) % 2


def staged(count, *stages):
    held = [{} for _ in stages]
    for t in range(count + len(stages) - 1):
        for i, stage in enumerate(stages):
            step = t - i
            if 0 <= step < count:
                held[i][step] = stage(step, *([held[i - 1].pop(step)] if i else []))


def attend(keys, queries_t, values_t, ctx_ref):
    masks = head_masks()

    def scores_of(h):
        block = slice((h // 4) * 128, (h // 4) * 128 + 128)
        return nn(keys[:, block] * masks[h % 4], queries_t[block, :])

    def weigh(h, scores):
        return softmax_keys(scores).astype(BF)

    def collect(h, low):
        feats = slice(h * HEAD, h * HEAD + HEAD)
        ctx_ref[feats, :] = nn(values_t[feats, :], low).astype(BF)

    staged(HEADS, scores_of, weigh, collect)


VMEM = pl.BlockSpec(memory_space=pltpu.VMEM)
SMEM = pl.BlockSpec(memory_space=pltpu.SMEM)
HBM = pl.BlockSpec(memory_space=pltpu.HBM)


def begin(sems, *pairs):
    copies = [pltpu.make_async_copy(src, dst, sems.at[i]) for i, (src, dst) in enumerate(pairs)]
    for copy in copies:
        copy.start()
    return copies


def settle(copies):
    for copy in copies:
        copy.wait()


def bf16(*shape):
    return jax.ShapeDtypeStruct(shape, BF)


def f32(*shape):
    return jax.ShapeDtypeStruct(shape, F32)


def kernel_call(kernel, name, micros, in_specs, out_specs, out_shape, scratch, limit=VMEM_LIMIT):
    return pl.pallas_call(
        kernel,
        in_specs=in_specs,
        out_specs=out_specs,
        out_shape=out_shape,
        scratch_shapes=scratch,
        compiler_params=pltpu.CompilerParams(vmem_limit_bytes=limit),
        cost_estimate=pl.CostEstimate(
            flops=int(micros * 400e6), bytes_accessed=1 << 20, transcendentals=0
        ),
        name=name,
    )


def dma(count):
    return pltpu.SemaphoreType.DMA((count,))


def vbf(*shape):
    return pltpu.VMEM(shape, BF)


def intra_first_kernel(
    f_any, gain_any, wq_any, wk_any, wv_any, wo_any,
    mid_ref, keys_ref, queries_ref, values_ref,
    w_ref, gain_ref, f_ref, ctx_ref, sems,
):
    copies = begin(
        sems,
        (f_any, f_ref),
        (gain_any, gain_ref),
        (wk_any.at[0], w_ref.at[1]),
        (wq_any.at[0], w_ref.at[0]),
        (wv_any.at[0], w_ref.at[2]),
        (wo_any.at[0], w_ref.at[3]),
    )
    copies[0].wait()
    rows = f_ref[...].astype(F32)
    unit, _ = standardize(rows)
    copies[1].wait()
    normed = (unit * gain_ref[0:1, :]).astype(BF)
    settle(copies[2:5])
    keys = nn(normed, w_ref[1]).astype(BF)
    queries_t = nt(w_ref[0].T, normed).astype(BF)
    values_t = nt(w_ref[2].T, normed).astype(BF)
    attend(keys, queries_t, values_t, ctx_ref)
    copies[5].wait()
    mid_ref[...] = (rows + tn(ctx_ref[...], w_ref[3])).astype(BF)
    keys_ref[...] = keys[HOP:]
    queries_ref[...] = queries_t[:, HOP:]
    values_ref[...] = values_t[:, HOP:]


def intra_second_kernel(
    n_ref, mid_in_ref, keys_ref, queries_ref, values_ref,
    f_any, grad_any, gain_any, wq_any, wk_any, wv_any, wo_any, packed_ref,
    f_ref, grad_ref, gain_ref, w_ref, ctx_ref, sems,
):
    copies = begin(
        sems,
        (gain_any, gain_ref),
        (wk_any.at[0], w_ref.at[1]),
        (wq_any.at[0], w_ref.at[0]),
        (wv_any.at[0], w_ref.at[2]),
        (wo_any.at[0], w_ref.at[3]),
        (f_any.at[pl.ds(HOP, HOP)], f_ref),
        (grad_any, grad_ref),
    )
    rows = n_ref[:HOP].astype(F32)
    unit, _ = standardize(rows)
    settle(copies[:4])
    normed = (unit * gain_ref[0:1, :]).astype(BF)
    keys = jnp.concatenate([keys_ref[...], nn(normed, w_ref[1]).astype(BF)], axis=0)
    queries_t = jnp.concatenate(
        [queries_ref[...], nt(w_ref[0].T, normed).astype(BF)], axis=1
    )
    values_t = jnp.concatenate([values_ref[...], nt(w_ref[2].T, normed).astype(BF)], axis=1)
    attend(keys, queries_t, values_t, ctx_ref)
    settle(copies[4:])
    rows = jnp.concatenate([f_ref[...].astype(F32), rows], axis=0)
    mids = (mid_in_ref[...], (rows + tn(ctx_ref[...], w_ref[3])).astype(BF))
    grads = grad_ref[...]
    pick = select_rows(256, 256, packed_source)
    for t in range(2):
        parts = []
        for part in range(4):
            high, low = part // 2, part % 2
            at = slice(low * HOP + 64 * t, low * HOP + 64 * t + 64)
            parts.append(
                jnp.concatenate([mids[high][at], grads[at, 128 * high : 128 * high + 128]], axis=1)
            )
        rows = jnp.concatenate(parts, axis=0)
        packed_ref[256 * t : 256 * t + 256, :] = nn(pick, rows).astype(BF)


def intra_first(frames, gains, wq, wk, wv, wo):
    return kernel_call(
        intra_first_kernel, "intra_first", 3, [HBM] * 6, [VMEM] * 4,
        (bf16(K, D), bf16(HOP, D), bf16(D, HOP), bf16(D, HOP)),
        [vbf(4, D, D), pltpu.VMEM((2, D), F32), vbf(K, D), vbf(D, K), dma(6)],
        FIRST_LIMIT,
    )(frames, gains, wq, wk, wv, wo)


def intra_second(following, *rest):
    return kernel_call(
        intra_second_kernel, "intra_second", 3, [VMEM] * 5 + [HBM] * 7, VMEM,
        bf16(512, 384),
        [
            vbf(HOP, D), vbf(K, D), pltpu.VMEM((2, D), F32), vbf(4, D, D), vbf(D, K), dma(7),
        ],
        SECOND_LIMIT,
    )(following, *rest)


def inter_kernel(
    packed_ref, gain_ref, wq_ref, wk_ref, wv_ref, wo_ref,
    out_ref, normed_t_ref, grads_ref, ctx_t, gq_t, gk_ref, gv_ref,
):
    gain = gain_ref[1:2, :]
    pick = select_rows(256, 256, middle_source)
    tiles = [nn(pick, packed_ref[256 * t : 256 * t + 256, :D]) for t in range(2)]
    rows = jnp.concatenate(
        [tiles[t][64 * p : 64 * p + 64] for p in range(4) for t in range(2)], axis=0
    )
    pick = select_rows(256, 256, cotangent_source)
    tiles = [nn(pick, packed_ref[256 * t : 256 * t + 256, D:]) for t in range(2)]
    hops = [
        jnp.concatenate(
            [
                jnp.concatenate(
                    [tiles[t][128 * c + 64 * r : 128 * c + 64 * r + 64] for c in range(2)], axis=1
                )
                for t in range(2)
            ],
            axis=0,
        )
        for r in range(2)
    ]
    last = jnp.zeros((1, D), F32)
    late = [jnp.concatenate([hop[1:], last], axis=0) for hop in hops]
    grads = jnp.concatenate(hops + late, axis=0).astype(BF)
    grads_ref[...] = grads
    unit, inverse = standardize(rows)
    normed = (unit * gain).astype(BF)
    normed_t_ref[...] = normed.T
    wq, wk, wv, wo = wq_ref[1], wk_ref[1], wv_ref[1], wo_ref[1]
    queries = nn(normed, wq).astype(BF)
    keys = nn(normed, wk).astype(BF)
    values = nn(normed, wv).astype(BF)
    grad_context = nt(grads, wo).astype(BF)
    queries_t = queries.T
    keys_t = keys.T
    values_t = values.T
    grad_context_t = grad_context.T
    masks = head_masks()
    downs = row_masks()

    def place(step):
        p, b = step // 2, step % 2
        return slice(128 * p, 128 * p + 128), slice(128 * b, 128 * b + 128)

    def columns(rows_t):
        return jnp.concatenate([rows_t * down for down in downs], axis=1)

    def stacked(rows):
        return jnp.concatenate([rows * mask for mask in masks], axis=0)

    def products(step):
        at, block = place(step)
        scores = nn(keys[at, block], columns(queries_t[block, at]))
        grad_probs = nn(values[at, block], columns(grad_context_t[block, at]))
        return scores, grad_probs

    def weigh(step, held):
        scores, grad_probs = held
        probs = softmax_keys(scores)
        inner = jnp.sum(grad_probs * probs, axis=0, keepdims=True)
        return probs.astype(BF), (probs * (grad_probs - inner) * SCALE).astype(BF)

    def collect(step, held):
        low, grad_scores = held
        at, block = place(step)
        gv_ref[at, block] = nn(low, stacked(grad_context[at, block])).astype(BF)
        gk_ref[at, block] = nn(grad_scores, stacked(queries[at, block])).astype(BF)
        for i in range(4):
            feats = slice(block.start + HEAD * i, block.start + HEAD * i + HEAD)
            cols = slice(128 * i, 128 * i + 128)
            ctx_t[feats, at] = nn(values_t[feats, at], low[:, cols]).astype(BF)
            gq_t[feats, at] = nn(keys_t[feats, at], grad_scores[:, cols]).astype(BF)

    staged(8, products, weigh, collect)
    gqt, gk, gv = gq_t[...], gk_ref[...], gv_ref[...]
    grad_normed = nt(gqt.T, wq) + nt(gk, wk) + nt(gv, wv)
    result = (grads.astype(F32) + norm_pullback(grad_normed, unit, inverse, gain)).astype(BF)
    back = select_rows(256, 256, segment_target)
    for t in range(2):
        part = jnp.concatenate(
            [result[128 * p + 64 * t : 128 * p + 64 * t + 64] for p in range(4)], axis=0
        )
        out_ref[256 * t : 256 * t + 256, :] = nn(back, part).astype(BF)


def inter(packed, gains, wq, wk, wv, wo):
    return kernel_call(
        inter_kernel, "inter", 5, [VMEM] * 6, [VMEM] * 7,
        (
            bf16(512, D), bf16(D, 512), bf16(512, D), bf16(D, 512), bf16(D, 512), bf16(512, D),
            bf16(512, D),
        ),
        [],
    )(packed, gains, wq, wk, wv, wo)


def split_by_core(core_ref, weights, keep_ref, send_ref):
    low_core = core_ref[0] == 0
    for i in range(2):
        keep_ref[i] = jnp.where(low_core, weights[i], weights[2 + i])
        send_ref[i] = jnp.where(low_core, weights[2 + i], weights[i]).astype(BF)


def inter_weights_kernel(
    core_ref, normed_t_ref, grads_ref, ctx_t_ref, gq_t_ref, gk_ref, gv_ref, keep_ref, send_ref
):
    normed_t = normed_t_ref[...]
    weights = (
        nt(normed_t, gq_t_ref[...]),
        nn(normed_t, gk_ref[...]),
        nn(normed_t, gv_ref[...]),
        nn(ctx_t_ref[...], grads_ref[...]),
    )
    split_by_core(core_ref, weights, keep_ref, send_ref)


def inter_weights(core, *operands):
    return kernel_call(
        inter_weights_kernel, "inter_weights", 1, [SMEM] + [VMEM] * 6, [VMEM] * 2,
        (f32(2, D, D), bf16(2, D, D)), [],
    )(core, *operands)


KEYS, QUERIES_T, VALUES, STATS = 0, 768, 1536, 2304
QUERIES, KEYS_T, NORMED_T, CONTEXT = 2496, 3264, 4032, 4800
HANDED_ROWS = 5824


def put_stats(handed_ref, stats):
    for i in range(3):
        part = stats.astype(BF)
        stats = stats - part.astype(F32)
        put_blocks(handed_ref, STATS + 64 * i, part)


def stats_of(handed_ref):
    parts = [
        jnp.concatenate(
            [
                handed_ref[STATS + 64 * i + 32 * j : STATS + 64 * i + 32 * j + 32, :].astype(F32)
                for j in range(2)
            ],
            axis=1,
        )
        for i in range(3)
    ]
    return parts[0] + parts[1] + parts[2]


def put_blocks(handed_ref, start, array):
    for i in range(array.shape[1] // 128):
        at = start + i * array.shape[0]
        handed_ref[at : at + array.shape[0], :] = array[:, 128 * i : 128 * i + 128]


def features_of(handed_ref, start, rows, at):
    return jnp.concatenate(
        [
            handed_ref[start + 256 * i + rows.start : start + 256 * i + rows.stop, :]
            for i in range(at.start // 128, at.stop // 128)
        ],
        axis=1,
    )


def tokens_of(handed_ref, start, at, b):
    return handed_ref[start + 384 * b + at.start : start + 384 * b + at.stop, :]


def begin_layer(sems, f_any, n_any, gain_any, wq_any, wk_any, wv_any, rows_ref, gain_ref, w_ref):
    return begin(
        sems,
        (f_any, rows_ref.at[pl.ds(0, K)]),
        (n_any.at[pl.ds(0, HOP)], rows_ref.at[pl.ds(K, HOP)]),
        (gain_any, gain_ref),
        (wq_any.at[0], w_ref.at[0]),
        (wk_any.at[0], w_ref.at[1]),
        (wv_any.at[0], w_ref.at[2]),
    )


def layer_scratch():
    return [vbf(3 * HOP, D), pltpu.VMEM((2, D), F32), vbf(3, D, D)]


def intra_prepare_kernel(
    f_any, n_any, gain_any, wq_any, wk_any, wv_any, handed_ref,
    stats_ref, ctx_ref, rows_ref, gain_ref, w_ref, sems,
):
    settle(begin_layer(sems, f_any, n_any, gain_any, wq_any, wk_any, wv_any, rows_ref, gain_ref, w_ref))
    unit, _ = standardize(rows_ref[...].astype(F32))
    normed = (unit * gain_ref[0:1, :]).astype(BF)
    queries = nn(normed, w_ref[0]).astype(BF)
    keys = nn(normed, w_ref[1]).astype(BF)
    values = nn(normed, w_ref[2]).astype(BF)
    queries_t = queries.T
    values_t = values.T
    put_blocks(handed_ref, NORMED_T, normed.T)
    put_blocks(handed_ref, QUERIES, queries)
    put_blocks(handed_ref, QUERIES_T, queries_t)
    put_blocks(handed_ref, KEYS, keys)
    put_blocks(handed_ref, KEYS_T, keys.T)
    put_blocks(handed_ref, VALUES, values)
    masks = head_masks()

    def scores_of(step):
        g, h = step // HEADS, step % HEADS
        at = slice(g * HOP, g * HOP + K)
        block = slice((h // 4) * 128, (h // 4) * 128 + 128)
        return nn(keys[at, block] * masks[h % 4], queries_t[block, at])

    def weigh(step, scores):
        highest = jnp.max(scores, axis=0, keepdims=True)
        powers = jnp.exp2((scores - highest) * (SCALE * LOG2E))
        inverse = 1.0 / jnp.sum(powers, axis=0, keepdims=True)
        stats_ref[2 * step : 2 * step + 1, :] = highest
        stats_ref[2 * step + 1 : 2 * step + 2, :] = inverse
        return (powers * inverse).astype(BF)

    def collect(step, low):
        g, h = step // HEADS, step % HEADS
        feats = slice(h * HEAD, h * HEAD + HEAD)
        ctx_ref[g, feats, :] = nn(values_t[feats, g * HOP : g * HOP + K], low).astype(BF)

    staged(2 * HEADS, scores_of, weigh, collect)
    for g in range(2):
        put_blocks(handed_ref, CONTEXT + 512 * g, ctx_ref[g])
    put_stats(handed_ref, stats_ref[...])


def intra_prepare(frames, following, gains, wq, wk, wv):
    return kernel_call(
        intra_prepare_kernel, "intra_prepare", 3, [HBM] * 6, VMEM, bf16(HANDED_ROWS, 128),
        [pltpu.VMEM((4 * HEADS, K), F32), vbf(2, D, K)] + layer_scratch() + [dma(6)],
        PREPARE_LIMIT,
    )(frames, following, gains, wq, wk, wv)


def intra_backward_kernel(
    core_ref, m_ref, handed_any, wo_any,
    keep_ref, send_ref, grads_ref, gq_t, gk_ref, gv_ref,
    handed_ref, stats_ref, wo_ref, sems,
):
    cuts = (KEYS, QUERIES, NORMED_T, HANDED_ROWS)
    spans = [pl.ds(start, end - start) for start, end in zip(cuts, cuts[1:])]
    copies = begin(
        sems,
        (wo_any.at[0], wo_ref),
        *[(handed_any.at[span], handed_ref.at[span]) for span in spans],
    )
    pick = select_rows(256, 256, owner_target)
    tiles = [nn(pick, m_ref[256 * t : 256 * t + 256, :]).astype(BF) for t in range(2)]
    masks = head_masks()
    context, context_t = [], []
    for g in range(2):
        grads_ref[g] = jnp.concatenate(
            [tiles[t][128 * g + 64 * h : 128 * g + 64 * h + 64] for h in range(2) for t in range(2)],
            axis=0,
        )
        if g == 0:
            copies[0].wait()
        context.append(nt(grads_ref[g], wo_ref[...]).astype(BF))
        context_t.append(context[g].T)

    copies[1].wait()
    stats_ref[...] = stats_of(handed_ref)

    def place(step):
        g, h = step // HEADS, step % HEADS
        return g, slice(g * HOP, g * HOP + K), h // 4, h % 4

    def products(step):
        g, at, b, i = place(step)
        block = slice(128 * b, 128 * b + 128)
        keys = tokens_of(handed_ref, KEYS, at, b) * masks[i]
        scores = nn(keys, features_of(handed_ref, QUERIES_T, block, at))
        values = tokens_of(handed_ref, VALUES, at, b) * masks[i]
        return scores, nn(values, context_t[g][block, :])

    def weigh(step, held):
        scores, grad_probs = held
        powers = jnp.exp2((scores - stats_ref[2 * step : 2 * step + 1, :]) * (SCALE * LOG2E))
        probs = powers * stats_ref[2 * step + 1 : 2 * step + 2, :]
        inner = jnp.sum(grad_probs * probs, axis=0, keepdims=True)
        return probs.astype(BF), (probs * (grad_probs - inner) * SCALE).astype(BF)

    sums = {}

    def collect(step, held):
        if step == 0:
            copies[2].wait()
        low, grad_scores = held
        g, at, b, i = place(step)
        block = slice(128 * b, 128 * b + 128)
        feats = slice(128 * b + HEAD * i, 128 * b + HEAD * i + HEAD)
        gv = nn(low, context[g][:, block] * masks[i])
        gk = nn(grad_scores, tokens_of(handed_ref, QUERIES, at, b) * masks[i])
        keys_t = features_of(handed_ref, KEYS_T, feats, at)
        gq_t[g, feats, :] = nn(keys_t, grad_scores).astype(BF)
        sums["v"] = gv if i == 0 else sums["v"] + gv
        sums["k"] = gk if i == 0 else sums["k"] + gk
        if i == 3:
            gv_ref[g, :, block] = sums["v"].astype(BF)
            gk_ref[g, :, block] = sums["k"].astype(BF)

    staged(2 * HEADS, products, weigh, collect)
    copies[3].wait()
    parts = []
    for g in range(2):
        normed_t = features_of(
            handed_ref, NORMED_T, slice(0, D), slice(g * HOP, g * HOP + K)
        )
        context_0 = jnp.concatenate(
            [handed_ref[pl.ds(CONTEXT + 512 * g + 256 * i, 256), :] for i in range(2)], axis=1
        )
        parts.append(
            (
                nt(normed_t, gq_t[g]),
                nn(normed_t, gk_ref[g]),
                nn(normed_t, gv_ref[g]),
                nn(context_0, grads_ref[g]),
            )
        )
    totals = [first + second for first, second in zip(*parts)]
    split_by_core(core_ref, totals, keep_ref, send_ref)


def intra_backward(core, grads, *rest):
    return kernel_call(
        intra_backward_kernel, "intra_backward", 4, [SMEM, VMEM] + [HBM] * 2, [VMEM] * 6,
        (
            f32(2, D, D), bf16(2, D, D), bf16(2, K, D), bf16(2, D, K), bf16(2, K, D), bf16(2, K, D),
        ),
        [vbf(HANDED_ROWS, 128), pltpu.VMEM((4 * HEADS, K), F32), vbf(D, D), dma(4)],
        BACKWARD_LIMIT,
    )(core, grads, *rest)


def intra_tail_kernel(
    grads_any, gq_t_any, gk_any, gv_any, f_any, n_any, gain_any, wq_any, wk_any, wv_any,
    first_ref, second_ref, carry_ref,
    grads_ref, gq_t_ref, gk_ref, gv_ref, rows_ref, gain_ref, w_ref, sems, own_sems,
):
    copies = begin_layer(sems, f_any, n_any, gain_any, wq_any, wk_any, wv_any, rows_ref, gain_ref, w_ref)
    copies += begin(
        own_sems,
        (grads_any, grads_ref), (gq_t_any, gq_t_ref), (gk_any, gk_ref), (gv_any, gv_ref),
    )
    settle(copies)
    unit, inverse = standardize(rows_ref[...].astype(F32))
    halves = []
    for g in range(2):
        at = slice(g * HOP, g * HOP + K)
        grad_normed = (
            nt(gq_t_ref[g].T, w_ref[0]) + nt(gk_ref[g], w_ref[1]) + nt(gv_ref[g], w_ref[2])
        )
        pulled = norm_pullback(grad_normed, unit[at], inverse[at], gain_ref[0:1, :])
        result = (grads_ref[g].astype(F32) + pulled).astype(BF)
        halves.append((result[:HOP], result[HOP:]))
    first_ref[...] = halves[0][0]
    second_ref[...] = (halves[1][0].astype(F32) + halves[0][1].astype(F32)).astype(BF)
    carry_ref[...] = halves[1][1]


def intra_tail(*operands):
    return kernel_call(
        intra_tail_kernel, "intra_tail", 2, [HBM] * 10, [VMEM] * 3,
        (bf16(HOP, D), bf16(HOP, D), bf16(HOP, D)),
        [vbf(2, K, D), vbf(2, D, K), vbf(2, K, D), vbf(2, K, D)]
        + layer_scratch()
        + [dma(6), dma(4)],
    )(*operands)


def finish_kernel(
    core_ref, mine_ref, other_ref, first_ref, second_ref, carried_ref, gain_ref, wq_ref, wk_ref, wv_ref,
    frames_ref, dq_ref, dk_ref, dv_ref, do_ref, dg_ref,
):
    frames_ref[:HOP] = (first_ref[...].astype(F32) + carried_ref[...].astype(F32)).astype(BF)
    frames_ref[HOP:] = second_ref[...]
    low_core = core_ref[0] == 0
    for layer in range(2):
        mine = mine_ref[:, layer].reshape(2, D, D).astype(F32)
        other = other_ref[:, layer].reshape(2, D, D).astype(F32)
        dq = jnp.where(low_core, mine[0], other[0])
        dk = jnp.where(low_core, mine[1], other[1])
        dv = jnp.where(low_core, other[0], mine[0])
        dq_ref[layer] = dq
        dk_ref[layer] = dk
        dv_ref[layer] = dv
        do_ref[layer] = jnp.where(low_core, other[1], mine[1])
        through = (
            dq * wq_ref[layer].astype(F32)
            + dk * wk_ref[layer].astype(F32)
            + dv * wv_ref[layer].astype(F32)
        )
        column = jnp.sum(through.T, axis=0, keepdims=True)
        dg_ref[layer : layer + 1, :] = column / gain_ref[layer : layer + 1, :]


def finish(core, *operands):
    full = f32(2, D, D)
    return kernel_call(
        finish_kernel, "finish", 2, [SMEM] + [VMEM] * 9, [VMEM] * 6,
        (bf16(K, D), full, full, full, full, f32(2, D)), [],
    )(core, *operands)


def shifted(shard, by):
    length = lax.axis_size(TM)
    pairs = [(i, i + by) for i in range(length) if 0 <= i + by < length]
    return lax.ppermute(shard, TM, pairs)


def exchanged(shard, axes):
    return lax.all_to_all(shard, axes, split_axis=0, concat_axis=0, tiled=True)


def swapped(shard):
    return lax.ppermute(shard, "core", [(0, 1), (1, 0)])


def spread_kernel(pieces_ref, out_ref):
    total = jnp.sum(pieces_ref[...].astype(F32), axis=0).astype(BF)
    for i in range(out_ref.shape[0]):
        out_ref[i] = total


def spread(pieces, count):
    return kernel_call(
        spread_kernel, "spread", 1, [VMEM], VMEM, bf16(count, *pieces.shape[1:]), []
    )(pieces)


def core_sum_kernel(keep_ref, arrived_ref, out_ref):
    out_ref[...] = (keep_ref[...] + arrived_ref[...].astype(F32)).astype(BF)


def core_sum(keep, send):
    return kernel_call(
        core_sum_kernel, "core_sum", 1, [VMEM] * 2, VMEM, bf16(2, D, D), []
    )(keep, swapped(send))


def both_sums_kernel(keep_ref, arrived_ref, inter_ref, out_ref):
    half = (keep_ref[...] + arrived_ref[...].astype(F32)).astype(BF)
    out_ref[:, :16] = half.reshape(32, 16, D)
    out_ref[:, 16:] = inter_ref[...].reshape(32, 16, D)


def both_sums(keep, send, inter_half):
    return kernel_call(
        both_sums_kernel, "both_sums", 1, [VMEM] * 3, VMEM, bf16(32, 32, D), []
    )(keep, swapped(send), inter_half)


def shards(frames, frames_grad, wq, wk, wv, wo, gains):
    frames = frames[0]
    core = lax.axis_index("core").astype(jnp.int32).reshape(1)
    following = shifted(frames, -1)
    front = intra_first(frames, gains, wq, wk, wv, wo)
    packed = intra_second(
        following, *front, frames, frames_grad[0], gains, wq, wk, wv, wo
    )
    across = exchanged(packed.reshape(64, 8, 384), TM).reshape(512, 384)
    grad_middle, *operands = inter(across, gains, wq, wk, wv, wo)
    grad_local = exchanged(grad_middle.reshape(64, 8, D), TM).reshape(512, D)
    inter_half = core_sum(*inter_weights(core, *operands))
    grad_local, inter_half = lax.optimization_barrier((grad_local, inter_half))
    handed = intra_prepare(frames, following, gains, wq, wk, wv)
    keep, send, *rest = intra_backward(core, grad_local, handed, wo)
    half = both_sums(keep, send, inter_half)
    first, second, carry = intra_tail(*rest, frames, following, gains, wq, wk, wv)
    carried = shifted(carry, 1)
    sent = spread(exchanged(half, PLANE), 4)
    sent, carried = lax.optimization_barrier((sent, carried))
    sent = spread(exchanged(sent, "za"), 32)
    whole = exchanged(sent, PLANE).reshape(32, 2, 16, D)
    other = swapped(whole)
    grad_frames, *weights = finish(
        core, whole, other, first, second, carried, gains, wq, wk, wv
    )
    return (grad_frames[None], *weights)


def solution(mesh):
    split = Mesh(mesh.devices.reshape(2, 2, 2, 4, 4, 2), AXES)
    placed = (P(DP, TM, None), P(DP, TM, None), P(), P(), P(), P(), P())
    return jax.shard_map(
        shards,
        mesh=split,
        in_specs=placed,
        out_specs=(P(DP, TM, None), P(), P(), P(), P(), P()),
        check_vma=False,
    )
```

```python
import math

import jax
import jax.numpy as jnp
from jax import lax
from jax.experimental import pallas as pl
from jax.experimental.pallas import tpu as pltpu
from jax.sharding import Mesh, PartitionSpec as P

HEADS = 8
HEAD = 32
D = 256
K = 256
HOP = 128
SEGMENTS = 128
EPSILON = 1e-05
SCALE = HEAD ** (-0.5)
LOG2E = math.log2(math.e)
BF = jnp.bfloat16
F32 = jnp.float32
VMEM_LIMIT = 16 * 1024 * 1024
FIRST_LIMIT = 54800 * 1024
SECOND_LIMIT = 54300 * 1024
BACKWARD_LIMIT = 52850 * 1024

AXES = ("yh", "core", "yl", "x", "za", "zb")
DP = ("yh", "core")
TM = ("yl", "x", "za", "zb")
PLANE = ("yh", "yl", "x", "zb")


def dot(left, right, left_dim, right_dim):
    return lax.dot_general(
        left, right, (((left_dim,), (right_dim,)), ((), ())), preferred_element_type=F32
    )


def nn(left, right):
    return dot(left, right, 1, 0)


def nt(left, right):
    return dot(left, right, 1, 1)


def tn(left, right):
    return dot(left, right, 0, 0)


def standardize(rows):
    average = jnp.mean(rows, axis=-1, keepdims=True)
    centered = rows - average
    variance = jnp.mean(centered * centered, axis=-1, keepdims=True)
    inverse = lax.rsqrt(variance + EPSILON)
    return centered * inverse, inverse


def norm_pullback(grad_normed, unit, inverse, gain):
    grad_unit = grad_normed * gain
    first = jnp.mean(grad_unit, axis=-1, keepdims=True)
    second = jnp.mean(grad_unit * unit, axis=-1, keepdims=True)
    return inverse * (grad_unit - first - unit * second)


def head_masks():
    lane = lax.broadcasted_iota(jnp.int32, (1, 128), 1)
    return [jnp.where(lane // HEAD == i, 1.0, 0.0).astype(BF) for i in range(4)]


def row_masks():
    row = lax.broadcasted_iota(jnp.int32, (128, 1), 0)
    return [jnp.where(row // HEAD == i, 1.0, 0.0).astype(BF) for i in range(4)]


def select_rows(out_rows, in_rows, source):
    out = lax.broadcasted_iota(jnp.int32, (out_rows, in_rows), 0)
    col = lax.broadcasted_iota(jnp.int32, (out_rows, in_rows), 1)
    return jnp.where(source(out) == col, 1.0, 0.0).astype(BF)


def softmax_keys(scores):
    highest = jnp.max(scores, axis=0, keepdims=True)
    powers = jnp.exp2((scores - highest) * (SCALE * LOG2E))
    return powers * (1.0 / jnp.sum(powers, axis=0, keepdims=True))


def owner_target(out):
    return ((out % 64) // 2) * 8 + (out // 64) * 2 + out % 2


def segment_target(out):
    return (out % 4) * 64 + out // 4


def packed_source(out):
    return ((out // 2) % 4) * 64 + (out // 8) * 2 + out % 2


def middle_source(out):
    return ((out % 64) // 2) * 8 + (out % 2) * 4 + out // 64


def cotangent_source(out):
    hop = out % 64
    return (hop // 2) * 8 + (out // 128) * 4 + (hop % 2) * 2 + (out // 64) % 2


def staged(count, *stages):
    held = [{} for _ in stages]
    for t in range(count + len(stages) - 1):
        for i, stage in enumerate(stages):
            step = t - i
            if 0 <= step < count:
                held[i][step] = stage(step, *([held[i - 1].pop(step)] if i else []))


def attend(keys, queries_t, values_t, ctx_ref):
    masks = head_masks()

    def scores_of(h):
        block = slice((h // 4) * 128, (h // 4) * 128 + 128)
        return nn(keys[:, block] * masks[h % 4], queries_t[block, :])

    def weigh(h, scores):
        return softmax_keys(scores).astype(BF)

    def collect(h, low):
        feats = slice(h * HEAD, h * HEAD + HEAD)
        ctx_ref[feats, :] = nn(values_t[feats, :], low).astype(BF)

    staged(HEADS, scores_of, weigh, collect)


VMEM = pl.BlockSpec(memory_space=pltpu.VMEM)
SMEM = pl.BlockSpec(memory_space=pltpu.SMEM)
HBM = pl.BlockSpec(memory_space=pltpu.HBM)


def begin(sems, *pairs):
    copies = [pltpu.make_async_copy(src, dst, sems.at[i]) for i, (src, dst) in enumerate(pairs)]
    for copy in copies:
        copy.start()
    return copies


def settle(copies):
    for copy in copies:
        copy.wait()


def bf16(*shape):
    return jax.ShapeDtypeStruct(shape, BF)


def f32(*shape):
    return jax.ShapeDtypeStruct(shape, F32)


def kernel_call(kernel, name, micros, in_specs, out_specs, out_shape, scratch, limit=VMEM_LIMIT):
    return pl.pallas_call(
        kernel,
        in_specs=in_specs,
        out_specs=out_specs,
        out_shape=out_shape,
        scratch_shapes=scratch,
        compiler_params=pltpu.CompilerParams(vmem_limit_bytes=limit),
        cost_estimate=pl.CostEstimate(
            flops=int(micros * 400e6), bytes_accessed=1 << 20, transcendentals=0
        ),
        name=name,
    )


def dma(count):
    return pltpu.SemaphoreType.DMA((count,))


def vbf(*shape):
    return pltpu.VMEM(shape, BF)


def intra_first_kernel(
    f_any, gain_any, wq_any, wk_any, wv_any, wo_any,
    mid_ref, keys_ref, queries_ref, values_ref,
    w_ref, gain_ref, f_ref, ctx_ref, sems,
):
    copies = begin(
        sems,
        (f_any, f_ref),
        (gain_any, gain_ref),
        (wk_any.at[0], w_ref.at[1]),
        (wq_any.at[0], w_ref.at[0]),
        (wv_any.at[0], w_ref.at[2]),
        (wo_any.at[0], w_ref.at[3]),
    )
    copies[0].wait()
    rows = f_ref[...].astype(F32)
    unit, _ = standardize(rows)
    copies[1].wait()
    normed = (unit * gain_ref[0:1, :]).astype(BF)
    settle(copies[2:5])
    keys = nn(normed, w_ref[1]).astype(BF)
    queries_t = nt(w_ref[0].T, normed).astype(BF)
    values_t = nt(w_ref[2].T, normed).astype(BF)
    attend(keys, queries_t, values_t, ctx_ref)
    copies[5].wait()
    mid_ref[...] = (rows + tn(ctx_ref[...], w_ref[3])).astype(BF)
    keys_ref[...] = keys[HOP:]
    queries_ref[...] = queries_t[:, HOP:]
    values_ref[...] = values_t[:, HOP:]


def intra_second_kernel(
    n_ref, mid_in_ref, keys_ref, queries_ref, values_ref,
    f_any, grad_any, gain_any, wq_any, wk_any, wv_any, wo_any, packed_ref,
    f_ref, grad_ref, gain_ref, w_ref, ctx_ref, sems,
):
    copies = begin(
        sems,
        (gain_any, gain_ref),
        (wk_any.at[0], w_ref.at[1]),
        (wq_any.at[0], w_ref.at[0]),
        (wv_any.at[0], w_ref.at[2]),
        (wo_any.at[0], w_ref.at[3]),
        (f_any.at[pl.ds(HOP, HOP)], f_ref),
        (grad_any, grad_ref),
    )
    rows = n_ref[:HOP].astype(F32)
    unit, _ = standardize(rows)
    settle(copies[:4])
    normed = (unit * gain_ref[0:1, :]).astype(BF)
    keys = jnp.concatenate([keys_ref[...], nn(normed, w_ref[1]).astype(BF)], axis=0)
    queries_t = jnp.concatenate(
        [queries_ref[...], nt(w_ref[0].T, normed).astype(BF)], axis=1
    )
    values_t = jnp.concatenate([values_ref[...], nt(w_ref[2].T, normed).astype(BF)], axis=1)
    attend(keys, queries_t, values_t, ctx_ref)
    settle(copies[4:])
    rows = jnp.concatenate([f_ref[...].astype(F32), rows], axis=0)
    mids = (mid_in_ref[...], (rows + tn(ctx_ref[...], w_ref[3])).astype(BF))
    grads = grad_ref[...]
    pick = select_rows(256, 256, packed_source)
    for t in range(2):
        parts = []
        for part in range(4):
            high, low = part // 2, part % 2
            at = slice(low * HOP + 64 * t, low * HOP + 64 * t + 64)
            parts.append(
                jnp.concatenate([mids[high][at], grads[at, 128 * high : 128 * high + 128]], axis=1)
            )
        rows = jnp.concatenate(parts, axis=0)
        packed_ref[256 * t : 256 * t + 256, :] = nn(pick, rows).astype(BF)


def intra_first(frames, gains, wq, wk, wv, wo):
    return kernel_call(
        intra_first_kernel, "intra_first", 3, [HBM] * 6, [VMEM] * 4,
        (bf16(K, D), bf16(HOP, D), bf16(D, HOP), bf16(D, HOP)),
        [vbf(4, D, D), pltpu.VMEM((2, D), F32), vbf(K, D), vbf(D, K), dma(6)],
        FIRST_LIMIT,
    )(frames, gains, wq, wk, wv, wo)


def intra_second(following, *rest):
    return kernel_call(
        intra_second_kernel, "intra_second", 3, [VMEM] * 5 + [HBM] * 7, VMEM,
        bf16(512, 384),
        [
            vbf(HOP, D), vbf(K, D), pltpu.VMEM((2, D), F32), vbf(4, D, D), vbf(D, K), dma(7),
        ],
        SECOND_LIMIT,
    )(following, *rest)


def inter_kernel(
    packed_ref, gain_ref, wq_ref, wk_ref, wv_ref, wo_ref,
    out_ref, normed_t_ref, grads_ref, ctx_t, gq_t, gk_ref, gv_ref,
):
    gain = gain_ref[1:2, :]
    pick = select_rows(256, 256, middle_source)
    tiles = [nn(pick, packed_ref[256 * t : 256 * t + 256, :D]) for t in range(2)]
    rows = jnp.concatenate(
        [tiles[t][64 * p : 64 * p + 64] for p in range(4) for t in range(2)], axis=0
    )
    pick = select_rows(256, 256, cotangent_source)
    tiles = [nn(pick, packed_ref[256 * t : 256 * t + 256, D:]) for t in range(2)]
    hops = [
        jnp.concatenate(
            [
                jnp.concatenate(
                    [tiles[t][128 * c + 64 * r : 128 * c + 64 * r + 64] for c in range(2)], axis=1
                )
                for t in range(2)
            ],
            axis=0,
        )
        for r in range(2)
    ]
    last = jnp.zeros((1, D), F32)
    late = [jnp.concatenate([hop[1:], last], axis=0) for hop in hops]
    grads = jnp.concatenate(hops + late, axis=0).astype(BF)
    grads_ref[...] = grads
    unit, inverse = standardize(rows)
    normed = (unit * gain).astype(BF)
    normed_t_ref[...] = normed.T
    wq, wk, wv, wo = wq_ref[1], wk_ref[1], wv_ref[1], wo_ref[1]
    queries = nn(normed, wq).astype(BF)
    keys = nn(normed, wk).astype(BF)
    values = nn(normed, wv).astype(BF)
    grad_context = nt(grads, wo).astype(BF)
    queries_t = queries.T
    keys_t = keys.T
    values_t = values.T
    grad_context_t = grad_context.T
    masks = head_masks()
    downs = row_masks()

    def place(step):
        p, b, pair = step // 4, (step // 2) % 2, step % 2
        return slice(128 * p, 128 * p + 128), slice(128 * b, 128 * b + 128), pair

    def columns(rows_t, pair):
        return jnp.concatenate([rows_t * downs[2 * pair], rows_t * downs[2 * pair + 1]], axis=1)

    def stacked(rows, pair):
        return jnp.concatenate([rows * masks[2 * pair], rows * masks[2 * pair + 1]], axis=0)

    def products(step):
        at, block, pair = place(step)
        scores = nn(keys[at, block], columns(queries_t[block, at], pair))
        grad_probs = nn(values[at, block], columns(grad_context_t[block, at], pair))
        return scores, grad_probs

    def weigh(step, held):
        scores, grad_probs = held
        probs = softmax_keys(scores)
        inner = jnp.sum(grad_probs * probs, axis=0, keepdims=True)
        return probs.astype(BF), (probs * (grad_probs - inner) * SCALE).astype(BF)

    sums = {}

    def collect(step, held):
        low, grad_scores = held
        at, block, pair = place(step)
        gv = nn(low, stacked(grad_context[at, block], pair))
        gk = nn(grad_scores, stacked(queries[at, block], pair))
        if pair == 0:
            sums["v"], sums["k"] = gv, gk
        else:
            gv_ref[at, block] = (sums["v"] + gv).astype(BF)
            gk_ref[at, block] = (sums["k"] + gk).astype(BF)
        start = block.start + 64 * pair
        for target, rows_t, right in ((ctx_t, values_t, low), (gq_t, keys_t, grad_scores)):
            both = nn(rows_t[start : start + 64, at], right)
            target[start : start + 32, at] = both[:32, :128].astype(BF)
            target[start + 32 : start + 64, at] = both[32:, 128:].astype(BF)

    staged(16, products, weigh, collect)
    gqt, gk, gv = gq_t[...], gk_ref[...], gv_ref[...]
    grad_normed = nt(gqt.T, wq) + nt(gk, wk) + nt(gv, wv)
    result = (grads.astype(F32) + norm_pullback(grad_normed, unit, inverse, gain)).astype(BF)
    back = select_rows(256, 256, segment_target)
    for t in range(2):
        part = jnp.concatenate(
            [result[128 * p + 64 * t : 128 * p + 64 * t + 64] for p in range(4)], axis=0
        )
        out_ref[256 * t : 256 * t + 256, :] = nn(back, part).astype(BF)


def inter(packed, gains, wq, wk, wv, wo):
    return kernel_call(
        inter_kernel, "inter", 5, [VMEM] * 6, [VMEM] * 7,
        (
            bf16(512, D), bf16(D, 512), bf16(512, D), bf16(D, 512), bf16(D, 512), bf16(512, D),
            bf16(512, D),
        ),
        [],
    )(packed, gains, wq, wk, wv, wo)


def split_by_core(core_ref, weights, keep_ref, send_ref):
    low_core = core_ref[0] == 0
    for i in range(2):
        keep_ref[i] = jnp.where(low_core, weights[i], weights[2 + i])
        send_ref[i] = jnp.where(low_core, weights[2 + i], weights[i]).astype(BF)


def inter_weights_kernel(
    core_ref, normed_t_ref, grads_ref, ctx_t_ref, gq_t_ref, gk_ref, gv_ref, keep_ref, send_ref
):
    normed_t = normed_t_ref[...]
    weights = (
        nt(normed_t, gq_t_ref[...]),
        nn(normed_t, gk_ref[...]),
        nn(normed_t, gv_ref[...]),
        nn(ctx_t_ref[...], grads_ref[...]),
    )
    split_by_core(core_ref, weights, keep_ref, send_ref)


def inter_weights(core, *operands):
    return kernel_call(
        inter_weights_kernel, "inter_weights", 1, [SMEM] + [VMEM] * 6, [VMEM] * 2,
        (f32(2, D, D), bf16(2, D, D)), [],
    )(core, *operands)


KEYS, QUERIES_T, VALUES, STATS = 0, 768, 1536, 2304
QUERIES, KEYS_T, NORMED_T, CONTEXT = 2496, 3264, 4032, 4800
HANDED_ROWS = 5824


def put_stats(handed_ref, stats):
    for i in range(3):
        part = stats.astype(BF)
        stats = stats - part.astype(F32)
        put_blocks(handed_ref, STATS + 64 * i, part)


def stats_of(handed_ref):
    parts = [
        jnp.concatenate(
            [
                handed_ref[STATS + 64 * i + 32 * j : STATS + 64 * i + 32 * j + 32, :].astype(F32)
                for j in range(2)
            ],
            axis=1,
        )
        for i in range(3)
    ]
    return parts[0] + parts[1] + parts[2]


def put_blocks(handed_ref, start, array):
    for i in range(array.shape[1] // 128):
        at = start + i * array.shape[0]
        handed_ref[at : at + array.shape[0], :] = array[:, 128 * i : 128 * i + 128]


def features_of(handed_ref, start, rows, at):
    return jnp.concatenate(
        [
            handed_ref[start + 256 * i + rows.start : start + 256 * i + rows.stop, :]
            for i in range(at.start // 128, at.stop // 128)
        ],
        axis=1,
    )


def tokens_of(handed_ref, start, at, b):
    return handed_ref[start + 384 * b + at.start : start + 384 * b + at.stop, :]


def begin_layer(sems, f_any, n_any, gain_any, wq_any, wk_any, wv_any, rows_ref, gain_ref, w_ref):
    return begin(
        sems,
        (f_any, rows_ref.at[pl.ds(0, K)]),
        (n_any.at[pl.ds(0, HOP)], rows_ref.at[pl.ds(K, HOP)]),
        (gain_any, gain_ref),
        (wq_any.at[0], w_ref.at[0]),
        (wk_any.at[0], w_ref.at[1]),
        (wv_any.at[0], w_ref.at[2]),
    )


def layer_scratch():
    return [vbf(3 * HOP, D), pltpu.VMEM((2, D), F32), vbf(3, D, D)]


def intra_prepare_kernel(
    f_ref, n_ref, gain_ref, wq_ref, wk_ref, wv_ref, handed_ref, stats_ref, ctx_ref
):
    rows = jnp.concatenate([f_ref[...], n_ref[:HOP]], axis=0)
    unit, _ = standardize(rows.astype(F32))
    normed = (unit * gain_ref[0:1, :]).astype(BF)
    queries = nn(normed, wq_ref[0]).astype(BF)
    keys = nn(normed, wk_ref[0]).astype(BF)
    values = nn(normed, wv_ref[0]).astype(BF)
    queries_t = queries.T
    values_t = values.T
    put_blocks(handed_ref, NORMED_T, normed.T)
    put_blocks(handed_ref, QUERIES, queries)
    put_blocks(handed_ref, QUERIES_T, queries_t)
    put_blocks(handed_ref, KEYS, keys)
    put_blocks(handed_ref, KEYS_T, keys.T)
    put_blocks(handed_ref, VALUES, values)
    masks = head_masks()

    def scores_of(step):
        g, h = step // HEADS, step % HEADS
        at = slice(g * HOP, g * HOP + K)
        block = slice((h // 4) * 128, (h // 4) * 128 + 128)
        return nn(keys[at, block] * masks[h % 4], queries_t[block, at])

    def weigh(step, scores):
        highest = jnp.max(scores, axis=0, keepdims=True)
        powers = jnp.exp2((scores - highest) * (SCALE * LOG2E))
        inverse = 1.0 / jnp.sum(powers, axis=0, keepdims=True)
        stats_ref[2 * step : 2 * step + 1, :] = highest
        stats_ref[2 * step + 1 : 2 * step + 2, :] = inverse
        return (powers * inverse).astype(BF)

    def collect(step, low):
        g, h = step // HEADS, step % HEADS
        feats = slice(h * HEAD, h * HEAD + HEAD)
        ctx_ref[g, feats, :] = nn(values_t[feats, g * HOP : g * HOP + K], low).astype(BF)

    staged(2 * HEADS, scores_of, weigh, collect)
    for g in range(2):
        put_blocks(handed_ref, CONTEXT + 512 * g, ctx_ref[g])
    put_stats(handed_ref, stats_ref[...])


def intra_prepare(frames, following, gains, wq, wk, wv):
    return kernel_call(
        intra_prepare_kernel, "intra_prepare", 3, [VMEM] * 6, VMEM, bf16(HANDED_ROWS, 128),
        [pltpu.VMEM((4 * HEADS, K), F32), vbf(2, D, K)],
    )(frames, following, gains, wq, wk, wv)


def intra_backward_kernel(
    core_ref, m_ref, handed_any, wo_any,
    keep_ref, send_ref, grads_ref, gq_t, gk_ref, gv_ref,
    handed_ref, stats_ref, wo_ref, sems,
):
    cuts = (KEYS, QUERIES, NORMED_T, HANDED_ROWS)
    spans = [pl.ds(start, end - start) for start, end in zip(cuts, cuts[1:])]
    copies = begin(
        sems,
        (wo_any.at[0], wo_ref),
        *[(handed_any.at[span], handed_ref.at[span]) for span in spans],
    )
    pick = select_rows(256, 256, owner_target)
    tiles = [nn(pick, m_ref[256 * t : 256 * t + 256, :]).astype(BF) for t in range(2)]
    masks = head_masks()
    context, context_t = [], []
    for g in range(2):
        grads_ref[g] = jnp.concatenate(
            [tiles[t][128 * g + 64 * h : 128 * g + 64 * h + 64] for h in range(2) for t in range(2)],
            axis=0,
        )
        if g == 0:
            copies[0].wait()
        context.append(nt(grads_ref[g], wo_ref[...]).astype(BF))
        context_t.append(context[g].T)

    copies[1].wait()
    stats_ref[...] = stats_of(handed_ref)

    def place(step):
        g, h = step // HEADS, step % HEADS
        return g, slice(g * HOP, g * HOP + K), h // 4, h % 4

    def products(step):
        g, at, b, i = place(step)
        block = slice(128 * b, 128 * b + 128)
        keys = tokens_of(handed_ref, KEYS, at, b) * masks[i]
        scores = nn(keys, features_of(handed_ref, QUERIES_T, block, at))
        values = tokens_of(handed_ref, VALUES, at, b) * masks[i]
        return scores, nn(values, context_t[g][block, :])

    def weigh(step, held):
        scores, grad_probs = held
        powers = jnp.exp2((scores - stats_ref[2 * step : 2 * step + 1, :]) * (SCALE * LOG2E))
        probs = powers * stats_ref[2 * step + 1 : 2 * step + 2, :]
        inner = jnp.sum(grad_probs * probs, axis=0, keepdims=True)
        return probs.astype(BF), (probs * (grad_probs - inner) * SCALE).astype(BF)

    sums = {}

    def collect(step, held):
        if step == 0:
            copies[2].wait()
        low, grad_scores = held
        g, at, b, i = place(step)
        block = slice(128 * b, 128 * b + 128)
        feats = slice(128 * b + HEAD * i, 128 * b + HEAD * i + HEAD)
        gv = nn(low, context[g][:, block] * masks[i])
        gk = nn(grad_scores, tokens_of(handed_ref, QUERIES, at, b) * masks[i])
        keys_t = features_of(handed_ref, KEYS_T, feats, at)
        gq_t[g, feats, :] = nn(keys_t, grad_scores).astype(BF)
        sums["v"] = gv if i == 0 else sums["v"] + gv
        sums["k"] = gk if i == 0 else sums["k"] + gk
        if i == 3:
            gv_ref[g, :, block] = sums["v"].astype(BF)
            gk_ref[g, :, block] = sums["k"].astype(BF)

    staged(2 * HEADS, products, weigh, collect)
    copies[3].wait()
    parts = []
    for g in range(2):
        normed_t = features_of(
            handed_ref, NORMED_T, slice(0, D), slice(g * HOP, g * HOP + K)
        )
        context_0 = jnp.concatenate(
            [handed_ref[pl.ds(CONTEXT + 512 * g + 256 * i, 256), :] for i in range(2)], axis=1
        )
        parts.append(
            (
                nt(normed_t, gq_t[g]),
                nn(normed_t, gk_ref[g]),
                nn(normed_t, gv_ref[g]),
                nn(context_0, grads_ref[g]),
            )
        )
    totals = [first + second for first, second in zip(*parts)]
    split_by_core(core_ref, totals, keep_ref, send_ref)


def intra_backward(core, grads, *rest):
    return kernel_call(
        intra_backward_kernel, "intra_backward", 4, [SMEM, VMEM] + [HBM] * 2, [VMEM] * 6,
        (
            f32(2, D, D), bf16(2, D, D), bf16(2, K, D), bf16(2, D, K), bf16(2, K, D), bf16(2, K, D),
        ),
        [vbf(HANDED_ROWS, 128), pltpu.VMEM((4 * HEADS, K), F32), vbf(D, D), dma(4)],
        BACKWARD_LIMIT,
    )(core, grads, *rest)


def intra_tail_kernel(
    grads_any, gq_t_any, gk_any, gv_any, f_any, n_any, gain_any, wq_any, wk_any, wv_any,
    first_ref, second_ref, carry_ref,
    grads_ref, gq_t_ref, gk_ref, gv_ref, rows_ref, gain_ref, w_ref, sems, own_sems,
):
    copies = begin_layer(sems, f_any, n_any, gain_any, wq_any, wk_any, wv_any, rows_ref, gain_ref, w_ref)
    copies += begin(
        own_sems,
        (grads_any, grads_ref), (gq_t_any, gq_t_ref), (gk_any, gk_ref), (gv_any, gv_ref),
    )
    settle(copies)
    unit, inverse = standardize(rows_ref[...].astype(F32))
    halves = []
    for g in range(2):
        at = slice(g * HOP, g * HOP + K)
        grad_normed = (
            nt(gq_t_ref[g].T, w_ref[0]) + nt(gk_ref[g], w_ref[1]) + nt(gv_ref[g], w_ref[2])
        )
        pulled = norm_pullback(grad_normed, unit[at], inverse[at], gain_ref[0:1, :])
        result = (grads_ref[g].astype(F32) + pulled).astype(BF)
        halves.append((result[:HOP], result[HOP:]))
    first_ref[...] = halves[0][0]
    second_ref[...] = (halves[1][0].astype(F32) + halves[0][1].astype(F32)).astype(BF)
    carry_ref[...] = halves[1][1]


def intra_tail(*operands):
    return kernel_call(
        intra_tail_kernel, "intra_tail", 2, [HBM] * 10, [VMEM] * 3,
        (bf16(HOP, D), bf16(HOP, D), bf16(HOP, D)),
        [vbf(2, K, D), vbf(2, D, K), vbf(2, K, D), vbf(2, K, D)]
        + layer_scratch()
        + [dma(6), dma(4)],
    )(*operands)


def finish_kernel(
    core_ref, mine_ref, other_ref, first_ref, second_ref, carried_ref, gain_ref, wq_ref, wk_ref, wv_ref,
    frames_ref, dq_ref, dk_ref, dv_ref, do_ref, dg_ref,
):
    frames_ref[:HOP] = (first_ref[...].astype(F32) + carried_ref[...].astype(F32)).astype(BF)
    frames_ref[HOP:] = second_ref[...]
    low_core = core_ref[0] == 0
    for layer in range(2):
        mine = mine_ref[:, layer].reshape(2, D, D).astype(F32)
        other = other_ref[:, layer].reshape(2, D, D).astype(F32)
        dq = jnp.where(low_core, mine[0], other[0])
        dk = jnp.where(low_core, mine[1], other[1])
        dv = jnp.where(low_core, other[0], mine[0])
        dq_ref[layer] = dq
        dk_ref[layer] = dk
        dv_ref[layer] = dv
        do_ref[layer] = jnp.where(low_core, other[1], mine[1])
        through = (
            dq * wq_ref[layer].astype(F32)
            + dk * wk_ref[layer].astype(F32)
            + dv * wv_ref[layer].astype(F32)
        )
        column = jnp.sum(through.T, axis=0, keepdims=True)
        dg_ref[layer : layer + 1, :] = column / gain_ref[layer : layer + 1, :]


def finish(core, *operands):
    full = f32(2, D, D)
    return kernel_call(
        finish_kernel, "finish", 2, [SMEM] + [VMEM] * 9, [VMEM] * 6,
        (bf16(K, D), full, full, full, full, f32(2, D)), [],
    )(core, *operands)


def shifted(shard, by):
    length = lax.axis_size(TM)
    pairs = [(i, i + by) for i in range(length) if 0 <= i + by < length]
    return lax.ppermute(shard, TM, pairs)


def exchanged(shard, axes):
    return lax.all_to_all(shard, axes, split_axis=0, concat_axis=0, tiled=True)


def swapped(shard):
    return lax.ppermute(shard, "core", [(0, 1), (1, 0)])


def spread_kernel(pieces_ref, out_ref):
    total = jnp.sum(pieces_ref[...].astype(F32), axis=0).astype(BF)
    for i in range(out_ref.shape[0]):
        out_ref[i] = total


def spread(pieces, count):
    return kernel_call(
        spread_kernel, "spread", 1, [VMEM], VMEM, bf16(count, *pieces.shape[1:]), []
    )(pieces)


def core_sum_kernel(keep_ref, arrived_ref, out_ref):
    out_ref[...] = (keep_ref[...] + arrived_ref[...].astype(F32)).astype(BF)


def core_sum(keep, send):
    return kernel_call(
        core_sum_kernel, "core_sum", 1, [VMEM] * 2, VMEM, bf16(2, D, D), []
    )(keep, swapped(send))


def both_sums_kernel(keep_ref, arrived_ref, inter_ref, out_ref):
    half = (keep_ref[...] + arrived_ref[...].astype(F32)).astype(BF)
    out_ref[:, :16] = half.reshape(32, 16, D)
    out_ref[:, 16:] = inter_ref[...].reshape(32, 16, D)


def both_sums(keep, send, inter_half):
    return kernel_call(
        both_sums_kernel, "both_sums", 1, [VMEM] * 3, VMEM, bf16(32, 32, D), []
    )(keep, swapped(send), inter_half)


def shards(frames, frames_grad, wq, wk, wv, wo, gains):
    frames = frames[0]
    core = lax.axis_index("core").astype(jnp.int32).reshape(1)
    following = shifted(frames, -1)
    front = intra_first(frames, gains, wq, wk, wv, wo)
    packed = intra_second(
        following, *front, frames, frames_grad[0], gains, wq, wk, wv, wo
    )
    across = exchanged(packed.reshape(64, 8, 384), TM).reshape(512, 384)
    grad_middle, *operands = inter(across, gains, wq, wk, wv, wo)
    grad_local = exchanged(grad_middle.reshape(64, 8, D), TM).reshape(512, D)
    inter_half = core_sum(*inter_weights(core, *operands))
    grad_local, inter_half = lax.optimization_barrier((grad_local, inter_half))
    handed = intra_prepare(frames, following, gains, wq, wk, wv)
    keep, send, *rest = intra_backward(core, grad_local, handed, wo)
    half = both_sums(keep, send, inter_half)
    first, second, carry = intra_tail(*rest, frames, following, gains, wq, wk, wv)
    carried = shifted(carry, 1)
    sent = spread(exchanged(half, PLANE), 4)
    sent, carried = lax.optimization_barrier((sent, carried))
    sent = spread(exchanged(sent, "za"), 32)
    whole = exchanged(sent, PLANE).reshape(32, 2, 16, D)
    other = swapped(whole)
    grad_frames, *weights = finish(
        core, whole, other, first, second, carried, gains, wq, wk, wv
    )
    return (grad_frames[None], *weights)


def solution(mesh):
    split = Mesh(mesh.devices.reshape(2, 2, 2, 4, 4, 2), AXES)
    placed = (P(DP, TM, None), P(DP, TM, None), P(), P(), P(), P(), P())
    return jax.shard_map(
        shards,
        mesh=split,
        in_specs=placed,
        out_specs=(P(DP, TM, None), P(), P(), P(), P(), P()),
        check_vma=False,
    )
```

```python
import math

import jax
import jax.numpy as jnp
from jax import lax
from jax.experimental import pallas as pl
from jax.experimental.pallas import tpu as pltpu
from jax.sharding import Mesh, PartitionSpec as P

HEADS = 8
HEAD = 32
D = 256
K = 256
HOP = 128
SEGMENTS = 128
EPSILON = 1e-05
SCALE = HEAD ** (-0.5)
LOG2E = math.log2(math.e)
BF = jnp.bfloat16
F32 = jnp.float32
VMEM_LIMIT = 16 * 1024 * 1024

AXES = ("yh", "core", "yl", "x", "za", "zb")
DP = ("yh", "core")
TM = ("yl", "x", "za", "zb")
PLANE = ("yh", "yl", "x", "zb")


def dot(left, right, left_dim, right_dim):
    return lax.dot_general(
        left, right, (((left_dim,), (right_dim,)), ((), ())), preferred_element_type=F32
    )


def nn(left, right):
    return dot(left, right, 1, 0)


def nt(left, right):
    return dot(left, right, 1, 1)


def tn(left, right):
    return dot(left, right, 0, 0)


def standardize(rows):
    average = jnp.mean(rows, axis=-1, keepdims=True)
    centered = rows - average
    variance = jnp.mean(centered * centered, axis=-1, keepdims=True)
    inverse = lax.rsqrt(variance + EPSILON)
    return centered * inverse, inverse


def norm_pullback(grad_normed, unit, inverse, gain):
    grad_unit = grad_normed * gain
    first = jnp.mean(grad_unit, axis=-1, keepdims=True)
    second = jnp.mean(grad_unit * unit, axis=-1, keepdims=True)
    return inverse * (grad_unit - first - unit * second)


def head_masks():
    lane = lax.broadcasted_iota(jnp.int32, (1, 128), 1)
    return [jnp.where(lane // HEAD == i, 1.0, 0.0).astype(BF) for i in range(4)]


def row_masks():
    row = lax.broadcasted_iota(jnp.int32, (128, 1), 0)
    return [jnp.where(row // HEAD == i, 1.0, 0.0).astype(BF) for i in range(4)]


def select_rows(out_rows, in_rows, source):
    out = lax.broadcasted_iota(jnp.int32, (out_rows, in_rows), 0)
    col = lax.broadcasted_iota(jnp.int32, (out_rows, in_rows), 1)
    return jnp.where(source(out) == col, 1.0, 0.0).astype(BF)


def softmax_keys(scores):
    highest = jnp.max(scores, axis=0, keepdims=True)
    powers = jnp.exp2((scores - highest) * (SCALE * LOG2E))
    return powers * (1.0 / jnp.sum(powers, axis=0, keepdims=True))


def owner_target(out):
    return ((out % 64) // 2) * 8 + (out // 64) * 2 + out % 2


def segment_target(out):
    return (out % 4) * 64 + out // 4


def packed_source(out):
    return ((out // 2) % 4) * 64 + (out // 8) * 2 + out % 2


def middle_source(out):
    return ((out % 64) // 2) * 8 + (out % 2) * 4 + out // 64


def cotangent_source(out):
    hop = out % 64
    return (hop // 2) * 8 + (out // 128) * 4 + (hop % 2) * 2 + (out // 64) % 2


def staged(count, *stages):
    held = [{} for _ in stages]
    for t in range(count + len(stages) - 1):
        for i, stage in enumerate(stages):
            step = t - i
            if 0 <= step < count:
                held[i][step] = stage(step, *([held[i - 1].pop(step)] if i else []))


def attend(keys, queries_t, values_t, ctx_ref):
    masks = head_masks()

    def scores_of(h):
        block = slice((h // 4) * 128, (h // 4) * 128 + 128)
        return nn(keys[:, block] * masks[h % 4], queries_t[block, :])

    def weigh(h, scores):
        return softmax_keys(scores).astype(BF)

    def collect(h, low):
        feats = slice(h * HEAD, h * HEAD + HEAD)
        ctx_ref[feats, :] = nn(values_t[feats, :], low).astype(BF)

    staged(HEADS, scores_of, weigh, collect)


VMEM = pl.BlockSpec(memory_space=pltpu.VMEM)
SMEM = pl.BlockSpec(memory_space=pltpu.SMEM)
HBM = pl.BlockSpec(memory_space=pltpu.HBM)


def begin(sems, *pairs):
    copies = [pltpu.make_async_copy(src, dst, sems.at[i]) for i, (src, dst) in enumerate(pairs)]
    for copy in copies:
        copy.start()
    return copies


def settle(copies):
    for copy in copies:
        copy.wait()


def bf16(*shape):
    return jax.ShapeDtypeStruct(shape, BF)


def f32(*shape):
    return jax.ShapeDtypeStruct(shape, F32)


def kernel_call(kernel, name, micros, in_specs, out_specs, out_shape, scratch, limit=VMEM_LIMIT):
    return pl.pallas_call(
        kernel,
        in_specs=in_specs,
        out_specs=out_specs,
        out_shape=out_shape,
        scratch_shapes=scratch,
        compiler_params=pltpu.CompilerParams(vmem_limit_bytes=limit),
        cost_estimate=pl.CostEstimate(
            flops=int(micros * 400e6), bytes_accessed=1 << 20, transcendentals=0
        ),
        name=name,
    )


def dma(count):
    return pltpu.SemaphoreType.DMA((count,))


def vbf(*shape):
    return pltpu.VMEM(shape, BF)


def pinned(*arrays):
    return [pltpu.with_memory_space_constraint(array, pltpu.HBM) for array in arrays]


def intra_first_kernel(
    f_any, gain_any, wq_any, wk_any, wv_any, wo_any,
    mid_ref, keys_ref, queries_ref, values_ref, w_ref, gain_ref,
    f_ref, ctx_ref, sems,
):
    copies = begin(
        sems,
        (f_any, f_ref),
        (gain_any, gain_ref),
        (wk_any.at[0], w_ref.at[1]),
        (wq_any.at[0], w_ref.at[0]),
        (wv_any.at[0], w_ref.at[2]),
        (wo_any.at[0], w_ref.at[3]),
    )
    copies[0].wait()
    rows = f_ref[...].astype(F32)
    unit, _ = standardize(rows)
    copies[1].wait()
    normed = (unit * gain_ref[0:1, :]).astype(BF)
    settle(copies[2:5])
    keys = nn(normed, w_ref[1]).astype(BF)
    queries_t = nt(w_ref[0].T, normed).astype(BF)
    values_t = nt(w_ref[2].T, normed).astype(BF)
    attend(keys, queries_t, values_t, ctx_ref)
    copies[5].wait()
    mid_ref[...] = (rows + tn(ctx_ref[...], w_ref[3])).astype(BF)
    keys_ref[...] = keys[HOP:]
    queries_ref[...] = queries_t[:, HOP:]
    values_ref[...] = values_t[:, HOP:]


def intra_second_kernel(
    n_ref, mid_in_ref, keys_ref, queries_ref, values_ref, w_ref, gain_ref, f_any, grad_any, packed_ref,
    f_ref, grad_ref, ctx_ref, sems,
):
    copies = begin(sems, (f_any.at[pl.ds(HOP, HOP)], f_ref), (grad_any, grad_ref))
    rows = n_ref[:HOP].astype(F32)
    unit, _ = standardize(rows)
    normed = (unit * gain_ref[0:1, :]).astype(BF)
    keys = jnp.concatenate([keys_ref[...], nn(normed, w_ref[1]).astype(BF)], axis=0)
    queries_t = jnp.concatenate(
        [queries_ref[...], nt(w_ref[0].T, normed).astype(BF)], axis=1
    )
    values_t = jnp.concatenate([values_ref[...], nt(w_ref[2].T, normed).astype(BF)], axis=1)
    attend(keys, queries_t, values_t, ctx_ref)
    settle(copies)
    rows = jnp.concatenate([f_ref[...].astype(F32), rows], axis=0)
    mids = (mid_in_ref[...], (rows + tn(ctx_ref[...], w_ref[3])).astype(BF))
    grads = grad_ref[...]
    pick = select_rows(256, 256, packed_source)
    for t in range(2):
        parts = []
        for part in range(4):
            high, low = part // 2, part % 2
            at = slice(low * HOP + 64 * t, low * HOP + 64 * t + 64)
            parts.append(
                jnp.concatenate([mids[high][at], grads[at, 128 * high : 128 * high + 128]], axis=1)
            )
        rows = jnp.concatenate(parts, axis=0)
        packed_ref[256 * t : 256 * t + 256, :] = nn(pick, rows).astype(BF)


def intra_first(*operands):
    return kernel_call(
        intra_first_kernel, "intra_first", 3, [HBM] * 6, [VMEM] * 6,
        (bf16(K, D), bf16(HOP, D), bf16(D, HOP), bf16(D, HOP), bf16(4, D, D), f32(2, D)),
        [vbf(K, D), vbf(D, K), dma(6)],
    )(*pinned(*operands))


def intra_second(following, frames, grads, *front):
    return kernel_call(
        intra_second_kernel, "intra_second", 3, [VMEM] * 7 + [HBM] * 2, VMEM, bf16(512, 384),
        [vbf(HOP, D), vbf(K, D), vbf(D, K), dma(2)],
    )(following, *front, *pinned(frames, grads))


def inter_kernel(
    packed_ref, gain_ref, wq_ref, wk_ref, wv_ref, wo_ref,
    out_ref, normed_t_ref, grads_ref, ctx_t, gq_t, gk_ref, gv_ref,
):
    gain = gain_ref[1:2, :]
    pick = select_rows(256, 256, middle_source)
    tiles = [nn(pick, packed_ref[256 * t : 256 * t + 256, :D]) for t in range(2)]
    rows = jnp.concatenate(
        [tiles[t][64 * p : 64 * p + 64] for p in range(4) for t in range(2)], axis=0
    )
    pick = select_rows(256, 256, cotangent_source)
    tiles = [nn(pick, packed_ref[256 * t : 256 * t + 256, D:]) for t in range(2)]
    hops = [
        jnp.concatenate(
            [
                jnp.concatenate(
                    [tiles[t][128 * c + 64 * r : 128 * c + 64 * r + 64] for c in range(2)], axis=1
                )
                for t in range(2)
            ],
            axis=0,
        )
        for r in range(2)
    ]
    last = jnp.zeros((1, D), F32)
    late = [jnp.concatenate([hop[1:], last], axis=0) for hop in hops]
    grads = jnp.concatenate(hops + late, axis=0).astype(BF)
    grads_ref[...] = grads
    unit, inverse = standardize(rows)
    normed = (unit * gain).astype(BF)
    normed_t_ref[...] = normed.T
    wq, wk, wv, wo = wq_ref[1], wk_ref[1], wv_ref[1], wo_ref[1]
    queries = nn(normed, wq).astype(BF)
    keys = nn(normed, wk).astype(BF)
    values = nn(normed, wv).astype(BF)
    grad_context = nt(grads, wo).astype(BF)
    queries_t = queries.T
    keys_t = keys.T
    values_t = values.T
    grad_context_t = grad_context.T
    masks = head_masks()
    downs = row_masks()

    def place(step):
        p, b, pair = step // 4, (step // 2) % 2, step % 2
        return slice(128 * p, 128 * p + 128), slice(128 * b, 128 * b + 128), pair

    def columns(rows_t, pair):
        return jnp.concatenate([rows_t * downs[2 * pair], rows_t * downs[2 * pair + 1]], axis=1)

    def stacked(rows, pair):
        return jnp.concatenate([rows * masks[2 * pair], rows * masks[2 * pair + 1]], axis=0)

    def products(step):
        at, block, pair = place(step)
        scores = nn(keys[at, block], columns(queries_t[block, at], pair))
        grad_probs = nn(values[at, block], columns(grad_context_t[block, at], pair))
        return scores, grad_probs

    def weigh(step, held):
        scores, grad_probs = held
        probs = softmax_keys(scores)
        inner = jnp.sum(grad_probs * probs, axis=0, keepdims=True)
        return probs.astype(BF), (probs * (grad_probs - inner) * SCALE).astype(BF)

    sums = {}

    def collect(step, held):
        low, grad_scores = held
        at, block, pair = place(step)
        gv = nn(low, stacked(grad_context[at, block], pair))
        gk = nn(grad_scores, stacked(queries[at, block], pair))
        if pair == 0:
            sums["v"], sums["k"] = gv, gk
        else:
            gv_ref[at, block] = (sums["v"] + gv).astype(BF)
            gk_ref[at, block] = (sums["k"] + gk).astype(BF)
        start = block.start + 64 * pair
        for target, rows_t, right in ((ctx_t, values_t, low), (gq_t, keys_t, grad_scores)):
            both = nn(rows_t[start : start + 64, at], right)
            target[start : start + 32, at] = both[:32, :128].astype(BF)
            target[start + 32 : start + 64, at] = both[32:, 128:].astype(BF)

    staged(16, products, weigh, collect)
    gqt, gk, gv = gq_t[...], gk_ref[...], gv_ref[...]
    grad_normed = nt(gqt.T, wq) + nt(gk, wk) + nt(gv, wv)
    result = (grads.astype(F32) + norm_pullback(grad_normed, unit, inverse, gain)).astype(BF)
    back = select_rows(256, 256, segment_target)
    for t in range(2):
        part = jnp.concatenate(
            [result[128 * p + 64 * t : 128 * p + 64 * t + 64] for p in range(4)], axis=0
        )
        out_ref[256 * t : 256 * t + 256, :] = nn(back, part).astype(BF)


def inter(packed, gains, wq, wk, wv, wo):
    return kernel_call(
        inter_kernel, "inter", 5, [VMEM] * 6, [VMEM] * 7,
        (
            bf16(512, D), bf16(D, 512), bf16(512, D), bf16(D, 512), bf16(D, 512), bf16(512, D),
            bf16(512, D),
        ),
        [],
    )(packed, gains, wq, wk, wv, wo)


def split_by_core(core_ref, weights, keep_ref, send_ref):
    low_core = core_ref[0] == 0
    for i in range(2):
        keep_ref[i] = jnp.where(low_core, weights[i], weights[2 + i])
        send_ref[i] = jnp.where(low_core, weights[2 + i], weights[i]).astype(BF)


def inter_weights_kernel(
    core_ref, normed_t_ref, grads_ref, ctx_t_ref, gq_t_ref, gk_ref, gv_ref, keep_ref, send_ref
):
    normed_t = normed_t_ref[...]
    weights = (
        nt(normed_t, gq_t_ref[...]),
        nn(normed_t, gk_ref[...]),
        nn(normed_t, gv_ref[...]),
        nn(ctx_t_ref[...], grads_ref[...]),
    )
    split_by_core(core_ref, weights, keep_ref, send_ref)


def inter_weights(core, *operands):
    return kernel_call(
        inter_weights_kernel, "inter_weights", 1, [SMEM] + [VMEM] * 6, [VMEM] * 2,
        (f32(2, D, D), bf16(2, D, D)), [],
    )(core, *operands)


KEYS, QUERIES_T, VALUES, STATS = 0, 768, 1536, 2304
QUERIES, KEYS_T, NORMED_T, CONTEXT = 2496, 3264, 4032, 4800
HANDED_ROWS = 5824


def put_stats(handed_ref, stats):
    for i in range(3):
        part = stats.astype(BF)
        stats = stats - part.astype(F32)
        put_blocks(handed_ref, STATS + 64 * i, part)


def stats_of(handed_ref):
    parts = [
        jnp.concatenate(
            [
                handed_ref[STATS + 64 * i + 32 * j : STATS + 64 * i + 32 * j + 32, :].astype(F32)
                for j in range(2)
            ],
            axis=1,
        )
        for i in range(3)
    ]
    return parts[0] + parts[1] + parts[2]


def put_blocks(handed_ref, start, array):
    for i in range(array.shape[1] // 128):
        at = start + i * array.shape[0]
        handed_ref[at : at + array.shape[0], :] = array[:, 128 * i : 128 * i + 128]


def features_of(handed_ref, start, rows, at):
    return jnp.concatenate(
        [
            handed_ref[start + 256 * i + rows.start : start + 256 * i + rows.stop, :]
            for i in range(at.start // 128, at.stop // 128)
        ],
        axis=1,
    )


def tokens_of(handed_ref, start, at, b):
    return handed_ref[start + 384 * b + at.start : start + 384 * b + at.stop, :]


def begin_layer(sems, f_any, n_any, gain_any, wq_any, wk_any, wv_any, rows_ref, gain_ref, w_ref):
    return begin(
        sems,
        (f_any, rows_ref.at[pl.ds(0, K)]),
        (n_any.at[pl.ds(0, HOP)], rows_ref.at[pl.ds(K, HOP)]),
        (gain_any, gain_ref),
        (wq_any.at[0], w_ref.at[0]),
        (wk_any.at[0], w_ref.at[1]),
        (wv_any.at[0], w_ref.at[2]),
    )


def layer_scratch():
    return [vbf(3 * HOP, D), pltpu.VMEM((2, D), F32), vbf(3, D, D)]


def intra_prepare_kernel(
    f_ref, n_ref, gain_ref, wq_ref, wk_ref, wv_ref, handed_ref, stats_ref, ctx_ref
):
    rows = jnp.concatenate([f_ref[...], n_ref[:HOP]], axis=0)
    unit, _ = standardize(rows.astype(F32))
    normed = (unit * gain_ref[0:1, :]).astype(BF)
    queries = nn(normed, wq_ref[0]).astype(BF)
    keys = nn(normed, wk_ref[0]).astype(BF)
    values = nn(normed, wv_ref[0]).astype(BF)
    queries_t = queries.T
    values_t = values.T
    put_blocks(handed_ref, NORMED_T, normed.T)
    put_blocks(handed_ref, QUERIES, queries)
    put_blocks(handed_ref, QUERIES_T, queries_t)
    put_blocks(handed_ref, KEYS, keys)
    put_blocks(handed_ref, KEYS_T, keys.T)
    put_blocks(handed_ref, VALUES, values)
    masks = head_masks()

    def scores_of(step):
        g, h = step // HEADS, step % HEADS
        at = slice(g * HOP, g * HOP + K)
        block = slice((h // 4) * 128, (h // 4) * 128 + 128)
        return nn(keys[at, block] * masks[h % 4], queries_t[block, at])

    def weigh(step, scores):
        highest = jnp.max(scores, axis=0, keepdims=True)
        powers = jnp.exp2((scores - highest) * (SCALE * LOG2E))
        inverse = 1.0 / jnp.sum(powers, axis=0, keepdims=True)
        stats_ref[2 * step : 2 * step + 1, :] = highest
        stats_ref[2 * step + 1 : 2 * step + 2, :] = inverse
        return (powers * inverse).astype(BF)

    def collect(step, low):
        g, h = step // HEADS, step % HEADS
        feats = slice(h * HEAD, h * HEAD + HEAD)
        ctx_ref[g, feats, :] = nn(values_t[feats, g * HOP : g * HOP + K], low).astype(BF)

    staged(2 * HEADS, scores_of, weigh, collect)
    for g in range(2):
        put_blocks(handed_ref, CONTEXT + 512 * g, ctx_ref[g])
    put_stats(handed_ref, stats_ref[...])


def intra_prepare(frames, following, gains, wq, wk, wv):
    return kernel_call(
        intra_prepare_kernel, "intra_prepare", 3, [VMEM] * 6, VMEM, bf16(HANDED_ROWS, 128),
        [pltpu.VMEM((4 * HEADS, K), F32), vbf(2, D, K)],
    )(frames, following, gains, wq, wk, wv)


def intra_backward_kernel(
    core_ref, m_ref, handed_any, wo_any,
    keep_ref, send_ref, grads_ref, gq_t, gk_ref, gv_ref,
    handed_ref, stats_ref, wo_ref, sems,
):
    cuts = (KEYS, QUERIES, NORMED_T, HANDED_ROWS)
    spans = [pl.ds(start, end - start) for start, end in zip(cuts, cuts[1:])]
    copies = begin(
        sems,
        (wo_any.at[0], wo_ref),
        *[(handed_any.at[span], handed_ref.at[span]) for span in spans],
    )
    pick = select_rows(256, 256, owner_target)
    tiles = [nn(pick, m_ref[256 * t : 256 * t + 256, :]).astype(BF) for t in range(2)]
    masks = head_masks()
    context, context_t = [], []
    for g in range(2):
        grads_ref[g] = jnp.concatenate(
            [tiles[t][128 * g + 64 * h : 128 * g + 64 * h + 64] for h in range(2) for t in range(2)],
            axis=0,
        )
        if g == 0:
            copies[0].wait()
        context.append(nt(grads_ref[g], wo_ref[...]).astype(BF))
        context_t.append(context[g].T)

    copies[1].wait()
    stats_ref[...] = stats_of(handed_ref)

    def place(step):
        g, h = step // HEADS, step % HEADS
        return g, slice(g * HOP, g * HOP + K), h // 4, h % 4

    def products(step):
        g, at, b, i = place(step)
        block = slice(128 * b, 128 * b + 128)
        keys = tokens_of(handed_ref, KEYS, at, b) * masks[i]
        scores = nn(keys, features_of(handed_ref, QUERIES_T, block, at))
        values = tokens_of(handed_ref, VALUES, at, b) * masks[i]
        return scores, nn(values, context_t[g][block, :])

    def weigh(step, held):
        scores, grad_probs = held
        powers = jnp.exp2((scores - stats_ref[2 * step : 2 * step + 1, :]) * (SCALE * LOG2E))
        probs = powers * stats_ref[2 * step + 1 : 2 * step + 2, :]
        inner = jnp.sum(grad_probs * probs, axis=0, keepdims=True)
        return probs.astype(BF), (probs * (grad_probs - inner) * SCALE).astype(BF)

    sums = {}

    def collect(step, held):
        if step == 0:
            copies[2].wait()
        low, grad_scores = held
        g, at, b, i = place(step)
        block = slice(128 * b, 128 * b + 128)
        feats = slice(128 * b + HEAD * i, 128 * b + HEAD * i + HEAD)
        gv = nn(low, context[g][:, block] * masks[i])
        gk = nn(grad_scores, tokens_of(handed_ref, QUERIES, at, b) * masks[i])
        keys_t = features_of(handed_ref, KEYS_T, feats, at)
        gq_t[g, feats, :] = nn(keys_t, grad_scores).astype(BF)
        sums["v"] = gv if i == 0 else sums["v"] + gv
        sums["k"] = gk if i == 0 else sums["k"] + gk
        if i == 3:
            gv_ref[g, :, block] = sums["v"].astype(BF)
            gk_ref[g, :, block] = sums["k"].astype(BF)

    staged(2 * HEADS, products, weigh, collect)
    copies[3].wait()
    parts = []
    for g in range(2):
        normed_t = features_of(
            handed_ref, NORMED_T, slice(0, D), slice(g * HOP, g * HOP + K)
        )
        context_0 = jnp.concatenate(
            [handed_ref[pl.ds(CONTEXT + 512 * g + 256 * i, 256), :] for i in range(2)], axis=1
        )
        parts.append(
            (
                nt(normed_t, gq_t[g]),
                nn(normed_t, gk_ref[g]),
                nn(normed_t, gv_ref[g]),
                nn(context_0, grads_ref[g]),
            )
        )
    totals = [first + second for first, second in zip(*parts)]
    split_by_core(core_ref, totals, keep_ref, send_ref)


def intra_backward(core, grads, *rest):
    return kernel_call(
        intra_backward_kernel, "intra_backward", 4, [SMEM, VMEM] + [HBM] * 2, [VMEM] * 6,
        (
            f32(2, D, D), bf16(2, D, D), bf16(2, K, D), bf16(2, D, K), bf16(2, K, D), bf16(2, K, D),
        ),
        [vbf(HANDED_ROWS, 128), pltpu.VMEM((4 * HEADS, K), F32), vbf(D, D), dma(4)],
    )(core, grads, *pinned(*rest))


def intra_tail_kernel(
    grads_any, gq_t_any, gk_any, gv_any, f_any, n_any, gain_any, wq_any, wk_any, wv_any,
    first_ref, second_ref, carry_ref,
    grads_ref, gq_t_ref, gk_ref, gv_ref, rows_ref, gain_ref, w_ref, sems, own_sems,
):
    copies = begin_layer(sems, f_any, n_any, gain_any, wq_any, wk_any, wv_any, rows_ref, gain_ref, w_ref)
    copies += begin(
        own_sems,
        (grads_any, grads_ref), (gq_t_any, gq_t_ref), (gk_any, gk_ref), (gv_any, gv_ref),
    )
    settle(copies)
    unit, inverse = standardize(rows_ref[...].astype(F32))
    halves = []
    for g in range(2):
        at = slice(g * HOP, g * HOP + K)
        grad_normed = (
            nt(gq_t_ref[g].T, w_ref[0]) + nt(gk_ref[g], w_ref[1]) + nt(gv_ref[g], w_ref[2])
        )
        pulled = norm_pullback(grad_normed, unit[at], inverse[at], gain_ref[0:1, :])
        result = (grads_ref[g].astype(F32) + pulled).astype(BF)
        halves.append((result[:HOP], result[HOP:]))
    first_ref[...] = halves[0][0]
    second_ref[...] = (halves[1][0].astype(F32) + halves[0][1].astype(F32)).astype(BF)
    carry_ref[...] = halves[1][1]


def intra_tail(*operands):
    return kernel_call(
        intra_tail_kernel, "intra_tail", 2, [HBM] * 10, [VMEM] * 3,
        (bf16(HOP, D), bf16(HOP, D), bf16(HOP, D)),
        [vbf(2, K, D), vbf(2, D, K), vbf(2, K, D), vbf(2, K, D)]
        + layer_scratch()
        + [dma(6), dma(4)],
    )(*operands)


def finish_kernel(
    core_ref, mine_ref, other_ref, first_ref, second_ref, carried_ref, gain_ref, wq_ref, wk_ref, wv_ref,
    frames_ref, dq_ref, dk_ref, dv_ref, do_ref, dg_ref,
):
    frames_ref[:HOP] = (first_ref[...].astype(F32) + carried_ref[...].astype(F32)).astype(BF)
    frames_ref[HOP:] = second_ref[...]
    low_core = core_ref[0] == 0
    for layer in range(2):
        mine = mine_ref[:, layer].reshape(2, D, D).astype(F32)
        other = other_ref[:, layer].reshape(2, D, D).astype(F32)
        dq = jnp.where(low_core, mine[0], other[0])
        dk = jnp.where(low_core, mine[1], other[1])
        dv = jnp.where(low_core, other[0], mine[0])
        dq_ref[layer] = dq
        dk_ref[layer] = dk
        dv_ref[layer] = dv
        do_ref[layer] = jnp.where(low_core, other[1], mine[1])
        through = (
            dq * wq_ref[layer].astype(F32)
            + dk * wk_ref[layer].astype(F32)
            + dv * wv_ref[layer].astype(F32)
        )
        column = jnp.sum(through.T, axis=0, keepdims=True)
        dg_ref[layer : layer + 1, :] = column / gain_ref[layer : layer + 1, :]


def finish(core, *operands):
    full = f32(2, D, D)
    return kernel_call(
        finish_kernel, "finish", 2, [SMEM] + [VMEM] * 9, [VMEM] * 6,
        (bf16(K, D), full, full, full, full, f32(2, D)), [],
    )(core, *operands)


def shifted(shard, by):
    length = lax.axis_size(TM)
    pairs = [(i, i + by) for i in range(length) if 0 <= i + by < length]
    return lax.ppermute(shard, TM, pairs)


def exchanged(shard, axes):
    return lax.all_to_all(shard, axes, split_axis=0, concat_axis=0, tiled=True)


def swapped(shard):
    return lax.ppermute(shard, "core", [(0, 1), (1, 0)])


def spread_kernel(pieces_ref, out_ref):
    total = jnp.sum(pieces_ref[...].astype(F32), axis=0).astype(BF)
    for i in range(out_ref.shape[0]):
        out_ref[i] = total


def spread(pieces, count):
    return kernel_call(
        spread_kernel, "spread", 1, [VMEM], VMEM, bf16(count, *pieces.shape[1:]), []
    )(pieces)


def core_sum_kernel(keep_ref, arrived_ref, out_ref):
    out_ref[...] = (keep_ref[...] + arrived_ref[...].astype(F32)).astype(BF)


def core_sum(keep, send):
    return kernel_call(
        core_sum_kernel, "core_sum", 1, [VMEM] * 2, VMEM, bf16(2, D, D), []
    )(keep, swapped(send))


def both_sums_kernel(keep_ref, arrived_ref, inter_ref, out_ref):
    half = (keep_ref[...] + arrived_ref[...].astype(F32)).astype(BF)
    out_ref[:, :16] = half.reshape(32, 16, D)
    out_ref[:, 16:] = inter_ref[...].reshape(32, 16, D)


def both_sums(keep, send, inter_half):
    return kernel_call(
        both_sums_kernel, "both_sums", 1, [VMEM] * 3, VMEM, bf16(32, 32, D), []
    )(keep, swapped(send), inter_half)


def shards(frames, frames_grad, wq, wk, wv, wo, gains):
    frames = frames[0]
    core = lax.axis_index("core").astype(jnp.int32).reshape(1)
    following = shifted(frames, -1)
    front = intra_first(frames, gains, wq, wk, wv, wo)
    packed = intra_second(following, frames, frames_grad[0], *front)
    across = exchanged(packed.reshape(64, 8, 384), TM).reshape(512, 384)
    grad_middle, *operands = inter(across, gains, wq, wk, wv, wo)
    grad_local = exchanged(grad_middle.reshape(64, 8, D), TM).reshape(512, D)
    inter_half = core_sum(*inter_weights(core, *operands))
    grad_local, inter_half = lax.optimization_barrier((grad_local, inter_half))
    handed = intra_prepare(frames, following, gains, wq, wk, wv)
    keep, send, *rest = intra_backward(core, grad_local, handed, wo)
    half = both_sums(keep, send, inter_half)
    first, second, carry = intra_tail(*rest, frames, following, gains, wq, wk, wv)
    carried = shifted(carry, 1)
    sent = spread(exchanged(half, PLANE), 4)
    sent, carried = lax.optimization_barrier((sent, carried))
    sent = spread(exchanged(sent, "za"), 32)
    whole = exchanged(sent, PLANE).reshape(32, 2, 16, D)
    other = swapped(whole)
    grad_frames, *weights = finish(
        core, whole, other, first, second, carried, gains, wq, wk, wv
    )
    return (grad_frames[None], *weights)


def solution(mesh):
    split = Mesh(mesh.devices.reshape(2, 2, 2, 4, 4, 2), AXES)
    placed = (P(DP, TM, None), P(DP, TM, None), P(), P(), P(), P(), P())
    return jax.shard_map(
        shards,
        mesh=split,
        in_specs=placed,
        out_specs=(P(DP, TM, None), P(), P(), P(), P(), P()),
        check_vma=False,
    )
```

```python
import math

import jax
import jax.numpy as jnp
from jax import lax
from jax.experimental import pallas as pl
from jax.experimental.pallas import tpu as pltpu
from jax.sharding import Mesh, PartitionSpec as P

HEADS = 8
HEAD = 32
D = 256
K = 256
HOP = 128
SEGMENTS = 128
EPSILON = 1e-05
SCALE = HEAD ** (-0.5)
LOG2E = math.log2(math.e)
BF = jnp.bfloat16
F32 = jnp.float32
VMEM_LIMIT = 16 * 1024 * 1024

AXES = ("yh", "core", "yl", "x", "za", "zb")
DP = ("yh", "core")
TM = ("yl", "x", "za", "zb")
PLANE = ("yh", "yl", "x", "zb")


def dot(left, right, left_dim, right_dim):
    return lax.dot_general(
        left, right, (((left_dim,), (right_dim,)), ((), ())), preferred_element_type=F32
    )


def nn(left, right):
    return dot(left, right, 1, 0)


def nt(left, right):
    return dot(left, right, 1, 1)


def tn(left, right):
    return dot(left, right, 0, 0)


def standardize(rows):
    average = jnp.mean(rows, axis=-1, keepdims=True)
    centered = rows - average
    variance = jnp.mean(centered * centered, axis=-1, keepdims=True)
    inverse = lax.rsqrt(variance + EPSILON)
    return centered * inverse, inverse


def norm_pullback(grad_normed, unit, inverse, gain):
    grad_unit = grad_normed * gain
    first = jnp.mean(grad_unit, axis=-1, keepdims=True)
    second = jnp.mean(grad_unit * unit, axis=-1, keepdims=True)
    return inverse * (grad_unit - first - unit * second)


def head_masks():
    lane = lax.broadcasted_iota(jnp.int32, (1, 128), 1)
    return [jnp.where(lane // HEAD == i, 1.0, 0.0).astype(BF) for i in range(4)]


def row_masks():
    row = lax.broadcasted_iota(jnp.int32, (128, 1), 0)
    return [jnp.where(row // HEAD == i, 1.0, 0.0).astype(BF) for i in range(4)]


def select_rows(out_rows, in_rows, source):
    out = lax.broadcasted_iota(jnp.int32, (out_rows, in_rows), 0)
    col = lax.broadcasted_iota(jnp.int32, (out_rows, in_rows), 1)
    return jnp.where(source(out) == col, 1.0, 0.0).astype(BF)


def softmax_keys(scores):
    highest = jnp.max(scores, axis=0, keepdims=True)
    powers = jnp.exp2((scores - highest) * (SCALE * LOG2E))
    return powers * (1.0 / jnp.sum(powers, axis=0, keepdims=True))


def owner_target(out):
    return ((out % 64) // 2) * 8 + (out // 64) * 2 + out % 2


def segment_target(out):
    return (out % 4) * 64 + out // 4


def packed_source(out):
    return ((out // 2) % 4) * 64 + (out // 8) * 2 + out % 2


def middle_source(out):
    return ((out % 64) // 2) * 8 + (out % 2) * 4 + out // 64


def cotangent_source(out):
    hop = out % 64
    return (hop // 2) * 8 + (out // 128) * 4 + (hop % 2) * 2 + (out // 64) % 2


def staged(count, *stages):
    held = [{} for _ in stages]
    for t in range(count + len(stages) - 1):
        for i, stage in enumerate(stages):
            step = t - i
            if 0 <= step < count:
                held[i][step] = stage(step, *([held[i - 1].pop(step)] if i else []))


def attend(keys, queries_t, values_t, ctx_ref, ahead):

    def scores_of(h):
        feats = slice(h * HEAD, h * HEAD + HEAD)
        return nn(keys[:, feats], queries_t[feats, :])

    def weigh(h, scores):
        return softmax_keys(scores).astype(BF)

    def collect(h, low):
        feats = slice(h * HEAD, h * HEAD + HEAD)
        ctx_ref[feats, :] = nn(values_t[feats, :], low).astype(BF)

    waiting = [lambda h, scores: scores] * ahead
    staged(HEADS, scores_of, *waiting, weigh, collect)


VMEM = pl.BlockSpec(memory_space=pltpu.VMEM)
SMEM = pl.BlockSpec(memory_space=pltpu.SMEM)
HBM = pl.BlockSpec(memory_space=pltpu.HBM)


def begin(sems, *pairs):
    copies = [pltpu.make_async_copy(src, dst, sems.at[i]) for i, (src, dst) in enumerate(pairs)]
    for copy in copies:
        copy.start()
    return copies


def settle(copies):
    for copy in copies:
        copy.wait()


def bf16(*shape):
    return jax.ShapeDtypeStruct(shape, BF)


def f32(*shape):
    return jax.ShapeDtypeStruct(shape, F32)


def kernel_call(kernel, name, micros, in_specs, out_specs, out_shape, scratch, limit=VMEM_LIMIT):
    return pl.pallas_call(
        kernel,
        in_specs=in_specs,
        out_specs=out_specs,
        out_shape=out_shape,
        scratch_shapes=scratch,
        compiler_params=pltpu.CompilerParams(vmem_limit_bytes=limit),
        cost_estimate=pl.CostEstimate(
            flops=int(micros * 400e6), bytes_accessed=1 << 20, transcendentals=0
        ),
        name=name,
    )


def dma(count):
    return pltpu.SemaphoreType.DMA((count,))


def vbf(*shape):
    return pltpu.VMEM(shape, BF)


def pinned(*arrays):
    return [pltpu.with_memory_space_constraint(array, pltpu.HBM) for array in arrays]


def intra_first_kernel(
    f_any, gain_any, wq_any, wk_any, wv_any, wo_any,
    mid_ref, keys_ref, queries_ref, values_ref, w_ref, gain_ref,
    f_ref, ctx_ref, sems,
):
    copies = begin(
        sems,
        (f_any, f_ref),
        (gain_any, gain_ref),
        (wk_any.at[0], w_ref.at[1]),
        (wq_any.at[0], w_ref.at[0]),
        (wv_any.at[0], w_ref.at[2]),
        (wo_any.at[0], w_ref.at[3]),
    )
    copies[0].wait()
    rows = f_ref[...].astype(F32)
    unit, _ = standardize(rows)
    copies[1].wait()
    normed = (unit * gain_ref[0:1, :]).astype(BF)
    settle(copies[2:5])
    keys = nn(normed, w_ref[1]).astype(BF)
    queries_t = nt(w_ref[0].T, normed).astype(BF)
    values_t = nt(w_ref[2].T, normed).astype(BF)
    attend(keys, queries_t, values_t, ctx_ref, 1)
    copies[5].wait()
    mid_ref[...] = (rows + tn(ctx_ref[...], w_ref[3])).astype(BF)
    keys_ref[...] = keys[HOP:]
    queries_ref[...] = queries_t[:, HOP:]
    values_ref[...] = values_t[:, HOP:]


def intra_second_kernel(
    n_ref, mid_in_ref, keys_ref, queries_ref, values_ref, w_ref, gain_ref, f_any, grad_any, packed_ref,
    f_ref, grad_ref, ctx_ref, sems,
):
    copies = begin(sems, (f_any.at[pl.ds(HOP, HOP)], f_ref), (grad_any, grad_ref))
    rows = n_ref[:HOP].astype(F32)
    unit, _ = standardize(rows)
    normed = (unit * gain_ref[0:1, :]).astype(BF)
    keys = jnp.concatenate([keys_ref[...], nn(normed, w_ref[1]).astype(BF)], axis=0)
    queries_t = jnp.concatenate(
        [queries_ref[...], nt(w_ref[0].T, normed).astype(BF)], axis=1
    )
    values_t = jnp.concatenate([values_ref[...], nt(w_ref[2].T, normed).astype(BF)], axis=1)
    attend(keys, queries_t, values_t, ctx_ref, 0)
    settle(copies)
    rows = jnp.concatenate([f_ref[...].astype(F32), rows], axis=0)
    mids = (mid_in_ref[...], (rows + tn(ctx_ref[...], w_ref[3])).astype(BF))
    grads = grad_ref[...]
    pick = select_rows(256, 256, packed_source)
    for t in range(2):
        parts = []
        for part in range(4):
            high, low = part // 2, part % 2
            at = slice(low * HOP + 64 * t, low * HOP + 64 * t + 64)
            parts.append(
                jnp.concatenate([mids[high][at], grads[at, 128 * high : 128 * high + 128]], axis=1)
            )
        rows = jnp.concatenate(parts, axis=0)
        packed_ref[256 * t : 256 * t + 256, :] = nn(pick, rows).astype(BF)


def intra_first(*operands):
    return kernel_call(
        intra_first_kernel, "intra_first", 3, [HBM] * 6, [VMEM] * 6,
        (bf16(K, D), bf16(HOP, D), bf16(D, HOP), bf16(D, HOP), bf16(4, D, D), f32(2, D)),
        [vbf(K, D), vbf(D, K), dma(6)],
    )(*pinned(*operands))


def intra_second(following, frames, grads, *front):
    return kernel_call(
        intra_second_kernel, "intra_second", 3, [VMEM] * 7 + [HBM] * 2, VMEM, bf16(512, 384),
        [vbf(HOP, D), vbf(K, D), vbf(D, K), dma(2)],
    )(following, *front, *pinned(frames, grads))


def inter_kernel(
    packed_ref, gain_ref, wq_ref, wk_ref, wv_ref, wo_ref,
    out_ref, normed_t_ref, grads_ref, ctx_t, gq_t, gk_ref, gv_ref,
):
    gain = gain_ref[1:2, :]
    pick = select_rows(256, 256, middle_source)
    tiles = [nn(pick, packed_ref[256 * t : 256 * t + 256, :D]) for t in range(2)]
    rows = jnp.concatenate(
        [tiles[t][64 * p : 64 * p + 64] for p in range(4) for t in range(2)], axis=0
    )
    pick = select_rows(256, 256, cotangent_source)
    tiles = [nn(pick, packed_ref[256 * t : 256 * t + 256, D:]) for t in range(2)]
    hops = [
        jnp.concatenate(
            [
                jnp.concatenate(
                    [tiles[t][128 * c + 64 * r : 128 * c + 64 * r + 64] for c in range(2)], axis=1
                )
                for t in range(2)
            ],
            axis=0,
        )
        for r in range(2)
    ]
    last = jnp.zeros((1, D), F32)
    late = [jnp.concatenate([hop[1:], last], axis=0) for hop in hops]
    grads = jnp.concatenate(hops + late, axis=0).astype(BF)
    grads_ref[...] = grads
    unit, inverse = standardize(rows)
    normed = (unit * gain).astype(BF)
    normed_t_ref[...] = normed.T
    wq, wk, wv, wo = wq_ref[1], wk_ref[1], wv_ref[1], wo_ref[1]
    queries = nn(normed, wq).astype(BF)
    keys = nn(normed, wk).astype(BF)
    values = nn(normed, wv).astype(BF)
    grad_context = nt(grads, wo).astype(BF)
    queries_t = queries.T
    keys_t = keys.T
    values_t = values.T
    grad_context_t = grad_context.T
    masks = head_masks()
    downs = row_masks()

    def place(step):
        p, b, pair = step // 4, (step // 2) % 2, step % 2
        return slice(128 * p, 128 * p + 128), slice(128 * b, 128 * b + 128), pair

    def columns(rows_t, pair):
        return jnp.concatenate([rows_t * downs[2 * pair], rows_t * downs[2 * pair + 1]], axis=1)

    def stacked(rows, pair):
        return jnp.concatenate([rows * masks[2 * pair], rows * masks[2 * pair + 1]], axis=0)

    def products(step):
        at, block, pair = place(step)
        scores = nn(keys[at, block], columns(queries_t[block, at], pair))
        grad_probs = nn(values[at, block], columns(grad_context_t[block, at], pair))
        return scores, grad_probs

    def weigh(step, held):
        scores, grad_probs = held
        return softmax_keys(scores), grad_probs

    def weigh_rest(step, held):
        probs, grad_probs = held
        inner = jnp.sum(grad_probs * probs, axis=0, keepdims=True)
        return probs.astype(BF), (probs * (grad_probs - inner) * SCALE).astype(BF)

    sums = {}

    def collect(step, held):
        low, grad_scores = held
        at, block, pair = place(step)
        gv = nn(low, stacked(grad_context[at, block], pair))
        gk = nn(grad_scores, stacked(queries[at, block], pair))
        if pair == 0:
            sums["v"], sums["k"] = gv, gk
        else:
            gv_ref[at, block] = (sums["v"] + gv).astype(BF)
            gk_ref[at, block] = (sums["k"] + gk).astype(BF)
        start = block.start + 64 * pair
        for target, rows_t, right in ((ctx_t, values_t, low), (gq_t, keys_t, grad_scores)):
            both = nn(rows_t[start : start + 64, at], right)
            target[start : start + 32, at] = both[:32, :128].astype(BF)
            target[start + 32 : start + 64, at] = both[32:, 128:].astype(BF)

    staged(16, products, weigh, weigh_rest, collect)
    gqt, gk, gv = gq_t[...], gk_ref[...], gv_ref[...]
    grad_normed = nt(gqt.T, wq) + nt(gk, wk) + nt(gv, wv)
    result = (grads.astype(F32) + norm_pullback(grad_normed, unit, inverse, gain)).astype(BF)
    back = select_rows(256, 256, segment_target)
    for t in range(2):
        part = jnp.concatenate(
            [result[128 * p + 64 * t : 128 * p + 64 * t + 64] for p in range(4)], axis=0
        )
        out_ref[256 * t : 256 * t + 256, :] = nn(back, part).astype(BF)


def inter(packed, gains, wq, wk, wv, wo):
    return kernel_call(
        inter_kernel, "inter", 5, [VMEM] * 6, [VMEM] * 7,
        (
            bf16(512, D), bf16(D, 512), bf16(512, D), bf16(D, 512), bf16(D, 512), bf16(512, D),
            bf16(512, D),
        ),
        [],
    )(packed, gains, wq, wk, wv, wo)


def split_by_core(core_ref, weights, keep_ref, send_ref):
    low_core = core_ref[0] == 0
    for i in range(2):
        keep_ref[i] = jnp.where(low_core, weights[i], weights[2 + i])
        send_ref[i] = jnp.where(low_core, weights[2 + i], weights[i]).astype(BF)


def inter_weights_kernel(
    core_ref, normed_t_ref, grads_ref, ctx_t_ref, gq_t_ref, gk_ref, gv_ref, keep_ref, send_ref
):
    normed_t = normed_t_ref[...]
    weights = (
        nt(normed_t, gq_t_ref[...]),
        nn(normed_t, gk_ref[...]),
        nn(normed_t, gv_ref[...]),
        nn(ctx_t_ref[...], grads_ref[...]),
    )
    split_by_core(core_ref, weights, keep_ref, send_ref)


def inter_weights(core, *operands):
    return kernel_call(
        inter_weights_kernel, "inter_weights", 1, [SMEM] + [VMEM] * 6, [VMEM] * 2,
        (f32(2, D, D), bf16(2, D, D)), [],
    )(core, *operands)


KEYS, QUERIES_T, VALUES, STATS = 0, 768, 1536, 2304
QUERIES, KEYS_T, NORMED_T, CONTEXT = 2496, 3264, 4032, 4800
HANDED_ROWS = 5824


def put_stats(handed_ref, stats):
    for i in range(3):
        part = stats.astype(BF)
        stats = stats - part.astype(F32)
        put_blocks(handed_ref, STATS + 64 * i, part)


def stats_of(handed_ref):
    parts = [
        jnp.concatenate(
            [
                handed_ref[STATS + 64 * i + 32 * j : STATS + 64 * i + 32 * j + 32, :].astype(F32)
                for j in range(2)
            ],
            axis=1,
        )
        for i in range(3)
    ]
    return parts[0] + parts[1] + parts[2]


def put_blocks(handed_ref, start, array):
    for i in range(array.shape[1] // 128):
        at = start + i * array.shape[0]
        handed_ref[at : at + array.shape[0], :] = array[:, 128 * i : 128 * i + 128]


def features_of(handed_ref, start, rows, at):
    return jnp.concatenate(
        [
            handed_ref[start + 256 * i + rows.start : start + 256 * i + rows.stop, :]
            for i in range(at.start // 128, at.stop // 128)
        ],
        axis=1,
    )


def tokens_of(handed_ref, start, at, b):
    return handed_ref[start + 384 * b + at.start : start + 384 * b + at.stop, :]


def begin_layer(sems, f_any, n_any, gain_any, wq_any, wk_any, wv_any, rows_ref, gain_ref, w_ref):
    return begin(
        sems,
        (f_any, rows_ref.at[pl.ds(0, K)]),
        (n_any.at[pl.ds(0, HOP)], rows_ref.at[pl.ds(K, HOP)]),
        (gain_any, gain_ref),
        (wq_any.at[0], w_ref.at[0]),
        (wk_any.at[0], w_ref.at[1]),
        (wv_any.at[0], w_ref.at[2]),
    )


def layer_scratch():
    return [vbf(3 * HOP, D), pltpu.VMEM((2, D), F32), vbf(3, D, D)]


def intra_prepare_kernel(
    f_ref, n_ref, gain_ref, wq_ref, wk_ref, wv_ref, handed_ref, stats_ref, ctx_ref
):
    rows = jnp.concatenate([f_ref[...], n_ref[:HOP]], axis=0)
    unit, _ = standardize(rows.astype(F32))
    normed = (unit * gain_ref[0:1, :]).astype(BF)
    queries = nn(normed, wq_ref[0]).astype(BF)
    keys = nn(normed, wk_ref[0]).astype(BF)
    values = nn(normed, wv_ref[0]).astype(BF)
    queries_t = queries.T
    values_t = values.T
    put_blocks(handed_ref, NORMED_T, normed.T)
    put_blocks(handed_ref, QUERIES, queries)
    put_blocks(handed_ref, QUERIES_T, queries_t)
    put_blocks(handed_ref, KEYS, keys)
    put_blocks(handed_ref, KEYS_T, keys.T)
    put_blocks(handed_ref, VALUES, values)
    masks = head_masks()

    def scores_of(step):
        g, h = step // HEADS, step % HEADS
        at = slice(g * HOP, g * HOP + K)
        block = slice((h // 4) * 128, (h // 4) * 128 + 128)
        return nn(keys[at, block] * masks[h % 4], queries_t[block, at])

    def weigh(step, scores):
        highest = jnp.max(scores, axis=0, keepdims=True)
        powers = jnp.exp2((scores - highest) * (SCALE * LOG2E))
        inverse = 1.0 / jnp.sum(powers, axis=0, keepdims=True)
        stats_ref[2 * step : 2 * step + 1, :] = highest
        stats_ref[2 * step + 1 : 2 * step + 2, :] = inverse
        return (powers * inverse).astype(BF)

    def collect(step, low):
        g, h = step // HEADS, step % HEADS
        feats = slice(h * HEAD, h * HEAD + HEAD)
        ctx_ref[g, feats, :] = nn(values_t[feats, g * HOP : g * HOP + K], low).astype(BF)

    staged(2 * HEADS, scores_of, weigh, collect)
    for g in range(2):
        put_blocks(handed_ref, CONTEXT + 512 * g, ctx_ref[g])
    put_stats(handed_ref, stats_ref[...])


def intra_prepare(frames, following, gains, wq, wk, wv):
    return kernel_call(
        intra_prepare_kernel, "intra_prepare", 3, [VMEM] * 6, VMEM, bf16(HANDED_ROWS, 128),
        [pltpu.VMEM((4 * HEADS, K), F32), vbf(2, D, K)],
    )(frames, following, gains, wq, wk, wv)


def intra_backward_kernel(
    core_ref, m_ref, wo_ref, handed_any,
    keep_ref, send_ref, grads_ref, gq_t, gk_ref, gv_ref,
    handed_ref, stats_ref, sems,
):
    cuts = (KEYS, QUERIES, NORMED_T, HANDED_ROWS)
    spans = [pl.ds(start, end - start) for start, end in zip(cuts, cuts[1:])]
    copies = begin(sems, *[(handed_any.at[span], handed_ref.at[span]) for span in spans])
    pick = select_rows(256, 256, owner_target)
    tiles = [nn(pick, m_ref[256 * t : 256 * t + 256, :]).astype(BF) for t in range(2)]
    masks = head_masks()
    context, context_t = [], []
    for g in range(2):
        grads_ref[g] = jnp.concatenate(
            [tiles[t][128 * g + 64 * h : 128 * g + 64 * h + 64] for h in range(2) for t in range(2)],
            axis=0,
        )
        context.append(nt(grads_ref[g], wo_ref[0]).astype(BF))
        context_t.append(context[g].T)

    copies[0].wait()
    stats_ref[...] = stats_of(handed_ref)

    def place(step):
        g, h = step // HEADS, step % HEADS
        return g, slice(g * HOP, g * HOP + K), h // 4, h % 4

    def products(step):
        g, at, b, i = place(step)
        block = slice(128 * b, 128 * b + 128)
        keys = tokens_of(handed_ref, KEYS, at, b) * masks[i]
        scores = nn(keys, features_of(handed_ref, QUERIES_T, block, at))
        values = tokens_of(handed_ref, VALUES, at, b) * masks[i]
        return scores, nn(values, context_t[g][block, :])

    def weigh(step, held):
        scores, grad_probs = held
        powers = jnp.exp2((scores - stats_ref[2 * step : 2 * step + 1, :]) * (SCALE * LOG2E))
        probs = powers * stats_ref[2 * step + 1 : 2 * step + 2, :]
        inner = jnp.sum(grad_probs * probs, axis=0, keepdims=True)
        return probs.astype(BF), (probs * (grad_probs - inner) * SCALE).astype(BF)

    sums = {}

    def collect(step, held):
        if step == 0:
            copies[1].wait()
        low, grad_scores = held
        g, at, b, i = place(step)
        block = slice(128 * b, 128 * b + 128)
        feats = slice(128 * b + HEAD * i, 128 * b + HEAD * i + HEAD)
        gv = nn(low, context[g][:, block] * masks[i])
        gk = nn(grad_scores, tokens_of(handed_ref, QUERIES, at, b) * masks[i])
        keys_t = features_of(handed_ref, KEYS_T, feats, at)
        gq_t[g, feats, :] = nn(keys_t, grad_scores).astype(BF)
        sums["v"] = gv if i == 0 else sums["v"] + gv
        sums["k"] = gk if i == 0 else sums["k"] + gk
        if i == 3:
            gv_ref[g, :, block] = sums["v"].astype(BF)
            gk_ref[g, :, block] = sums["k"].astype(BF)

    staged(2 * HEADS, products, weigh, collect)
    copies[2].wait()
    parts = []
    for g in range(2):
        normed_t = features_of(
            handed_ref, NORMED_T, slice(0, D), slice(g * HOP, g * HOP + K)
        )
        context_0 = jnp.concatenate(
            [handed_ref[pl.ds(CONTEXT + 512 * g + 256 * i, 256), :] for i in range(2)], axis=1
        )
        parts.append(
            (
                nt(normed_t, gq_t[g]),
                nn(normed_t, gk_ref[g]),
                nn(normed_t, gv_ref[g]),
                nn(context_0, grads_ref[g]),
            )
        )
    totals = [first + second for first, second in zip(*parts)]
    split_by_core(core_ref, totals, keep_ref, send_ref)


def intra_backward(core, grads, handed, wo):
    return kernel_call(
        intra_backward_kernel, "intra_backward", 4, [SMEM] + [VMEM] * 2 + [HBM], [VMEM] * 6,
        (
            f32(2, D, D), bf16(2, D, D), bf16(2, K, D), bf16(2, D, K), bf16(2, K, D), bf16(2, K, D),
        ),
        [vbf(HANDED_ROWS, 128), pltpu.VMEM((4 * HEADS, K), F32), dma(3)],
    )(core, grads, wo, *pinned(handed))


def intra_tail_kernel(
    grads_any, gq_t_any, gk_any, gv_any, f_any, n_any, gain_any, wq_any, wk_any, wv_any,
    first_ref, second_ref, carry_ref,
    grads_ref, gq_t_ref, gk_ref, gv_ref, rows_ref, gain_ref, w_ref, sems, own_sems,
):
    copies = begin_layer(sems, f_any, n_any, gain_any, wq_any, wk_any, wv_any, rows_ref, gain_ref, w_ref)
    copies += begin(
        own_sems,
        (grads_any, grads_ref), (gq_t_any, gq_t_ref), (gk_any, gk_ref), (gv_any, gv_ref),
    )
    settle(copies)
    unit, inverse = standardize(rows_ref[...].astype(F32))
    halves = []
    for g in range(2):
        at = slice(g * HOP, g * HOP + K)
        grad_normed = (
            nt(gq_t_ref[g].T, w_ref[0]) + nt(gk_ref[g], w_ref[1]) + nt(gv_ref[g], w_ref[2])
        )
        pulled = norm_pullback(grad_normed, unit[at], inverse[at], gain_ref[0:1, :])
        result = (grads_ref[g].astype(F32) + pulled).astype(BF)
        halves.append((result[:HOP], result[HOP:]))
    first_ref[...] = halves[0][0]
    second_ref[...] = (halves[1][0].astype(F32) + halves[0][1].astype(F32)).astype(BF)
    carry_ref[...] = halves[1][1]


def intra_tail(*operands):
    return kernel_call(
        intra_tail_kernel, "intra_tail", 2, [HBM] * 10, [VMEM] * 3,
        (bf16(HOP, D), bf16(HOP, D), bf16(HOP, D)),
        [vbf(2, K, D), vbf(2, D, K), vbf(2, K, D), vbf(2, K, D)]
        + layer_scratch()
        + [dma(6), dma(4)],
    )(*operands)


def finish_kernel(
    core_ref, mine_ref, other_ref, first_ref, second_ref, carried_ref, gain_ref, wq_ref, wk_ref, wv_ref,
    frames_ref, dq_ref, dk_ref, dv_ref, do_ref, dg_ref,
):
    frames_ref[:HOP] = (first_ref[...].astype(F32) + carried_ref[...].astype(F32)).astype(BF)
    frames_ref[HOP:] = second_ref[...]
    low_core = core_ref[0] == 0
    for layer in range(2):
        mine = mine_ref[:, layer].reshape(2, D, D).astype(F32)
        other = other_ref[:, layer].reshape(2, D, D).astype(F32)
        dq = jnp.where(low_core, mine[0], other[0])
        dk = jnp.where(low_core, mine[1], other[1])
        dv = jnp.where(low_core, other[0], mine[0])
        dq_ref[layer] = dq
        dk_ref[layer] = dk
        dv_ref[layer] = dv
        do_ref[layer] = jnp.where(low_core, other[1], mine[1])
        through = (
            dq * wq_ref[layer].astype(F32)
            + dk * wk_ref[layer].astype(F32)
            + dv * wv_ref[layer].astype(F32)
        )
        column = jnp.sum(through.T, axis=0, keepdims=True)
        dg_ref[layer : layer + 1, :] = column / gain_ref[layer : layer + 1, :]


def finish(core, *operands):
    full = f32(2, D, D)
    return kernel_call(
        finish_kernel, "finish", 2, [SMEM] + [VMEM] * 9, [VMEM] * 6,
        (bf16(K, D), full, full, full, full, f32(2, D)), [],
    )(core, *operands)


def shifted(shard, by):
    length = lax.axis_size(TM)
    pairs = [(i, i + by) for i in range(length) if 0 <= i + by < length]
    return lax.ppermute(shard, TM, pairs)


def exchanged(shard, axes):
    return lax.all_to_all(shard, axes, split_axis=0, concat_axis=0, tiled=True)


def swapped(shard):
    return lax.ppermute(shard, "core", [(0, 1), (1, 0)])


def spread_kernel(pieces_ref, out_ref):
    total = jnp.sum(pieces_ref[...].astype(F32), axis=0).astype(BF)
    for i in range(out_ref.shape[0]):
        out_ref[i] = total


def spread(pieces, count):
    return kernel_call(
        spread_kernel, "spread", 1, [VMEM], VMEM, bf16(count, *pieces.shape[1:]), []
    )(pieces)


def core_sum_kernel(keep_ref, arrived_ref, out_ref):
    out_ref[...] = (keep_ref[...] + arrived_ref[...].astype(F32)).astype(BF)


def core_sum(keep, send):
    return kernel_call(
        core_sum_kernel, "core_sum", 1, [VMEM] * 2, VMEM, bf16(2, D, D), []
    )(keep, swapped(send))


def both_sums_kernel(keep_ref, arrived_ref, inter_ref, out_ref):
    half = (keep_ref[...] + arrived_ref[...].astype(F32)).astype(BF)
    out_ref[:, :16] = half.reshape(32, 16, D)
    out_ref[:, 16:] = inter_ref[...].reshape(32, 16, D)


def both_sums(keep, send, inter_half):
    return kernel_call(
        both_sums_kernel, "both_sums", 1, [VMEM] * 3, VMEM, bf16(32, 32, D), []
    )(keep, swapped(send), inter_half)


def shards(frames, frames_grad, wq, wk, wv, wo, gains):
    frames = frames[0]
    core = lax.axis_index("core").astype(jnp.int32).reshape(1)
    following = shifted(frames, -1)
    front = intra_first(frames, gains, wq, wk, wv, wo)
    packed = intra_second(following, frames, frames_grad[0], *front)
    across = exchanged(packed.reshape(64, 8, 384), TM).reshape(512, 384)
    grad_middle, *operands = inter(across, gains, wq, wk, wv, wo)
    grad_local = exchanged(grad_middle.reshape(64, 8, D), TM).reshape(512, D)
    inter_half = core_sum(*inter_weights(core, *operands))
    grad_local, inter_half = lax.optimization_barrier((grad_local, inter_half))
    handed = intra_prepare(frames, following, gains, wq, wk, wv)
    keep, send, *rest = intra_backward(core, grad_local, handed, wo)
    half = both_sums(keep, send, inter_half)
    first, second, carry = intra_tail(*rest, frames, following, gains, wq, wk, wv)
    carried = shifted(carry, 1)
    sent = spread(exchanged(half, PLANE), 4)
    sent, carried = lax.optimization_barrier((sent, carried))
    sent = spread(exchanged(sent, "za"), 32)
    whole = exchanged(sent, PLANE).reshape(32, 2, 16, D)
    other = swapped(whole)
    grad_frames, *weights = finish(
        core, whole, other, first, second, carried, gains, wq, wk, wv
    )
    return (grad_frames[None], *weights)


def solution(mesh):
    split = Mesh(mesh.devices.reshape(2, 2, 2, 4, 4, 2), AXES)
    placed = (P(DP, TM, None), P(DP, TM, None), P(), P(), P(), P(), P())
    return jax.shard_map(
        shards,
        mesh=split,
        in_specs=placed,
        out_specs=(P(DP, TM, None), P(), P(), P(), P(), P()),
        check_vma=False,
    )
```

```python
import math

import jax
import jax.numpy as jnp
from jax import lax
from jax.experimental import pallas as pl
from jax.experimental.pallas import tpu as pltpu
from jax.sharding import Mesh, PartitionSpec as P

HEADS = 8
HEAD = 32
D = 256
K = 256
HOP = 128
SEGMENTS = 128
EPSILON = 1e-05
SCALE = HEAD ** (-0.5)
LOG2E = math.log2(math.e)
BF = jnp.bfloat16
F32 = jnp.float32
VMEM_LIMIT = 16 * 1024 * 1024

AXES = ("yh", "core", "yl", "x", "za", "zb")
DP = ("yh", "core")
TM = ("yl", "x", "za", "zb")
PLANE = ("yh", "yl", "x", "zb")


def dot(left, right, left_dim, right_dim):
    return lax.dot_general(
        left, right, (((left_dim,), (right_dim,)), ((), ())), preferred_element_type=F32
    )


def nn(left, right):
    return dot(left, right, 1, 0)


def nt(left, right):
    return dot(left, right, 1, 1)


def tn(left, right):
    return dot(left, right, 0, 0)


def standardize(rows):
    average = jnp.mean(rows, axis=-1, keepdims=True)
    centered = rows - average
    variance = jnp.mean(centered * centered, axis=-1, keepdims=True)
    inverse = lax.rsqrt(variance + EPSILON)
    return centered * inverse, inverse


def norm_pullback(grad_normed, unit, inverse, gain):
    grad_unit = grad_normed * gain
    first = jnp.mean(grad_unit, axis=-1, keepdims=True)
    second = jnp.mean(grad_unit * unit, axis=-1, keepdims=True)
    return inverse * (grad_unit - first - unit * second)


def head_masks():
    lane = lax.broadcasted_iota(jnp.int32, (1, 128), 1)
    return [jnp.where(lane // HEAD == i, 1.0, 0.0).astype(BF) for i in range(4)]


def row_masks():
    row = lax.broadcasted_iota(jnp.int32, (128, 1), 0)
    return [jnp.where(row // HEAD == i, 1.0, 0.0).astype(BF) for i in range(4)]


def select_rows(out_rows, in_rows, source):
    out = lax.broadcasted_iota(jnp.int32, (out_rows, in_rows), 0)
    col = lax.broadcasted_iota(jnp.int32, (out_rows, in_rows), 1)
    return jnp.where(source(out) == col, 1.0, 0.0).astype(BF)


def softmax_keys(scores):
    highest = jnp.max(scores, axis=0, keepdims=True)
    powers = jnp.exp2((scores - highest) * (SCALE * LOG2E))
    return powers * (1.0 / jnp.sum(powers, axis=0, keepdims=True))


def owner_target(out):
    return ((out % 64) // 2) * 8 + (out // 64) * 2 + out % 2


def segment_target(out):
    return (out % 4) * 64 + out // 4


def packed_source(out):
    return ((out // 2) % 4) * 64 + (out // 8) * 2 + out % 2


def middle_source(out):
    return ((out % 64) // 2) * 8 + (out % 2) * 4 + out // 64


def cotangent_source(out):
    hop = out % 64
    return (hop // 2) * 8 + (out // 128) * 4 + (hop % 2) * 2 + (out // 64) % 2


def staged(count, *stages):
    held = [{} for _ in stages]
    for t in range(count + len(stages) - 1):
        for i, stage in enumerate(stages):
            step = t - i
            if 0 <= step < count:
                held[i][step] = stage(step, *([held[i - 1].pop(step)] if i else []))


def attend(keys, queries_t, values_t, ctx_ref, ahead):

    def scores_of(h):
        feats = slice(h * HEAD, h * HEAD + HEAD)
        return nn(keys[:, feats], queries_t[feats, :])

    def weigh(h, scores):
        return softmax_keys(scores).astype(BF)

    def collect(h, low):
        feats = slice(h * HEAD, h * HEAD + HEAD)
        ctx_ref[feats, :] = nn(values_t[feats, :], low).astype(BF)

    waiting = [lambda h, scores: scores] * ahead
    staged(HEADS, scores_of, *waiting, weigh, collect)


VMEM = pl.BlockSpec(memory_space=pltpu.VMEM)
SMEM = pl.BlockSpec(memory_space=pltpu.SMEM)
HBM = pl.BlockSpec(memory_space=pltpu.HBM)


def begin(sems, *pairs):
    copies = [pltpu.make_async_copy(src, dst, sems.at[i]) for i, (src, dst) in enumerate(pairs)]
    for copy in copies:
        copy.start()
    return copies


def settle(copies):
    for copy in copies:
        copy.wait()


def bf16(*shape):
    return jax.ShapeDtypeStruct(shape, BF)


def f32(*shape):
    return jax.ShapeDtypeStruct(shape, F32)


def kernel_call(kernel, name, micros, in_specs, out_specs, out_shape, scratch, limit=VMEM_LIMIT):
    return pl.pallas_call(
        kernel,
        in_specs=in_specs,
        out_specs=out_specs,
        out_shape=out_shape,
        scratch_shapes=scratch,
        compiler_params=pltpu.CompilerParams(vmem_limit_bytes=limit),
        cost_estimate=pl.CostEstimate(
            flops=int(micros * 400e6), bytes_accessed=1 << 20, transcendentals=0
        ),
        name=name,
    )


def dma(count):
    return pltpu.SemaphoreType.DMA((count,))


def vbf(*shape):
    return pltpu.VMEM(shape, BF)


def pinned(*arrays):
    return [pltpu.with_memory_space_constraint(array, pltpu.HBM) for array in arrays]


def intra_first_kernel(
    f_any, gain_any, wq_any, wk_any, wv_any, wo_any,
    mid_ref, keys_ref, queries_ref, values_ref, w_ref, gain_ref,
    f_ref, ctx_ref, sems,
):
    copies = begin(
        sems,
        (f_any, f_ref),
        (gain_any, gain_ref),
        (wk_any.at[0], w_ref.at[1]),
        (wq_any.at[0], w_ref.at[0]),
        (wv_any.at[0], w_ref.at[2]),
        (wo_any.at[0], w_ref.at[3]),
    )
    copies[0].wait()
    rows = f_ref[...].astype(F32)
    unit, _ = standardize(rows)
    copies[1].wait()
    normed = (unit * gain_ref[0:1, :]).astype(BF)
    settle(copies[2:5])
    keys = nn(normed, w_ref[1]).astype(BF)
    queries_t = nt(w_ref[0].T, normed).astype(BF)
    values_t = nt(w_ref[2].T, normed).astype(BF)
    attend(keys, queries_t, values_t, ctx_ref, 1)
    copies[5].wait()
    mid_ref[...] = (rows + tn(ctx_ref[...], w_ref[3])).astype(BF)
    keys_ref[...] = keys[HOP:]
    queries_ref[...] = queries_t[:, HOP:]
    values_ref[...] = values_t[:, HOP:]


def intra_second_kernel(
    n_ref, mid_in_ref, keys_ref, queries_ref, values_ref, w_ref, gain_ref, f_any, grad_any, packed_ref,
    f_ref, grad_ref, ctx_ref, sems,
):
    copies = begin(sems, (f_any.at[pl.ds(HOP, HOP)], f_ref), (grad_any, grad_ref))
    rows = n_ref[:HOP].astype(F32)
    unit, _ = standardize(rows)
    normed = (unit * gain_ref[0:1, :]).astype(BF)
    keys = jnp.concatenate([keys_ref[...], nn(normed, w_ref[1]).astype(BF)], axis=0)
    queries_t = jnp.concatenate(
        [queries_ref[...], nt(w_ref[0].T, normed).astype(BF)], axis=1
    )
    values_t = jnp.concatenate([values_ref[...], nt(w_ref[2].T, normed).astype(BF)], axis=1)
    attend(keys, queries_t, values_t, ctx_ref, 0)
    settle(copies)
    rows = jnp.concatenate([f_ref[...].astype(F32), rows], axis=0)
    mids = (mid_in_ref[...], (rows + tn(ctx_ref[...], w_ref[3])).astype(BF))
    grads = grad_ref[...]
    pick = select_rows(256, 256, packed_source)
    for t in range(2):
        parts = []
        for part in range(4):
            high, low = part // 2, part % 2
            at = slice(low * HOP + 64 * t, low * HOP + 64 * t + 64)
            parts.append(
                jnp.concatenate([mids[high][at], grads[at, 128 * high : 128 * high + 128]], axis=1)
            )
        rows = jnp.concatenate(parts, axis=0)
        packed_ref[256 * t : 256 * t + 256, :] = nn(pick, rows).astype(BF)


def intra_first(*operands):
    return kernel_call(
        intra_first_kernel, "intra_first", 3, [HBM] * 6, [VMEM] * 6,
        (bf16(K, D), bf16(HOP, D), bf16(D, HOP), bf16(D, HOP), bf16(4, D, D), f32(2, D)),
        [vbf(K, D), vbf(D, K), dma(6)],
    )(*pinned(*operands))


def intra_second(following, frames, grads, *front):
    return kernel_call(
        intra_second_kernel, "intra_second", 3, [VMEM] * 7 + [HBM] * 2, VMEM, bf16(512, 384),
        [vbf(HOP, D), vbf(K, D), vbf(D, K), dma(2)],
    )(following, *front, *pinned(frames, grads))


def inter_kernel(
    packed_ref, gain_ref, wq_ref, wk_ref, wv_ref, wo_ref,
    out_ref, normed_t_ref, grads_ref, ctx_t, gq_t, gk_ref, gv_ref,
):
    gain = gain_ref[1:2, :]
    pick = select_rows(256, 256, middle_source)
    tiles = [nn(pick, packed_ref[256 * t : 256 * t + 256, :D]) for t in range(2)]
    rows = jnp.concatenate(
        [tiles[t][64 * p : 64 * p + 64] for p in range(4) for t in range(2)], axis=0
    )
    pick = select_rows(256, 256, cotangent_source)
    tiles = [nn(pick, packed_ref[256 * t : 256 * t + 256, D:]) for t in range(2)]
    hops = [
        jnp.concatenate(
            [
                jnp.concatenate(
                    [tiles[t][128 * c + 64 * r : 128 * c + 64 * r + 64] for c in range(2)], axis=1
                )
                for t in range(2)
            ],
            axis=0,
        )
        for r in range(2)
    ]
    last = jnp.zeros((1, D), F32)
    late = [jnp.concatenate([hop[1:], last], axis=0) for hop in hops]
    grads = jnp.concatenate(hops + late, axis=0).astype(BF)
    grads_ref[...] = grads
    unit, inverse = standardize(rows)
    normed = (unit * gain).astype(BF)
    normed_t_ref[...] = normed.T
    wq, wk, wv, wo = wq_ref[1], wk_ref[1], wv_ref[1], wo_ref[1]
    queries = nn(normed, wq).astype(BF)
    keys = nn(normed, wk).astype(BF)
    values = nn(normed, wv).astype(BF)
    grad_context = nt(grads, wo).astype(BF)
    queries_t = queries.T
    keys_t = keys.T
    values_t = values.T
    grad_context_t = grad_context.T
    masks = head_masks()
    downs = row_masks()

    def place(step):
        p, b, pair = step // 4, (step // 2) % 2, step % 2
        return slice(128 * p, 128 * p + 128), slice(128 * b, 128 * b + 128), pair

    def columns(rows_t, pair):
        return jnp.concatenate([rows_t * downs[2 * pair], rows_t * downs[2 * pair + 1]], axis=1)

    def stacked(rows, pair):
        return jnp.concatenate([rows * masks[2 * pair], rows * masks[2 * pair + 1]], axis=0)

    def products(step):
        at, block, pair = place(step)
        scores = nn(keys[at, block], columns(queries_t[block, at], pair))
        grad_probs = nn(values[at, block], columns(grad_context_t[block, at], pair))
        return scores, grad_probs

    def weigh(step, held):
        scores, grad_probs = held
        return softmax_keys(scores), grad_probs

    def weigh_rest(step, held):
        probs, grad_probs = held
        inner = jnp.sum(grad_probs * probs, axis=0, keepdims=True)
        return probs.astype(BF), (probs * (grad_probs - inner) * SCALE).astype(BF)

    sums = {}

    def collect(step, held):
        low, grad_scores = held
        at, block, pair = place(step)
        gv = nn(low, stacked(grad_context[at, block], pair))
        gk = nn(grad_scores, stacked(queries[at, block], pair))
        if pair == 0:
            sums["v"], sums["k"] = gv, gk
        else:
            gv_ref[at, block] = (sums["v"] + gv).astype(BF)
            gk_ref[at, block] = (sums["k"] + gk).astype(BF)
        start = block.start + 64 * pair
        for target, rows_t, right in ((ctx_t, values_t, low), (gq_t, keys_t, grad_scores)):
            both = nn(rows_t[start : start + 64, at], right)
            target[start : start + 32, at] = both[:32, :128].astype(BF)
            target[start + 32 : start + 64, at] = both[32:, 128:].astype(BF)

    staged(16, products, weigh, weigh_rest, collect)
    gqt, gk, gv = gq_t[...], gk_ref[...], gv_ref[...]
    grad_normed = nt(gqt.T, wq) + nt(gk, wk) + nt(gv, wv)
    result = (grads.astype(F32) + norm_pullback(grad_normed, unit, inverse, gain)).astype(BF)
    back = select_rows(256, 256, segment_target)
    for t in range(2):
        part = jnp.concatenate(
            [result[128 * p + 64 * t : 128 * p + 64 * t + 64] for p in range(4)], axis=0
        )
        out_ref[256 * t : 256 * t + 256, :] = nn(back, part).astype(BF)


def inter(packed, gains, wq, wk, wv, wo):
    return kernel_call(
        inter_kernel, "inter", 5, [VMEM] * 6, [VMEM] * 7,
        (
            bf16(512, D), bf16(D, 512), bf16(512, D), bf16(D, 512), bf16(D, 512), bf16(512, D),
            bf16(512, D),
        ),
        [],
    )(packed, gains, wq, wk, wv, wo)


def split_by_core(core_ref, weights, keep_ref, send_ref):
    low_core = core_ref[0] == 0
    for i in range(2):
        keep_ref[i] = jnp.where(low_core, weights[i], weights[2 + i])
        send_ref[i] = jnp.where(low_core, weights[2 + i], weights[i]).astype(BF)


def inter_weights_kernel(
    core_ref, normed_t_ref, grads_ref, ctx_t_ref, gq_t_ref, gk_ref, gv_ref, keep_ref, send_ref
):
    normed_t = normed_t_ref[...]
    weights = (
        nt(normed_t, gq_t_ref[...]),
        nn(normed_t, gk_ref[...]),
        nn(normed_t, gv_ref[...]),
        nn(ctx_t_ref[...], grads_ref[...]),
    )
    split_by_core(core_ref, weights, keep_ref, send_ref)


def inter_weights(core, *operands):
    return kernel_call(
        inter_weights_kernel, "inter_weights", 1, [SMEM] + [VMEM] * 6, [VMEM] * 2,
        (f32(2, D, D), bf16(2, D, D)), [],
    )(core, *operands)


KEYS, QUERIES_T, VALUES, STATS = 0, 768, 1536, 2304
QUERIES, KEYS_T, NORMED_T, CONTEXT = 2496, 3264, 4032, 4800
HANDED_ROWS = 5824


def put_stats(handed_ref, stats):
    for i in range(3):
        part = stats.astype(BF)
        stats = stats - part.astype(F32)
        put_blocks(handed_ref, STATS + 64 * i, part)


def stats_of(handed_ref):
    parts = [
        jnp.concatenate(
            [
                handed_ref[STATS + 64 * i + 32 * j : STATS + 64 * i + 32 * j + 32, :].astype(F32)
                for j in range(2)
            ],
            axis=1,
        )
        for i in range(3)
    ]
    return parts[0] + parts[1] + parts[2]


def put_blocks(handed_ref, start, array):
    for i in range(array.shape[1] // 128):
        at = start + i * array.shape[0]
        handed_ref[at : at + array.shape[0], :] = array[:, 128 * i : 128 * i + 128]


def features_of(handed_ref, start, rows, at):
    return jnp.concatenate(
        [
            handed_ref[start + 256 * i + rows.start : start + 256 * i + rows.stop, :]
            for i in range(at.start // 128, at.stop // 128)
        ],
        axis=1,
    )


def tokens_of(handed_ref, start, at, b):
    return handed_ref[start + 384 * b + at.start : start + 384 * b + at.stop, :]


def begin_layer(sems, f_any, n_any, gain_any, wq_any, wk_any, wv_any, rows_ref, gain_ref, w_ref):
    return begin(
        sems,
        (f_any, rows_ref.at[pl.ds(0, K)]),
        (n_any.at[pl.ds(0, HOP)], rows_ref.at[pl.ds(K, HOP)]),
        (gain_any, gain_ref),
        (wq_any.at[0], w_ref.at[0]),
        (wk_any.at[0], w_ref.at[1]),
        (wv_any.at[0], w_ref.at[2]),
    )


def layer_scratch():
    return [vbf(3 * HOP, D), pltpu.VMEM((2, D), F32), vbf(3, D, D)]


def intra_prepare_kernel(
    f_ref, n_ref, gain_ref, wq_ref, wk_ref, wv_ref, handed_ref, stats_ref, ctx_ref
):
    rows = jnp.concatenate([f_ref[...], n_ref[:HOP]], axis=0)
    unit, _ = standardize(rows.astype(F32))
    normed = (unit * gain_ref[0:1, :]).astype(BF)
    queries = nn(normed, wq_ref[0]).astype(BF)
    keys = nn(normed, wk_ref[0]).astype(BF)
    values = nn(normed, wv_ref[0]).astype(BF)
    queries_t = queries.T
    values_t = values.T
    put_blocks(handed_ref, NORMED_T, normed.T)
    put_blocks(handed_ref, QUERIES, queries)
    put_blocks(handed_ref, QUERIES_T, queries_t)
    put_blocks(handed_ref, KEYS, keys)
    put_blocks(handed_ref, KEYS_T, keys.T)
    put_blocks(handed_ref, VALUES, values)
    masks = head_masks()

    def scores_of(step):
        g, h = step // HEADS, step % HEADS
        at = slice(g * HOP, g * HOP + K)
        block = slice((h // 4) * 128, (h // 4) * 128 + 128)
        return nn(keys[at, block] * masks[h % 4], queries_t[block, at])

    def weigh(step, scores):
        highest = jnp.max(scores, axis=0, keepdims=True)
        powers = jnp.exp2((scores - highest) * (SCALE * LOG2E))
        inverse = 1.0 / jnp.sum(powers, axis=0, keepdims=True)
        stats_ref[2 * step : 2 * step + 1, :] = highest
        stats_ref[2 * step + 1 : 2 * step + 2, :] = inverse
        return (powers * inverse).astype(BF)

    def collect(step, low):
        g, h = step // HEADS, step % HEADS
        feats = slice(h * HEAD, h * HEAD + HEAD)
        ctx_ref[g, feats, :] = nn(values_t[feats, g * HOP : g * HOP + K], low).astype(BF)

    staged(2 * HEADS, scores_of, weigh, collect)
    for g in range(2):
        put_blocks(handed_ref, CONTEXT + 512 * g, ctx_ref[g])
    put_stats(handed_ref, stats_ref[...])


def intra_prepare(frames, following, gains, wq, wk, wv):
    return kernel_call(
        intra_prepare_kernel, "intra_prepare", 3, [VMEM] * 6, VMEM, bf16(HANDED_ROWS, 128),
        [pltpu.VMEM((4 * HEADS, K), F32), vbf(2, D, K)],
    )(frames, following, gains, wq, wk, wv)


def intra_backward_kernel(
    core_ref, m_ref, wo_ref, handed_any,
    keep_ref, send_ref, grads_ref, gq_t, gk_ref, gv_ref,
    handed_ref, stats_ref, sems,
):
    cuts = (KEYS, QUERIES, NORMED_T, HANDED_ROWS)
    spans = [pl.ds(start, end - start) for start, end in zip(cuts, cuts[1:])]
    copies = begin(sems, *[(handed_any.at[span], handed_ref.at[span]) for span in spans])
    pick = select_rows(256, 256, owner_target)
    tiles = [nn(pick, m_ref[256 * t : 256 * t + 256, :]).astype(BF) for t in range(2)]
    masks = head_masks()
    context, context_t = [], []
    for g in range(2):
        grads_ref[g] = jnp.concatenate(
            [tiles[t][128 * g + 64 * h : 128 * g + 64 * h + 64] for h in range(2) for t in range(2)],
            axis=0,
        )
        context.append(nt(grads_ref[g], wo_ref[0]).astype(BF))
        context_t.append(context[g].T)

    copies[0].wait()
    stats_ref[...] = stats_of(handed_ref)

    def place(step):
        g, h = step // HEADS, step % HEADS
        return g, slice(g * HOP, g * HOP + K), h // 4, h % 4

    def products(step):
        g, at, b, i = place(step)
        block = slice(128 * b, 128 * b + 128)
        keys = tokens_of(handed_ref, KEYS, at, b) * masks[i]
        scores = nn(keys, features_of(handed_ref, QUERIES_T, block, at))
        values = tokens_of(handed_ref, VALUES, at, b) * masks[i]
        return scores, nn(values, context_t[g][block, :])

    def weigh(step, held):
        scores, grad_probs = held
        powers = jnp.exp2((scores - stats_ref[2 * step : 2 * step + 1, :]) * (SCALE * LOG2E))
        probs = powers * stats_ref[2 * step + 1 : 2 * step + 2, :]
        inner = jnp.sum(grad_probs * probs, axis=0, keepdims=True)
        return probs.astype(BF), (probs * (grad_probs - inner) * SCALE).astype(BF)

    sums = {}

    def collect(step, held):
        if step == 0:
            copies[1].wait()
        low, grad_scores = held
        g, at, b, i = place(step)
        block = slice(128 * b, 128 * b + 128)
        feats = slice(128 * b + HEAD * i, 128 * b + HEAD * i + HEAD)
        gv = nn(low, context[g][:, block] * masks[i])
        gk = nn(grad_scores, tokens_of(handed_ref, QUERIES, at, b) * masks[i])
        keys_t = features_of(handed_ref, KEYS_T, feats, at)
        gq_t[g, feats, :] = nn(keys_t, grad_scores).astype(BF)
        sums["v"] = gv if i == 0 else sums["v"] + gv
        sums["k"] = gk if i == 0 else sums["k"] + gk
        if i == 3:
            gv_ref[g, :, block] = sums["v"].astype(BF)
            gk_ref[g, :, block] = sums["k"].astype(BF)

    staged(2 * HEADS, products, weigh, collect)
    copies[2].wait()
    parts = []
    for g in range(2):
        normed_t = features_of(
            handed_ref, NORMED_T, slice(0, D), slice(g * HOP, g * HOP + K)
        )
        context_0 = jnp.concatenate(
            [handed_ref[pl.ds(CONTEXT + 512 * g + 256 * i, 256), :] for i in range(2)], axis=1
        )
        parts.append(
            (
                nt(normed_t, gq_t[g]),
                nn(normed_t, gk_ref[g]),
                nn(normed_t, gv_ref[g]),
                nn(context_0, grads_ref[g]),
            )
        )
    totals = [first + second for first, second in zip(*parts)]
    split_by_core(core_ref, totals, keep_ref, send_ref)


def intra_backward(core, grads, handed, wo):
    return kernel_call(
        intra_backward_kernel, "intra_backward", 4, [SMEM] + [VMEM] * 2 + [HBM], [VMEM] * 6,
        (
            f32(2, D, D), bf16(2, D, D), bf16(2, K, D), bf16(2, D, K), bf16(2, K, D), bf16(2, K, D),
        ),
        [vbf(HANDED_ROWS, 128), pltpu.VMEM((4 * HEADS, K), F32), dma(3)],
    )(core, grads, wo, *pinned(handed))


def intra_tail_kernel(
    grads_any, gq_t_any, gk_any, gv_any, f_any, n_any, gain_any, wq_any, wk_any, wv_any,
    first_ref, second_ref, carry_ref,
    grads_ref, gq_t_ref, gk_ref, gv_ref, rows_ref, gain_ref, w_ref, sems, own_sems,
):
    copies = begin_layer(sems, f_any, n_any, gain_any, wq_any, wk_any, wv_any, rows_ref, gain_ref, w_ref)
    copies += begin(
        own_sems,
        (grads_any, grads_ref), (gq_t_any, gq_t_ref), (gk_any, gk_ref), (gv_any, gv_ref),
    )
    settle(copies)
    unit, inverse = standardize(rows_ref[...].astype(F32))
    halves = []
    for g in range(2):
        at = slice(g * HOP, g * HOP + K)
        grad_normed = (
            nt(gq_t_ref[g].T, w_ref[0]) + nt(gk_ref[g], w_ref[1]) + nt(gv_ref[g], w_ref[2])
        )
        pulled = norm_pullback(grad_normed, unit[at], inverse[at], gain_ref[0:1, :])
        result = (grads_ref[g].astype(F32) + pulled).astype(BF)
        halves.append((result[:HOP], result[HOP:]))
    first_ref[...] = halves[0][0]
    second_ref[...] = (halves[1][0].astype(F32) + halves[0][1].astype(F32)).astype(BF)
    carry_ref[...] = halves[1][1]


def intra_tail(*operands):
    return kernel_call(
        intra_tail_kernel, "intra_tail", 2, [HBM] * 10, [VMEM] * 3,
        (bf16(HOP, D), bf16(HOP, D), bf16(HOP, D)),
        [vbf(2, K, D), vbf(2, D, K), vbf(2, K, D), vbf(2, K, D)]
        + layer_scratch()
        + [dma(6), dma(4)],
    )(*operands)


def finish_kernel(
    core_ref, mine_ref, other_ref, first_ref, second_ref, carried_ref, gain_ref, wq_ref, wk_ref, wv_ref,
    frames_ref, dq_ref, dk_ref, dv_ref, do_ref, dg_ref,
):
    frames_ref[:HOP] = (first_ref[...].astype(F32) + carried_ref[...].astype(F32)).astype(BF)
    frames_ref[HOP:] = second_ref[...]
    low_core = core_ref[0] == 0
    for layer in range(2):
        mine = mine_ref[:, layer].reshape(2, D, D).astype(F32)
        other = other_ref[:, layer].reshape(2, D, D).astype(F32)
        dq = jnp.where(low_core, mine[0], other[0])
        dk = jnp.where(low_core, mine[1], other[1])
        dv = jnp.where(low_core, other[0], mine[0])
        dq_ref[layer] = dq
        dk_ref[layer] = dk
        dv_ref[layer] = dv
        do_ref[layer] = jnp.where(low_core, other[1], mine[1])
        through = (
            dq * wq_ref[layer].astype(F32)
            + dk * wk_ref[layer].astype(F32)
            + dv * wv_ref[layer].astype(F32)
        )
        column = jnp.sum(through.T, axis=0, keepdims=True)
        dg_ref[layer : layer + 1, :] = column / gain_ref[layer : layer + 1, :]


def finish(core, *operands):
    full = f32(2, D, D)
    return kernel_call(
        finish_kernel, "finish", 2, [SMEM] + [VMEM] * 9, [VMEM] * 6,
        (bf16(K, D), full, full, full, full, f32(2, D)), [],
    )(core, *operands)


def shifted(shard, by):
    length = lax.axis_size(TM)
    pairs = [(i, i + by) for i in range(length) if 0 <= i + by < length]
    return lax.ppermute(shard, TM, pairs)


def exchanged(shard, axes):
    return lax.all_to_all(shard, axes, split_axis=0, concat_axis=0, tiled=True)


def swapped(shard):
    return lax.ppermute(shard, "core", [(0, 1), (1, 0)])


def spread_kernel(pieces_ref, out_ref):
    total = jnp.sum(pieces_ref[...].astype(F32), axis=0).astype(BF)
    for i in range(out_ref.shape[0]):
        out_ref[i] = total


def spread(pieces, count):
    return kernel_call(
        spread_kernel, "spread", 1, [VMEM], VMEM, bf16(count, *pieces.shape[1:]), []
    )(pieces)


def core_sum_kernel(keep_ref, arrived_ref, out_ref):
    out_ref[...] = (keep_ref[...] + arrived_ref[...].astype(F32)).astype(BF)


def core_sum(keep, send):
    return kernel_call(
        core_sum_kernel, "core_sum", 1, [VMEM] * 2, VMEM, bf16(2, D, D), []
    )(keep, swapped(send))


def both_sums_kernel(keep_ref, arrived_ref, inter_ref, out_ref):
    half = (keep_ref[...] + arrived_ref[...].astype(F32)).astype(BF)
    out_ref[:, :16] = half.reshape(32, 16, D)
    out_ref[:, 16:] = inter_ref[...].reshape(32, 16, D)


def both_sums(keep, send, inter_half):
    return kernel_call(
        both_sums_kernel, "both_sums", 1, [VMEM] * 3, VMEM, bf16(32, 32, D), []
    )(keep, swapped(send), inter_half)


def shards(frames, frames_grad, wq, wk, wv, wo, gains):
    frames = frames[0]
    core = lax.axis_index("core").astype(jnp.int32).reshape(1)
    following = shifted(frames, -1)
    front = intra_first(frames, gains, wq, wk, wv, wo)
    packed = intra_second(following, frames, frames_grad[0], *front)
    across = exchanged(packed.reshape(64, 8, 384), TM).reshape(512, 384)
    grad_middle, *operands = inter(across, gains, wq, wk, wv, wo)
    grad_local = exchanged(grad_middle.reshape(64, 8, D), TM).reshape(512, D)
    inter_half = core_sum(*inter_weights(core, *operands))
    grad_local, inter_half = lax.optimization_barrier((grad_local, inter_half))
    handed = intra_prepare(frames, following, gains, wq, wk, wv)
    keep, send, *rest = intra_backward(core, grad_local, handed, wo)
    half = both_sums(keep, send, inter_half)
    first, second, carry = intra_tail(*rest, frames, following, gains, wq, wk, wv)
    half, carry = lax.optimization_barrier((half, carry))
    carried = shifted(carry, 1)
    sent = spread(exchanged(half, PLANE), 4)
    sent, carried = lax.optimization_barrier((sent, carried))
    sent = spread(exchanged(sent, "za"), 32)
    whole = exchanged(sent, PLANE).reshape(32, 2, 16, D)
    other = swapped(whole)
    grad_frames, *weights = finish(
        core, whole, other, first, second, carried, gains, wq, wk, wv
    )
    return (grad_frames[None], *weights)


def solution(mesh):
    split = Mesh(mesh.devices.reshape(2, 2, 2, 4, 4, 2), AXES)
    placed = (P(DP, TM, None), P(DP, TM, None), P(), P(), P(), P(), P())
    return jax.shard_map(
        shards,
        mesh=split,
        in_specs=placed,
        out_specs=(P(DP, TM, None), P(), P(), P(), P(), P()),
        check_vma=False,
    )
```
